128 devices in a mesh: lat: 8 (over y, z_lo), lon: 16 (over z_hi, x, core).
Axes of the slice: x: 4, y: 4, z: 4 (z_hi: 2, z_lo: 2; z = z_hi * 2 + z_lo), core: 2. Of those that a mesh axis runs over, the one named last changes fastest.
Arguments:
- tokens: bfloat16 [64, 768, 512], P('lat', 'lon'), may hold values from -6 to 6
- cotangent: bfloat16 [64, 768, 512], P('lat', 'lon'), may hold values from -6 to 6
- gain_attn: float32 [512], replicated, may hold values from 0.5 to 1.5
- w_qkv: bfloat16 [512, 1536], replicated, may hold values from -3 to 3
- w_proj: bfloat16 [512, 512], replicated, may hold values from -0.25 to 0.25
- rel_table: float32 [8, 225], replicated, may hold values from -4 to 4
- gain_mlp: float32 [512], replicated, may hold values from 0.5 to 1.5
- w_fc1: bfloat16 [512, 2048], replicated, may hold values from -0.25 to 0.25
- w_fc2: bfloat16 [2048, 512], replicated, may hold values from -0.125 to 0.125
Outputs:
- output: bfloat16 [64, 768, 512], P('lat', 'lon')
- grad_tokens: float32 [64, 768, 512], P('lat', 'lon')
- grad_qkv: float32 [512, 1536], P(('lat', 'lon'))
- grad_proj: float32 [512, 512], P(('lat', 'lon'))
- grad_table: float32 [8, 225], replicated
- grad_fc1: float32 [512, 2048], P(('lat', 'lon'))
- grad_fc2: float32 [2048, 512], P(('lat', 'lon'))
- grad_gain_attn: float32 [512], replicated
- grad_gain_mlp: float32 [512], replicated
The draws below stay inside these ranges and needn't reach their ends.
All inputs are finite; a program needn't handle non-finite values.
Results may differ from the reference program's by a relative error of at most 0.017.
Values may be sent and summed in bfloat16 or wider, within the bound.
A program may use at most 128 MiB of HBM per device.

```python
import math
import jax
import jax.numpy as jnp
from jax import lax

D = 512
HEADS = 8
FFN = 2048
NLAT = 64
NLON = 768


def draw_w_qkv(key, part):
    key = jax.random.fold_in(key, 7)
    entry_key = jax.random.fold_in(key, 0)
    entries = jax.random.truncated_normal(entry_key, -4.0, 4.0, (D, 3 * D), jnp.float32) * (1.5 / math.sqrt(D))
    return entries.astype(jnp.bfloat16)


def levels(own_key, dims, pieces, smallest, top_value):
    def one(dim, shards_of):
        draws = jax.random.uniform(jax.random.fold_in(jax.random.fold_in(own_key, 6), dim), (shards_of,), jnp.float32, smallest / len(pieces), top_value / len(pieces))
        return jnp.repeat(jnp.exp(draws), dims[dim] // shards_of).reshape((-1,) + (1,) * (len(dims) - dim - 1))

    factor_of = one(*pieces[0])
    for cut in pieces[1:]:
        factor_of = factor_of * one(*cut)
    return factor_of


def normal_values(stream_key, shape, scale, most, pieces=(), kind=jnp.bfloat16):
    level = levels(stream_key, shape, pieces, -0.22, 0.18) if pieces else 1.0
    drawn = jax.random.normal(stream_key, shape, jnp.float32) * scale * level
    return jnp.minimum(jnp.maximum(drawn, -most), most).astype(kind)


def setup_inputs(seed: int = 0) -> dict:
    arg_keys = jax.random.split(jax.random.key(seed), 10)
    tokens = normal_values(arg_keys[0], (NLAT, NLON, D), 1.0, 6.0, ((0, 8), (1, 16)))
    cotangent = normal_values(arg_keys[1], (NLAT, NLON, D), 1.0, 6.0, ((0, 8), (1, 16)))
    gain_attn = jnp.clip(1.0 + 0.1 * jax.random.normal(arg_keys[2], (D,), jnp.float32), 0.5, 1.5)
    w_qkv = draw_w_qkv(jax.random.fold_in(arg_keys[9], 71), 0)
    w_proj = normal_values(arg_keys[4], (D, D), D ** -0.5, 0.25)
    rel_table = normal_values(arg_keys[5], (HEADS, 225), 1.0, 4.0, (), jnp.float32)
    gain_mlp = jnp.clip(1.0 + 0.1 * jax.random.normal(arg_keys[6], (D,), jnp.float32), 0.5, 1.5)
    w_fc1 = normal_values(arg_keys[7], (D, FFN), D ** -0.5, 0.25)
    w_fc2 = normal_values(arg_keys[8], (FFN, D), FFN ** -0.5, 0.125)
    return {"tokens": tokens, "cotangent": cotangent, "gain_attn": gain_attn, "w_qkv": w_qkv, "w_proj": w_proj, "rel_table": rel_table, "gain_mlp": gain_mlp, "w_fc1": w_fc1, "w_fc2": w_fc2}


NORM_EPSILON = 1e-05

def layer_norm(vectors, gain):
    centred = vectors - lax.optimization_barrier(jnp.mean(vectors, axis=-1, keepdims=True))
    factor = lax.rsqrt(lax.optimization_barrier(jnp.mean(centred * centred, axis=-1, keepdims=True)) + NORM_EPSILON)
    normal = centred * factor
    return (normal * gain, normal, factor)

def norm_back(grad_out, normal, factor, gain):
    grad_hat = grad_out * gain
    inner = grad_hat - lax.optimization_barrier(jnp.mean(grad_hat, axis=-1, keepdims=True)) - normal * lax.optimization_barrier(jnp.mean(grad_hat * normal, axis=-1, keepdims=True))
    return factor * inner

def offset_table():
    places = jnp.arange(64, dtype=jnp.int32)
    row_of = places // 8
    col_of = places % 8
    offsets = (row_of[:, None] - row_of[None, :] + 7) * 15 + (col_of[:, None] - col_of[None, :] + 7)
    return (offsets.reshape(-1)[:, None] == jnp.arange(225, dtype=jnp.int32)[None, :]).astype(jnp.float32)

def to_windows(grid):
    height, breadth, features = grid.shape
    blocks = grid.reshape(height // 8, 8, breadth // 8, 8, features).transpose(0, 2, 1, 3, 4)
    return blocks.reshape(-1, 64, features)

def from_windows(blocks, height, breadth):
    features = blocks.shape[-1]
    grid = blocks.reshape(height // 8, breadth // 8, 8, 8, features).transpose(0, 2, 1, 3, 4)
    return grid.reshape(height, breadth, features)

def arrange(grid):
    padded = jnp.pad(grid, ((4, 4), (0, 0), (0, 0)))
    return to_windows(jnp.roll(padded, 4, axis=1))

def restore(blocks):
    grid = from_windows(blocks, NLAT + 8, NLON)
    return jnp.roll(grid, -4, axis=1)[4:-4]

def split_heads(blocks):
    return blocks.reshape(blocks.shape[0], 64, HEADS, -1).astype(jnp.float32)

def window_forward(query_win, keys_win, values_win, key_valid, bias):
    query_heads = split_heads(query_win)
    keys_heads = split_heads(keys_win)
    values_heads = split_heads(values_win)
    scores = jnp.einsum('wqhe,wkhe->whqk', query_heads, keys_heads) + bias[None]
    scores = jnp.where(key_valid[:, None, None, :], scores, -1e+30)
    largest = lax.optimization_barrier(jnp.max(scores, axis=-1, keepdims=True))
    exp_scores = jnp.exp(scores - largest)
    attn_probs = exp_scores / lax.optimization_barrier(jnp.sum(exp_scores, axis=-1, keepdims=True))
    probs_low = attn_probs.astype(jnp.bfloat16)
    mixed = jnp.einsum('whqk,wkhe->wqhe', probs_low.astype(jnp.float32), values_heads)
    mixed = mixed.reshape(query_win.shape[0], 64, -1).astype(jnp.bfloat16)
    return (mixed, attn_probs, probs_low)

def window_backward(grad_mixed, query_win, keys_win, values_win, attn_probs, probs_low, onehot):
    window_count = query_win.shape[0]
    grad_heads = split_heads(grad_mixed)
    query_heads = split_heads(query_win)
    keys_heads = split_heads(keys_win)
    values_heads = split_heads(values_win)
    grad_probs = jnp.einsum('wqhe,wkhe->whqk', grad_heads, values_heads)
    grad_values = jnp.einsum('whqk,wqhe->wkhe', probs_low.astype(jnp.float32), grad_heads)
    grad_scores = attn_probs * (grad_probs - lax.optimization_barrier(jnp.sum(attn_probs * grad_probs, axis=-1, keepdims=True)))
    grad_bias = lax.optimization_barrier(jnp.sum(grad_scores, axis=0)).reshape(HEADS, 4096)
    grad_table = jnp.dot(grad_bias, onehot, precision=lax.Precision.HIGHEST)
    scores_low = grad_scores.astype(jnp.bfloat16).astype(jnp.float32)
    grad_query = jnp.einsum('whqk,wkhe->wqhe', scores_low, keys_heads) * 0.125
    grad_keys = jnp.einsum('whqk,wqhe->wkhe', scores_low, query_heads)
    return (grad_query.reshape(window_count, 64, -1), grad_keys.reshape(window_count, 64, -1), grad_values.reshape(window_count, 64, -1), grad_table)

def reference(tokens, cotangent, gain_attn, w_qkv, w_proj, rel_table, gain_mlp, w_fc1, w_fc2):
    grid_shape = (NLAT, NLON, D)
    flat_tokens = tokens.reshape(-1, D).astype(jnp.float32)
    norm1, hat1, factor1 = layer_norm(flat_tokens, gain_attn)
    norm1_low = norm1.astype(jnp.bfloat16)
    qkv = jnp.dot(norm1_low, w_qkv, preferred_element_type=jnp.float32)
    query = (qkv[:, :D] * 0.125).astype(jnp.bfloat16)
    keys = qkv[:, D:2 * D].astype(jnp.bfloat16)
    values = qkv[:, 2 * D:].astype(jnp.bfloat16)
    onehot = offset_table()
    bias = jnp.dot(rel_table, onehot.T, precision=lax.Precision.HIGHEST).reshape(HEADS, 64, 64)
    key_valid = arrange(jnp.ones((NLAT, NLON, 1), jnp.float32))[..., 0] > 0.5
    query_win = arrange(query.reshape(grid_shape))
    keys_win = arrange(keys.reshape(grid_shape))
    values_win = arrange(values.reshape(grid_shape))
    mixed, attn_probs, probs_low = window_forward(query_win, keys_win, values_win, key_valid, bias)
    attended = restore(mixed).reshape(-1, D)
    resid = flat_tokens + jnp.dot(attended, w_proj, preferred_element_type=jnp.float32)
    norm2, hat2, factor2 = layer_norm(resid, gain_mlp)
    norm2_low = norm2.astype(jnp.bfloat16)
    hidden = jnp.dot(norm2_low, w_fc1, preferred_element_type=jnp.float32)
    active, gelu_back = jax.vjp(jax.nn.gelu, hidden)
    active_low = active.astype(jnp.bfloat16)
    output = (resid + jnp.dot(active_low, w_fc2, preferred_element_type=jnp.float32)).astype(jnp.bfloat16)
    grad_out = cotangent.reshape(-1, D)
    grad_fc2 = jnp.dot(active_low.T, grad_out, preferred_element_type=jnp.float32)
    grad_active = jnp.dot(grad_out, w_fc2.T, preferred_element_type=jnp.float32)
    grad_hidden = gelu_back(grad_active)[0].astype(jnp.bfloat16)
    grad_fc1 = jnp.dot(norm2_low.T, grad_hidden, preferred_element_type=jnp.float32)
    grad_norm2 = jnp.dot(grad_hidden, w_fc1.T, preferred_element_type=jnp.float32)
    grad_gain_mlp = lax.optimization_barrier(jnp.sum(grad_norm2 * hat2, axis=0))
    grad_resid = grad_out.astype(jnp.float32) + norm_back(grad_norm2, hat2, factor2, gain_mlp)
    grad_resid_low = grad_resid.astype(jnp.bfloat16)
    grad_proj = jnp.dot(attended.T, grad_resid_low, preferred_element_type=jnp.float32)
    grad_attended = jnp.dot(grad_resid_low, w_proj.T, preferred_element_type=jnp.float32).astype(jnp.bfloat16)
    grad_query, grad_keys, grad_values, grad_table = window_backward(arrange(grad_attended.reshape(grid_shape)), query_win, keys_win, values_win, attn_probs, probs_low, onehot)
    grad_rows = jnp.concatenate([restore(grad_query), restore(grad_keys), restore(grad_values)], axis=-1)
    grad_rows = grad_rows.reshape(-1, 3 * D).astype(jnp.bfloat16)
    grad_qkv = jnp.dot(norm1_low.T, grad_rows, preferred_element_type=jnp.float32)
    grad_norm1 = jnp.dot(grad_rows, w_qkv.T, preferred_element_type=jnp.float32)
    grad_gain_attn = lax.optimization_barrier(jnp.sum(grad_norm1 * hat1, axis=0))
    grad_tokens = (grad_resid + norm_back(grad_norm1, hat1, factor1, gain_attn)).reshape(grid_shape)
    return (output.reshape(grid_shape), grad_tokens, grad_qkv, grad_proj, grad_table, grad_fc1, grad_fc2, grad_gain_attn, grad_gain_mlp)
```

```python
import jax
import jax.numpy as jnp
from jax import lax
from jax.experimental import pallas as pl
from jax.experimental.pallas import tpu as pltpu
from jax.sharding import PartitionSpec as P

NORM_EPSILON = 1e-05
D = 512


def padded(shard, sides, width, wrap):
    for axis, dim in sides:
        count, length = (lax.axis_size(axis), shard.shape[dim])
        up = [(i, (i + 1) % count) for i in range(count if wrap else count - 1)]
        down = [(j, i) for i, j in up]
        last = lax.slice_in_dim(shard, length - width, length, axis=dim)
        initial = lax.slice_in_dim(shard, 0, width, axis=dim)
        before = lax.ppermute(last, axis, up)
        after = lax.ppermute(initial, axis, down)
        shard = jnp.concatenate([before, shard, after], axis=dim)
    return shard


def layer_norm(vectors, gain):
    centred = vectors - jnp.mean(vectors, axis=-1, keepdims=True)
    factor = lax.rsqrt(jnp.mean(centred * centred, axis=-1, keepdims=True) + NORM_EPSILON)
    normal = centred * factor
    return (normal * gain, normal, factor)


def norm_back(grad_out, normal, factor, gain):
    grad_hat = grad_out * gain
    inner = (
        grad_hat
        - jnp.mean(grad_hat, axis=-1, keepdims=True)
        - normal * jnp.mean(grad_hat * normal, axis=-1, keepdims=True)
    )
    return factor * inner


def offset_table():
    places = jnp.arange(64, dtype=jnp.int32)
    row_of = places // 8
    col_of = places % 8
    offsets = (row_of[:, None] - row_of[None, :] + 7) * 15 + (col_of[:, None] - col_of[None, :] + 7)
    return (offsets.reshape(-1)[:, None] == jnp.arange(225, dtype=jnp.int32)[None, :]).astype(
        jnp.float32
    )


def to_windows(grid):
    height, breadth, features = grid.shape
    blocks = grid.reshape(height // 8, 8, breadth // 8, 8, features).transpose(0, 2, 1, 3, 4)
    return blocks.reshape(-1, 64, features)


def from_windows(blocks, height, breadth):
    features = blocks.shape[-1]
    grid = blocks.reshape(height // 8, breadth // 8, 8, 8, features).transpose(0, 2, 1, 3, 4)
    return grid.reshape(height, breadth, features)


def split_heads(blocks, head_count):
    return blocks.reshape(blocks.shape[0], 64, head_count, -1)


def window_forward(query_win, keys_win, values_win, key_valid, bias):
    head_count = bias.shape[0]
    query_heads = split_heads(query_win, head_count)
    keys_heads = split_heads(keys_win, head_count)
    values_heads = split_heads(values_win, head_count)
    scores = (
        jnp.einsum("wqhe,wkhe->whqk", query_heads, keys_heads, preferred_element_type=jnp.float32)
        + bias[None]
    )
    scores = jnp.where(key_valid[:, None, None, :], scores, -1e30)
    largest = jnp.max(scores, axis=-1, keepdims=True)
    exp_scores = jnp.exp(scores - largest)
    attn_probs = exp_scores / jnp.sum(exp_scores, axis=-1, keepdims=True)
    probs_low = attn_probs.astype(jnp.bfloat16)
    mixed = jnp.einsum(
        "whqk,wkhe->wqhe", probs_low, values_heads, preferred_element_type=jnp.float32
    )
    mixed = mixed.reshape(query_win.shape[0], 64, -1).astype(jnp.bfloat16)
    return (mixed, attn_probs, probs_low)


def window_backward(grad_mixed, query_win, keys_win, values_win, attn_probs, probs_low, onehot):
    head_count = attn_probs.shape[1]
    window_count = query_win.shape[0]
    grad_heads = split_heads(grad_mixed, head_count)
    query_heads = split_heads(query_win, head_count)
    keys_heads = split_heads(keys_win, head_count)
    values_heads = split_heads(values_win, head_count)
    grad_probs = jnp.einsum(
        "wqhe,wkhe->whqk", grad_heads, values_heads, preferred_element_type=jnp.float32
    )
    grad_values = jnp.einsum(
        "whqk,wqhe->wkhe", probs_low, grad_heads, preferred_element_type=jnp.float32
    )
    grad_scores = attn_probs * (
        grad_probs - jnp.sum(attn_probs * grad_probs, axis=-1, keepdims=True)
    )
    grad_bias = jnp.sum(grad_scores, axis=0).reshape(head_count, 4096)
    grad_table = jnp.dot(grad_bias, onehot, precision=lax.Precision.HIGHEST)
    scores_low = grad_scores.astype(jnp.bfloat16)
    grad_query = (
        jnp.einsum("whqk,wkhe->wqhe", scores_low, keys_heads, preferred_element_type=jnp.float32)
        * 0.125
    )
    grad_keys = jnp.einsum(
        "whqk,wqhe->wkhe", scores_low, query_heads, preferred_element_type=jnp.float32
    )
    return (
        grad_query.reshape(window_count, 64, -1),
        grad_keys.reshape(window_count, 64, -1),
        grad_values.reshape(window_count, 64, -1),
        grad_table,
    )


def fold_rims(grad_outer):
    edge_rows = jnp.concatenate([grad_outer[:4], grad_outer[-4:]], axis=0)
    got_rows = padded(edge_rows.astype(jnp.bfloat16), (("lat", 0),), 4, False).astype(
        edge_rows.dtype
    )
    inner = grad_outer[4:-4]
    inner = inner.at[:4].add(got_rows[:4]).at[-4:].add(got_rows[-4:])
    edge_cols = jnp.concatenate([inner[:, :4], inner[:, -4:]], axis=1)
    got_cols = padded(edge_cols.astype(jnp.bfloat16), (("lon", 1),), 4, True).astype(
        edge_cols.dtype
    )
    inner = inner[:, 4:-4]
    return inner.at[:, :4].add(got_cols[:, :4]).at[:, -4:].add(got_cols[:, -4:])


MESH = pl.DeviceIdType.MESH
F32 = jnp.float32
BF16 = jnp.bfloat16


def place():
    lat = lax.axis_index("lat")
    lon = lax.axis_index("lon")
    return {
        "c": lax.rem(lon, 2),
        "x": lax.rem(lon // 2, 4),
        "y": lat // 2,
        "z": (lon // 8) * 2 + lax.rem(lat, 2),
    }


def moved(at, axis, step):
    size = 2 if axis == "c" else 4
    there = dict(at)
    there[axis] = lax.rem(at[axis] + step, size)
    lat = there["y"] * 2 + lax.rem(there["z"], 2)
    lon = (there["z"] // 2) * 8 + there["x"] * 2 + there["c"]
    return (lat, lon)


class Copies:
    def __init__(self, send_sems, recv_sems):
        self.send_sems, self.recv_sems, self.used = send_sems, recv_sems, 0

    def start(self, src, dst, device):
        copy = pltpu.make_async_remote_copy(
            src_ref=src,
            dst_ref=dst,
            send_sem=self.send_sems.at[self.used],
            recv_sem=self.recv_sems.at[self.used],
            device_id=device,
            device_id_type=MESH,
        )
        self.used += 1
        copy.start()
        return copy


def add_into(target, other, count):
    @pl.loop(0, count)
    def _(i):
        target[i] = (target[i].astype(F32) + other[i].astype(F32)).astype(BF16)


def greet(at, hops):
    barrier = pltpu.get_barrier_semaphore()
    for axis, step in hops:
        pl.semaphore_signal(barrier, inc=1, device_id=moved(at, axis, step), device_id_type=MESH)
    pl.semaphore_wait(barrier, len(hops))


class Part:
    def __init__(self, at, copies, axes, own, pair, half1, piece1, half2, piece2):
        self.at, self.copies = at, copies
        self.first, self.second = axes
        self.own, self.pair = own, pair
        self.half1, self.piece1, self.half2, self.piece2 = half1, piece1, half2, piece2
        self.rows = own.shape[3]

    def slot(self, step):
        return lax.rem(self.at[self.first] + step, 4)

    def begin(self):
        c = self.at["c"]
        self.pair_copies = {}
        for step in (2, 1, 3, 0):
            j = self.slot(step)
            self.pair_copies[step] = self.copies.start(
                self.own.at[1 - c, j], self.pair.at[j], moved(self.at, "c", 1)
            )

    def pair_sum(self, step):
        self.pair_copies[step].wait()
        j = self.slot(step)
        add_into(self.pair.at[j], self.own.at[self.at["c"], j], 4)

    def first_halves(self):
        self.pair_sum(2)
        j = self.slot(2)
        self.up = self.copies.start(
            self.pair.at[j, 0:2], self.half1.at[0], moved(self.at, self.first, 1)
        )
        self.down = self.copies.start(
            self.pair.at[j, 2:4], self.half1.at[1], moved(self.at, self.first, 3)
        )
        self.pair_sum(1)
        self.pair_sum(3)

    def first_pieces(self):
        self.up.wait()
        add_into(self.pair.at[self.slot(1), 0:2], self.half1.at[0], 2)
        self.up = self.copies.start(
            self.pair.at[self.slot(1)], self.piece1.at[0], moved(self.at, self.first, 1)
        )
        self.down.wait()
        add_into(self.pair.at[self.slot(3), 2:4], self.half1.at[1], 2)
        self.down = self.copies.start(
            self.pair.at[self.slot(3)], self.piece1.at[1], moved(self.at, self.first, 3)
        )
        self.pair_sum(0)

    def second_halves(self):
        self.up.wait()
        self.down.wait()
        mine = self.pair.at[self.slot(0)]

        @pl.loop(0, 4)
        def _(i):
            total = (
                mine[i].astype(F32)
                + self.piece1[0, i].astype(F32)
                + self.piece1[1, i].astype(F32)
            )
            mine[i] = total.astype(BF16)

        k, half = lax.rem(self.at[self.second] + 2, 4), self.rows // 2
        self.up = self.copies.start(
            mine.at[k, 0:half], self.half2.at[0], moved(self.at, self.second, 1)
        )
        self.down = self.copies.start(
            mine.at[k, half : 2 * half], self.half2.at[1], moved(self.at, self.second, 3)
        )

    def second_pieces(self):
        mine, half = self.pair.at[self.slot(0)], self.rows // 2
        k = lax.rem(self.at[self.second] + 1, 4)
        self.up.wait()
        mine[k, 0:half] = (mine[k, 0:half].astype(F32) + self.half2[0].astype(F32)).astype(BF16)
        self.up = self.copies.start(
            mine.at[k], self.piece2.at[0], moved(self.at, self.second, 1)
        )
        k = lax.rem(self.at[self.second] + 3, 4)
        self.down.wait()
        mine[k, half : 2 * half] = (
            mine[k, half : 2 * half].astype(F32) + self.half2[1].astype(F32)
        ).astype(BF16)
        self.down = self.copies.start(
            mine.at[k], self.piece2.at[1], moved(self.at, self.second, 3)
        )

    def finish(self):
        self.up.wait()
        self.down.wait()
        k = self.at[self.second]
        return (
            self.pair[self.slot(0), k].astype(F32)
            + self.piece2[0].astype(F32)
            + self.piece2[1].astype(F32)
        )


def part_scratch(rows, columns=D):
    return [
        pltpu.VMEM((4, 4, rows, columns), BF16),
        pltpu.VMEM((2, 2, rows, columns), BF16),
        pltpu.VMEM((2, 4, rows, columns), BF16),
        pltpu.VMEM((2, rows // 2, columns), BF16),
        pltpu.VMEM((2, rows, columns), BF16),
    ]


def share_all(at, copies, axis, held, slots):
    size = 2 if axis == "c" else 4
    slots[at[axis]] = held[...]
    return [
        copies.start(held, slots.at[at[axis]], moved(at, axis, step)) for step in range(1, size)
    ]


def sum_shared(started, held, slots):
    for copy in started:
        copy.wait()
    total = slots[0]
    for i in range(1, slots.shape[0]):
        total = total + slots[i]
    held[...] = total


def reduce_kernel(
    grad_a, grad_b, small, qkv_out, proj_out, fc1_out, fc2_out, small_out, *scratch
):
    a_bufs, b_bufs = scratch[0:5], scratch[5:10]
    lines, line_in, held, pair_slots, slots, send_sems, recv_sems = scratch[10:]
    at = place()
    copies = Copies(send_sems, recv_sems)
    greet(
        at,
        [("c", 1)] + [(axis, step) for axis in ("y", "z", "x") for step in (1, 2, 3)],
    )
    part_a = Part(at, copies, ("y", "z"), grad_a, *a_bufs)
    part_b = Part(at, copies, ("z", "y"), grad_b, *b_bufs)
    held[0] = small[...]
    part_a.begin()
    part_b.begin()
    shared = share_all(at, copies, "c", held.at[0], pair_slots)
    part_a.first_halves()
    part_b.first_halves()
    sum_shared(shared, held.at[1], pair_slots)
    shared = share_all(at, copies, "y", held.at[1], slots.at[0])
    part_a.first_pieces()
    part_b.first_pieces()
    sum_shared(shared, held.at[2], slots.at[0])
    shared = share_all(at, copies, "z", held.at[2], slots.at[1])
    part_a.second_halves()
    part_b.second_halves()
    sum_shared(shared, held.at[3], slots.at[1])
    shared = share_all(at, copies, "x", held.at[3], slots.at[2])
    part_a.second_pieces()
    part_b.second_pieces()
    total_a = part_a.finish()
    total_b = part_b.finish()
    for x in range(4):
        four = slice(4 * x, 4 * x + 4)
        rows = [total_a[64:80][four], total_a[80:96][four], total_b[80:96][four], total_b[64:80][four]]
        rows += [total_b[16 * i : 16 * i + 16][four] for i in range(4)]
        lines[x] = jnp.concatenate(rows + [total_a[16 * x : 16 * x + 16]], axis=0).astype(BF16)
    started = [
        copies.start(
            lines.at[lax.rem(at["x"] + step, 4)], line_in.at[step - 1], moved(at, "x", step)
        )
        for step in (1, 2, 3)
    ]
    total = lines[at["x"]].astype(F32)
    for step in (1, 2, 3):
        started[step - 1].wait()
        total = total + line_in[step - 1].astype(F32)
    for i in range(3):
        qkv_out[:, 512 * i : 512 * i + 512] = total[4 * i : 4 * i + 4]
    proj_out[...] = total[12:16]
    for i in range(4):
        fc1_out[:, 512 * i : 512 * i + 512] = total[16 + 4 * i : 20 + 4 * i]
    fc2_out[...] = total[32:48]
    sum_shared(shared, small_out, slots.at[2])


def by_device(grad, first_z):
    each = grad.shape[0] // 128
    wide = grad.shape[1] // D
    split = grad.reshape(4, 2, 2, 4, 2, each, wide, D)
    order = (4, 2, 1, 0, 6, 3, 5, 7) if first_z else (4, 0, 2, 1, 6, 3, 5, 7)
    return split.transpose(order).reshape(2, 4, 4, wide * 4 * each, D).astype(BF16)


def reduce_all(grad_qkv, grad_proj, grad_fc1, grad_fc2, small):
    grad_a = jnp.concatenate(
        [by_device(grad_fc2, False), by_device(grad_qkv[:, : 2 * D], False)], axis=3
    )
    grad_b = jnp.concatenate(
        [
            by_device(grad_fc1, True),
            by_device(grad_proj, True),
            by_device(grad_qkv[:, 2 * D :], True),
        ],
        axis=3,
    )
    copies = 40
    return pl.pallas_call(
        reduce_kernel,
        out_shape=(
            jax.ShapeDtypeStruct((4, 3 * D), F32),
            jax.ShapeDtypeStruct((4, D), F32),
            jax.ShapeDtypeStruct((4, 4 * D), F32),
            jax.ShapeDtypeStruct((16, D), F32),
            jax.ShapeDtypeStruct((8, D), F32),
        ),
        in_specs=[pl.BlockSpec(memory_space=pltpu.VMEM)] * 3,
        out_specs=[pl.BlockSpec(memory_space=pltpu.VMEM)] * 5,
        scratch_shapes=part_scratch(96)
        + part_scratch(96)
        + [
            pltpu.VMEM((4, 48, D), BF16),
            pltpu.VMEM((3, 48, D), BF16),
            pltpu.VMEM((4, 8, D), F32),
            pltpu.VMEM((2, 8, D), F32),
            pltpu.VMEM((3, 4, 8, D), F32),
            pltpu.SemaphoreType.DMA((copies,)),
            pltpu.SemaphoreType.DMA((copies,)),
        ],
        compiler_params=pltpu.CompilerParams(
            collective_id=0, has_side_effects=True, vmem_limit_bytes=56 * 2**20
        ),
        name="reduce_grads",
    )(grad_a, grad_b, small)


def shards(tokens, cotangent, gain_attn, w_qkv, w_proj, rel_table, gain_mlp, w_fc1, w_fc2):
    lat_rows, lon_cols, features = tokens.shape
    outer_rows = lat_rows + 8
    outer_cols = lon_cols + 8
    flat_tokens = tokens.reshape(-1, features).astype(jnp.float32)
    norm1, hat1, factor1 = layer_norm(flat_tokens, gain_attn)
    norm1_low = norm1.astype(jnp.bfloat16)
    qkv = jnp.dot(norm1_low, w_qkv, preferred_element_type=jnp.float32)
    query = (qkv[:, :features] * 0.125).astype(jnp.bfloat16)
    own_pairs = qkv[:, features:].astype(jnp.bfloat16).reshape(lat_rows, lon_cols, 2 * features)
    pairs = padded(own_pairs, (("lat", 0), ("lon", 1)), 4, True)
    query_outer = jnp.pad(query.reshape(lat_rows, lon_cols, features), ((4, 4), (4, 4), (0, 0)))
    query_win = to_windows(query_outer)
    keys_win = to_windows(pairs[..., :features])
    values_win = to_windows(pairs[..., features:])
    lat_total = lat_rows * lax.axis_size("lat")
    row_place = lax.axis_index("lat") * lat_rows - 4 + jnp.arange(outer_rows, dtype=jnp.int32)
    inside = ((row_place >= 0) & (row_place < lat_total)).astype(jnp.float32)
    key_valid = (
        to_windows(jnp.broadcast_to(inside[:, None, None], (outer_rows, outer_cols, 1)))[..., 0]
        > 0.5
    )
    onehot = offset_table()
    head_count = rel_table.shape[0]
    bias = jnp.dot(rel_table, onehot.T, precision=lax.Precision.HIGHEST).reshape(head_count, 64, 64)
    mixed, attn_probs, probs_low = window_forward(query_win, keys_win, values_win, key_valid, bias)
    attended = from_windows(mixed, outer_rows, outer_cols)[4:-4, 4:-4].reshape(-1, features)
    resid = flat_tokens + jnp.dot(attended, w_proj, preferred_element_type=jnp.float32)
    norm2, hat2, factor2 = layer_norm(resid, gain_mlp)
    norm2_low = norm2.astype(jnp.bfloat16)
    hidden = jnp.dot(norm2_low, w_fc1, preferred_element_type=jnp.float32)
    active, gelu_back = jax.vjp(jax.nn.gelu, hidden)
    active_low = active.astype(jnp.bfloat16)
    output = (resid + jnp.dot(active_low, w_fc2, preferred_element_type=jnp.float32)).astype(
        jnp.bfloat16
    )
    grad_out = cotangent.reshape(-1, features)
    grad_fc2 = jnp.dot(active_low.T, grad_out, preferred_element_type=jnp.float32)
    grad_active = jnp.dot(grad_out, w_fc2.T, preferred_element_type=jnp.float32)
    grad_hidden = gelu_back(grad_active)[0].astype(jnp.bfloat16)
    grad_fc1 = jnp.dot(norm2_low.T, grad_hidden, preferred_element_type=jnp.float32)
    grad_norm2 = jnp.dot(grad_hidden, w_fc1.T, preferred_element_type=jnp.float32)
    grad_gain_mlp = jnp.sum(grad_norm2 * hat2, axis=0)
    grad_resid = grad_out.astype(jnp.float32) + norm_back(grad_norm2, hat2, factor2, gain_mlp)
    grad_resid_low = grad_resid.astype(jnp.bfloat16)
    grad_proj = jnp.dot(attended.T, grad_resid_low, preferred_element_type=jnp.float32)
    grad_attended = jnp.dot(grad_resid_low, w_proj.T, preferred_element_type=jnp.float32).astype(
        jnp.bfloat16
    )
    grad_outer = jnp.pad(
        grad_attended.reshape(lat_rows, lon_cols, features), ((4, 4), (4, 4), (0, 0))
    )
    grad_query, grad_keys, grad_values, grad_table = window_backward(
        to_windows(grad_outer), query_win, keys_win, values_win, attn_probs, probs_low, onehot
    )
    grad_query_own = from_windows(grad_query, outer_rows, outer_cols)[4:-4, 4:-4]
    grad_pairs = from_windows(
        jnp.concatenate([grad_keys, grad_values], axis=-1), outer_rows, outer_cols
    )
    grad_pairs = fold_rims(grad_pairs)
    grad_rows = (
        jnp.concatenate([grad_query_own, grad_pairs], axis=-1)
        .reshape(-1, 3 * features)
        .astype(jnp.bfloat16)
    )
    grad_qkv = jnp.dot(norm1_low.T, grad_rows, preferred_element_type=jnp.float32)
    grad_norm1 = jnp.dot(grad_rows, w_qkv.T, preferred_element_type=jnp.float32)
    grad_gain_attn = jnp.sum(grad_norm1 * hat1, axis=0)
    grad_tokens = grad_resid + norm_back(grad_norm1, hat1, factor1, gain_attn)
    small = jnp.concatenate(
        [
            grad_gain_attn[None],
            grad_gain_mlp[None],
            jnp.pad(grad_table, ((0, 0), (0, 31))).reshape(4, D),
            jnp.zeros((2, D), F32),
        ],
        axis=0,
    )
    grad_qkv, grad_proj, grad_fc1, grad_fc2, small = reduce_all(
        grad_qkv, grad_proj, grad_fc1, grad_fc2, small
    )
    grad_gain_attn, grad_gain_mlp = small[0], small[1]
    grad_table = small[2:6].reshape(head_count, 256)[:, :225]
    return (
        output.reshape(lat_rows, lon_cols, features),
        grad_tokens.reshape(lat_rows, lon_cols, features),
        grad_qkv,
        grad_proj,
        grad_table,
        grad_fc1,
        grad_fc2,
        grad_gain_attn,
        grad_gain_mlp,
    )


def solution(mesh):
    placed = (P("lat", "lon", None), P("lat", "lon", None), P(), P(), P(), P(), P(), P(), P())
    return jax.shard_map(
        shards,
        mesh=mesh,
        in_specs=placed,
        out_specs=(
            P("lat", "lon", None),
            P("lat", "lon", None),
            P(("lat", "lon"), None),
            P(("lat", "lon"), None),
            P(),
            P(("lat", "lon"), None),
            P(("lat", "lon"), None),
            P(),
            P(),
        ),
        check_vma=False,
    )
```

```python
import jax
import jax.numpy as jnp
from jax import lax
from jax.experimental import pallas as pl
from jax.experimental.pallas import tpu as pltpu
from jax.sharding import PartitionSpec as P

NORM_EPSILON = 1e-05
D = 512


MESH = pl.DeviceIdType.MESH
F32 = jnp.float32
BF16 = jnp.bfloat16


def place():
    lat = lax.axis_index("lat")
    lon = lax.axis_index("lon")
    return {
        "c": lax.rem(lon, 2),
        "x": lax.rem(lon // 2, 4),
        "y": lat // 2,
        "z": (lon // 8) * 2 + lax.rem(lat, 2),
    }


def moved(at, axis, step):
    size = 2 if axis == "c" else 4
    there = dict(at)
    there[axis] = lax.rem(at[axis] + step, size)
    lat = there["y"] * 2 + lax.rem(there["z"], 2)
    lon = (there["z"] // 2) * 8 + there["x"] * 2 + there["c"]
    return (lat, lon)


class Copies:
    def __init__(self, send_sems, recv_sems):
        self.send_sems, self.recv_sems, self.used = send_sems, recv_sems, 0

    def start(self, src, dst, device):
        copy = pltpu.make_async_remote_copy(
            src_ref=src,
            dst_ref=dst,
            send_sem=self.send_sems.at[self.used],
            recv_sem=self.recv_sems.at[self.used],
            device_id=device,
            device_id_type=MESH,
        )
        self.used += 1
        copy.start()
        return copy


def add_into(target, other, count):
    @pl.loop(0, count)
    def _(i):
        target[i] = (target[i].astype(F32) + other[i].astype(F32)).astype(BF16)


def greet(at, hops, shifts):
    barrier = pltpu.get_barrier_semaphore()
    for step in shifts:
        pl.semaphore_signal(barrier, inc=1, device_id=neighbour(*step), device_id_type=MESH)
    for axis, step in hops:
        pl.semaphore_signal(barrier, inc=1, device_id=moved(at, axis, step), device_id_type=MESH)
    pl.semaphore_wait(barrier, len(hops) + len(shifts))


class Part:
    def __init__(self, at, copies, axes, own, pair, half1, piece1, half2, piece2):
        self.at, self.copies = at, copies
        self.first, self.second = axes
        self.own, self.pair = own, pair
        self.half1, self.piece1, self.half2, self.piece2 = half1, piece1, half2, piece2
        self.rows = own.shape[3]

    def slot(self, step):
        return lax.rem(self.at[self.first] + step, 4)

    def begin(self):
        c = self.at["c"]
        self.pair_copies = {}
        for step in (2, 1, 3, 0):
            j = self.slot(step)
            self.pair_copies[step] = self.copies.start(
                self.own.at[1 - c, j], self.pair.at[j], moved(self.at, "c", 1)
            )

    def pair_sum(self, step):
        self.pair_copies[step].wait()
        j = self.slot(step)
        add_into(self.pair.at[j], self.own.at[self.at["c"], j], 4)

    def first_halves(self):
        self.pair_sum(2)
        j = self.slot(2)
        self.up = self.copies.start(
            self.pair.at[j, 0:2], self.half1.at[0], moved(self.at, self.first, 1)
        )
        self.down = self.copies.start(
            self.pair.at[j, 2:4], self.half1.at[1], moved(self.at, self.first, 3)
        )
        self.pair_sum(1)
        self.pair_sum(3)

    def first_pieces(self):
        self.up.wait()
        add_into(self.pair.at[self.slot(1), 0:2], self.half1.at[0], 2)
        self.up = self.copies.start(
            self.pair.at[self.slot(1)], self.piece1.at[0], moved(self.at, self.first, 1)
        )
        self.down.wait()
        add_into(self.pair.at[self.slot(3), 2:4], self.half1.at[1], 2)
        self.down = self.copies.start(
            self.pair.at[self.slot(3)], self.piece1.at[1], moved(self.at, self.first, 3)
        )
        self.pair_sum(0)

    def second_halves(self):
        self.up.wait()
        self.down.wait()
        mine = self.pair.at[self.slot(0)]

        @pl.loop(0, 4)
        def _(i):
            total = (
                mine[i].astype(F32)
                + self.piece1[0, i].astype(F32)
                + self.piece1[1, i].astype(F32)
            )
            mine[i] = total.astype(BF16)

        k, half = lax.rem(self.at[self.second] + 2, 4), self.rows // 2
        self.up = self.copies.start(
            mine.at[k, 0:half], self.half2.at[0], moved(self.at, self.second, 1)
        )
        self.down = self.copies.start(
            mine.at[k, half : 2 * half], self.half2.at[1], moved(self.at, self.second, 3)
        )

    def second_pieces(self):
        mine, half = self.pair.at[self.slot(0)], self.rows // 2
        k = lax.rem(self.at[self.second] + 1, 4)
        self.up.wait()
        mine[k, 0:half] = (mine[k, 0:half].astype(F32) + self.half2[0].astype(F32)).astype(BF16)
        self.up = self.copies.start(
            mine.at[k], self.piece2.at[0], moved(self.at, self.second, 1)
        )
        k = lax.rem(self.at[self.second] + 3, 4)
        self.down.wait()
        mine[k, half : 2 * half] = (
            mine[k, half : 2 * half].astype(F32) + self.half2[1].astype(F32)
        ).astype(BF16)
        self.down = self.copies.start(
            mine.at[k], self.piece2.at[1], moved(self.at, self.second, 3)
        )

    def finish(self):
        self.up.wait()
        self.down.wait()
        k = self.at[self.second]
        return (
            self.pair[self.slot(0), k].astype(F32)
            + self.piece2[0].astype(F32)
            + self.piece2[1].astype(F32)
        )


def part_scratch(rows, columns=D):
    return [
        pltpu.VMEM((4, 4, rows, columns), BF16),
        pltpu.VMEM((2, 2, rows, columns), BF16),
        pltpu.VMEM((2, 4, rows, columns), BF16),
        pltpu.VMEM((2, rows // 2, columns), BF16),
        pltpu.VMEM((2, rows, columns), BF16),
    ]


def share_all(at, copies, axis, held, slots):
    size = 2 if axis == "c" else 4
    slots[at[axis]] = held[...]
    return [
        copies.start(held, slots.at[at[axis]], moved(at, axis, step)) for step in range(1, size)
    ]


def sum_shared(started, held, slots):
    for copy in started:
        copy.wait()
    total = slots[0]
    for i in range(1, slots.shape[0]):
        total = total + slots[i]
    held[...] = total


def reduce_kernel(
    grad_a, grad_b, small, out_grid, grad_grid,
    qkv_out, proj_out, fc1_out, fc2_out, small_out, output, grad_tokens, *scratch
):
    a_bufs, b_bufs = scratch[0:5], scratch[5:10]
    lines, line_in, held, pair_slots, slots, send_sems, recv_sems = scratch[10:17]
    out_bufs, token_bufs = scratch[17:21], scratch[21:25]
    at = place()
    copies = Copies(send_sems, recv_sems)
    greet(
        at,
        [("c", 1)] + [(axis, step) for axis in ("y", "z", "x") for step in (1, 2, 3)],
        ((1, 0), (0, 1), (1, 1), (-1, 0), (0, -1), (-1, -1)),
    )
    part_a = Part(at, copies, ("y", "z"), grad_a, *a_bufs)
    part_b = Part(at, copies, ("z", "y"), grad_b, *b_bufs)
    held[0] = small[...]
    part_a.begin()
    part_b.begin()
    shared = share_all(at, copies, "c", held.at[0], pair_slots)
    out_rows, out_in, out_edge, out_edge_in = out_bufs
    token_rows, token_in, token_edge, token_edge_in = token_bufs
    back_out = shift_back_start(copies, out_grid, out_rows, out_in, out_edge, out_edge_in)
    back_tokens = shift_back_start(
        copies, grad_grid, token_rows, token_in, token_edge, token_edge_in
    )
    part_a.first_halves()
    part_b.first_halves()
    sum_shared(shared, held.at[1], pair_slots)
    shared = share_all(at, copies, "y", held.at[1], slots.at[0])
    part_a.first_pieces()
    part_b.first_pieces()
    sum_shared(shared, held.at[2], slots.at[0])
    shared = share_all(at, copies, "z", held.at[2], slots.at[1])
    part_a.second_halves()
    part_b.second_halves()
    sum_shared(shared, held.at[3], slots.at[1])
    shared = share_all(at, copies, "x", held.at[3], slots.at[2])
    shift_back_finish(back_out, out_grid, out_in, out_edge_in, output)
    shift_back_finish(back_tokens, grad_grid, token_in, token_edge_in, grad_tokens)
    part_a.second_pieces()
    part_b.second_pieces()
    total_a = part_a.finish()
    total_b = part_b.finish()
    for x in range(4):
        four = slice(4 * x, 4 * x + 4)
        rows = [total_a[64:80][four], total_a[80:96][four], total_b[80:96][four], total_b[64:80][four]]
        rows += [total_b[16 * i : 16 * i + 16][four] for i in range(4)]
        lines[x] = jnp.concatenate(rows + [total_a[16 * x : 16 * x + 16]], axis=0).astype(BF16)
    started = [
        copies.start(
            lines.at[lax.rem(at["x"] + step, 4)], line_in.at[step - 1], moved(at, "x", step)
        )
        for step in (1, 2, 3)
    ]
    total = lines[at["x"]].astype(F32)
    for step in (1, 2, 3):
        started[step - 1].wait()
        total = total + line_in[step - 1].astype(F32)
    for i in range(3):
        qkv_out[:, 512 * i : 512 * i + 512] = total[4 * i : 4 * i + 4]
    proj_out[...] = total[12:16]
    for i in range(4):
        fc1_out[:, 512 * i : 512 * i + 512] = total[16 + 4 * i : 20 + 4 * i]
    fc2_out[...] = total[32:48]
    sum_shared(shared, small_out, slots.at[2])


def reduce_all(grad_a, grad_b, small, out_grid, grad_grid):
    copies = 48
    return pl.pallas_call(
        reduce_kernel,
        out_shape=(
            jax.ShapeDtypeStruct((4, 3 * D), F32),
            jax.ShapeDtypeStruct((4, D), F32),
            jax.ShapeDtypeStruct((4, 4 * D), F32),
            jax.ShapeDtypeStruct((16, D), F32),
            jax.ShapeDtypeStruct((2, 8, D), F32),
            jax.ShapeDtypeStruct((8, 48, D), BF16),
            jax.ShapeDtypeStruct((8, 48, D), F32),
        ),
        in_specs=[pl.BlockSpec(memory_space=pltpu.VMEM)] * 5,
        out_specs=[pl.BlockSpec(memory_space=pltpu.VMEM)] * 7,
        scratch_shapes=part_scratch(96)
        + part_scratch(96)
        + [
            pltpu.VMEM((4, 48, D), BF16),
            pltpu.VMEM((3, 48, D), BF16),
            pltpu.VMEM((4, 2, 8, D), F32),
            pltpu.VMEM((2, 2, 8, D), F32),
            pltpu.VMEM((3, 4, 2, 8, D), F32),
            pltpu.SemaphoreType.DMA((copies,)),
            pltpu.SemaphoreType.DMA((copies,)),
        ]
        + ([pltpu.VMEM((4, 48, D), BF16)] + SHIFT_SCRATCH) * 2,
        compiler_params=pltpu.CompilerParams(
            collective_id=0, has_side_effects=True, vmem_limit_bytes=56 * 2**20
        ),
        name="reduce_grads",
    )(grad_a, grad_b, small, out_grid, grad_grid)


def neighbour(step_lat, step_lon):
    return (
        lax.rem(lax.axis_index("lat") + step_lat + 8, 8),
        lax.rem(lax.axis_index("lon") + step_lon + 16, 16),
    )


def greet_shift():
    barrier = pltpu.get_barrier_semaphore()
    steps = ((1, 0), (0, 1), (1, 1), (-1, 0), (0, -1), (-1, -1))
    for step in steps:
        pl.semaphore_signal(barrier, inc=1, device_id=neighbour(*step), device_id_type=MESH)
    pl.semaphore_wait(barrier, len(steps))


def shift_in_start(copies, source, rows_in, edge, edge_in):
    started = [copies.start(source.at[4:8], rows_in, neighbour(1, 0))]
    for half in range(2):
        ends = [source[4 * half + r, 32:48].astype(F32)[12:16] for r in range(4)]
        edge[half] = jnp.concatenate(ends, axis=0).astype(BF16)
    started.append(copies.start(edge.at[0], edge_in.at[0], neighbour(0, 1)))
    started.append(copies.start(edge.at[1], edge_in.at[1], neighbour(1, 1)))
    return started


def shift_in_finish(started, source, rows_in, edge_in, grid):
    for copy in started:
        copy.wait()
    for row in range(8):
        held = (rows_in[row] if row < 4 else source[row - 4]).astype(F32)
        turned = pltpu.roll(held, 4, 0)
        ends = edge_in[1 if row < 4 else 0].astype(F32)[4 * (row % 4) : 4 * (row % 4) + 4]
        grid[row] = jnp.concatenate(
            [jnp.concatenate([ends, turned[4:8]], axis=0), turned[8:48]], axis=0
        )


def shift_back_start(copies, grid, rows_out, rows_in, edge, edge_in):
    for row in range(4):
        rows_out[row] = pltpu.roll(grid[row], 44, 0).astype(BF16)
    started = [copies.start(rows_out, rows_in, neighbour(-1, 0))]
    for half in range(2):
        firsts = [grid[4 * half + r, 0:8][0:4] for r in range(4)]
        edge[half] = jnp.concatenate(firsts, axis=0).astype(BF16)
    started.append(copies.start(edge.at[1], edge_in.at[1], neighbour(0, -1)))
    started.append(copies.start(edge.at[0], edge_in.at[0], neighbour(-1, -1)))
    return started


def shift_back_finish(started, grid, rows_in, edge_in, result):
    for copy in started:
        copy.wait()
    for row in range(8):
        if row < 4:
            turned = pltpu.roll(grid[row + 4], 44, 0)
        else:
            turned = rows_in[row - 4].astype(F32)
        ends = edge_in[1 if row < 4 else 0].astype(F32)[4 * (row % 4) : 4 * (row % 4) + 4]
        whole = jnp.concatenate(
            [turned[0:40], jnp.concatenate([turned[40:44], ends], axis=0)], axis=0
        )
        result[row] = whole.astype(result.dtype)


SHIFT_SCRATCH = [
    pltpu.VMEM((4, 48, D), BF16),
    pltpu.VMEM((2, 16, D), BF16),
    pltpu.VMEM((2, 16, D), BF16),
]


def shift_kernel(tokens, cotangent, x_grid, c_grid, *scratch):
    copies = Copies(*scratch[6:])
    greet_shift()
    started = []
    for source, bufs in ((tokens, scratch[0:3]), (cotangent, scratch[3:6])):
        started.append(shift_in_start(copies, source, *bufs))
    for source, bufs, grid, copied in (
        (tokens, scratch[0:3], x_grid, started[0]),
        (cotangent, scratch[3:6], c_grid, started[1]),
    ):
        shift_in_finish(copied, source, bufs[0], bufs[2], grid)


def shift_in(tokens, cotangent):
    vmem = pl.BlockSpec(memory_space=pltpu.VMEM)
    return pl.pallas_call(
        shift_kernel,
        out_shape=(jax.ShapeDtypeStruct((8, 48, D), F32),) * 2,
        in_specs=[vmem] * 2,
        out_specs=[vmem] * 2,
        scratch_shapes=SHIFT_SCRATCH * 2
        + [pltpu.SemaphoreType.DMA((6,)), pltpu.SemaphoreType.DMA((6,))],
        compiler_params=pltpu.CompilerParams(
            collective_id=1, has_side_effects=True, vmem_limit_bytes=56 * 2**20
        ),
        name="shift_in",
    )(tokens, cotangent)


TOKENS = 384
WINDOWS = 6
PAIRS = 4
TILE = 16


def mm(a, b):
    return lax.dot_general(a, b, (((1,), (0,)), ((), ())), preferred_element_type=F32)


def mm_nt(a, b):
    return lax.dot_general(a, b, (((1,), (1,)), ((), ())), preferred_element_type=F32)


def mm_tn(a, b):
    return lax.dot_general(a, b, (((0,), (0,)), ((), ())), preferred_element_type=F32)


def split_low(value):
    high = value.astype(BF16)
    return high, (value - high.astype(F32)).astype(BF16)


def iota(shape, dim):
    return lax.broadcasted_iota(jnp.int32, shape, dim)


def tiles(body):
    @pl.loop(0, TOKENS // TILE)
    def _(i):
        body(i, pl.ds(pl.multiple_of(i * TILE, TILE), TILE))


def grid_tile(grid, i):
    window, row = i // 4, lax.rem(i, 4) * 2
    columns = pl.ds(pl.multiple_of(window * 8, 8), 8)
    return jnp.concatenate([grid[row, columns], grid[row + 1, columns]], axis=0)


def store_grid_tile(grid, i, tile):
    window, row = i // 4, lax.rem(i, 4) * 2
    columns = pl.ds(pl.multiple_of(window * 8, 8), 8)
    grid[row, columns] = tile[0:8]
    grid[row + 1, columns] = tile[8:16]


def normalise(vectors):
    centred = vectors - jnp.mean(vectors, axis=-1, keepdims=True)
    factor = lax.rsqrt(jnp.mean(centred * centred, axis=-1, keepdims=True) + NORM_EPSILON)
    return centred * factor, factor


def normalise_back(grad_out, normal, factor, gain):
    grad_hat = grad_out * gain
    inner = (
        grad_hat
        - jnp.mean(grad_hat, axis=-1, keepdims=True)
        - normal * jnp.mean(grad_hat * normal, axis=-1, keepdims=True)
    )
    return factor * inner


def line_order(first_z):
    place_of = iota((1, D), 1)
    core, first, second = place_of >> 8, (place_of >> 6) & 3, (place_of >> 4) & 3
    x, r = (place_of >> 2) & 3, place_of & 3
    y, z = (second, first) if first_z else (first, second)
    feature = (y << 7) | ((z & 1) << 6) | ((z >> 1) << 5) | (x << 3) | (core << 2) | r
    return jnp.where(iota((D, D), 0) == feature, 1.0, 0.0).astype(BF16)


def pair_offsets():
    row, column = iota((256, 128), 0), iota((256, 128), 1)
    target = ((column >> 6) << 7) + 15 * ((column >> 3) & 7) + (column & 7)
    return jnp.where(row == target, 1.0, 0.0).astype(BF16)


def store_wide(halves, i, rows):
    halves[0, 8 * i : 8 * i + 8] = rows[:, 0:128]
    halves[1, 8 * i : 8 * i + 8] = rows[:, 128:256]


def load_strided(halves, first):
    return jnp.concatenate([halves[k, pl.ds(first, 8, stride=8), :] for k in range(2)], axis=1)


def expand_bias(rel, table, shifted, bias, masked):
    table[...] = jnp.zeros_like(table)
    table[:, 0:225] = rel[...]
    whole = table[...]
    for b in range(8):
        store_wide(shifted, b, pltpu.roll(whole, (256 - (7 - b)) % 256, 1))
    spread = pair_offsets()
    key, query = iota((64, 128), 0), iota((64, 128), 1) & 63
    apart = jnp.where((key >> 5) == (query >> 5), 0.0, -1e30)
    apart = jnp.where(masked, apart, 0.0)
    for p in range(PAIRS):
        heads = []
        for h in (2 * p, 2 * p + 1):
            rows = load_strided(shifted, h)
            turned = [pltpu.roll(rows, 256 - (105 - 15 * a), 1)[:, 0:128] for a in range(8)]
            heads.append(jnp.concatenate(turned, axis=0))
        high, low = split_low(jnp.concatenate(heads, axis=1))
        bias[p] = mm(high, spread) + mm(low, spread) + apart


def collect_table(grad_bias, collected, total):
    spread = pair_offsets()
    for p in range(PAIRS):
        high, low = split_low(grad_bias[p])
        both = mm_nt(high, spread) + mm_nt(low, spread)
        for k in range(2):
            one = both[:, 128 * k : 128 * k + 128]
            one = jnp.concatenate([one, jnp.zeros_like(one)], axis=1)
            rows = one[56:64]
            for a in range(7):
                rows = rows + pltpu.roll(one[8 * a : 8 * a + 8], 105 - 15 * a, 1)
            h = 2 * p + k
            store_wide(collected, h, rows)
    table = load_strided(collected, 7)
    for b in range(7):
        table = table + pltpu.roll(load_strided(collected, b), 7 - b, 1)
    total[...] = table


def both_heads(pair):
    left = iota(pair.shape, 1) < 64
    zero = jnp.zeros_like(pair)
    return jnp.concatenate([jnp.where(left, pair, zero), jnp.where(left, zero, pair)], axis=0)


def own_heads(crossed):
    return jnp.where(iota((64, 128), 1) < 64, crossed[0:64], crossed[64:128])


def window_rows(w):
    return pl.ds(pl.multiple_of(w * 64, 64), 64)


def attend(w, qkv, bias, probs, attended):
    rows = window_rows(w)
    for p in range(PAIRS):
        query = qkv[rows, 128 * p : 128 * p + 128]
        keys = qkv[rows, D + 128 * p : D + 128 * p + 128]
        values = qkv[rows, 2 * D + 128 * p : 2 * D + 128 * p + 128]
        scores = mm_nt(keys, both_heads(query)) + bias[p]
        powers = jnp.exp(scores - jnp.max(scores, axis=0, keepdims=True))
        each = powers / jnp.sum(powers, axis=0, keepdims=True)
        probs[w, p] = each
        crossed = mm_tn(each.astype(BF16), values)
        attended[rows, 128 * p : 128 * p + 128] = own_heads(crossed).astype(BF16)


def attend_back(w, qkv, probs, grad_attended, grad_bias, grad_rows):
    rows = window_rows(w)
    for p in range(PAIRS):
        query = both_heads(qkv[rows, 128 * p : 128 * p + 128])
        keys = qkv[rows, D + 128 * p : D + 128 * p + 128]
        values = qkv[rows, 2 * D + 128 * p : 2 * D + 128 * p + 128]
        grads = both_heads(grad_attended[rows, 128 * p : 128 * p + 128])
        each = probs[w, p]
        grad_probs = mm_nt(values, grads)
        grad_scores = each * (grad_probs - jnp.sum(each * grad_probs, axis=0, keepdims=True))
        grad_bias[p] += grad_scores
        low = grad_scores.astype(BF16)
        grad_query = own_heads(mm_tn(low, keys)) * 0.125
        grad_rows[rows, 128 * p : 128 * p + 128] = grad_query.astype(BF16)
        grad_rows[rows, D + 128 * p : D + 128 * p + 128] = mm(low, query).astype(BF16)
        grad_rows[rows, 2 * D + 128 * p : 2 * D + 128 * p + 128] = mm(
            each.astype(BF16), grads
        ).astype(BF16)


GELU_SCALE = 0.7978845608028654
GELU_CUBE = 0.044715


def gelu_both(hidden):
    square = hidden * hidden
    swing = jnp.tanh(GELU_SCALE * hidden * (1.0 + GELU_CUBE * square))
    half = 0.5 + 0.5 * swing
    slope = half + (0.5 * GELU_SCALE) * hidden * (1.0 - swing * swing) * (
        1.0 + 3.0 * GELU_CUBE * square
    )
    return hidden * half, slope


def eight(tile):
    return tile[0:8] + tile[8:16]


COMPUTE_SCRATCH = [
    ("hat1", (TOKENS, D), F32),
    ("factor1", (TOKENS, 128), F32),
    ("norm1", (TOKENS, D), BF16),
    ("qkv", (TOKENS, 3 * D), BF16),
    ("attended", (TOKENS, D), BF16),
    ("resid", (TOKENS, D), F32),
    ("hat2", (TOKENS, D), F32),
    ("factor2", (TOKENS, 128), F32),
    ("norm2", (TOKENS, D), BF16),
    ("norm2_z", (TOKENS, D), BF16),
    ("cot", (TOKENS, D), BF16),
    ("hidden", (TOKENS, D), F32),
    ("grad_active", (TOKENS, D), F32),
    ("active", (TOKENS, D), BF16),
    ("grad_hidden", (TOKENS, D), BF16),
    ("mlp_out", (TOKENS, D), F32),
    ("grad_norm", (TOKENS, D), F32),
    ("grad_resid", (TOKENS, D), F32),
    ("grad_resid_low", (TOKENS, D), BF16),
    ("grad_attended", (TOKENS, D), BF16),
    ("grad_rows", (TOKENS, 3 * D), BF16),
    ("probs", (WINDOWS, PAIRS, 64, 128), F32),
    ("bias", (PAIRS, 64, 128), F32),
    ("grad_bias", (PAIRS, 64, 128), F32),
    ("table", (8, 256), F32),
    ("shifted", (2, 64, 128), F32),
    ("gain_sums", (2, 8, D), F32),
]


class Block:
    def __init__(self, refs):
        for (name, _, _), ref in zip(COMPUTE_SCRATCH, refs):
            setattr(self, name, ref)


def attention_forward(s, x_grid, gain_attn, w_qkv, rel, masked):
    expand_bias(rel, s.table, s.shifted, s.bias, masked)

    def first_norm(i, rows):
        normal, factor = normalise(grid_tile(x_grid, i))
        s.hat1[rows] = normal
        s.factor1[rows] = jnp.broadcast_to(factor, (TILE, 128))
        s.norm1[rows] = (normal * gain_attn[...]).astype(BF16)

    tiles(first_norm)
    for i in range(3):
        columns = slice(D * i, D * i + D)
        part = mm(s.norm1[...], w_qkv[:, columns])
        s.qkv[:, columns] = (part * 0.125 if i == 0 else part).astype(BF16)

    @pl.loop(0, WINDOWS)
    def _(w):
        attend(w, s.qkv, s.bias, s.probs, s.attended)


def mlp(s, x_grid, c_grid, w_proj, gain_mlp, w_fc1, w_fc2, out_grid, grad_a, grad_b, each=None):
    s.resid[...] = mm(s.attended[...], w_proj[...])

    def second_norm(i, rows):
        resid = s.resid[rows] + grid_tile(x_grid, i)
        normal, factor = normalise(resid)
        s.resid[rows] = resid
        s.hat2[rows] = normal
        s.factor2[rows] = jnp.broadcast_to(factor, (TILE, 128))
        s.norm2[rows] = (normal * gain_mlp[...]).astype(BF16)
        s.cot[rows] = grid_tile(c_grid, i).astype(BF16)

    tiles(second_norm)
    s.norm2_z[...] = mm(s.norm2[...], line_order(True)).astype(BF16)
    s.mlp_out[...] = jnp.zeros_like(s.mlp_out)
    s.grad_norm[...] = jnp.zeros_like(s.grad_norm)

    @pl.loop(0, 4)
    def _(j):
        columns = pl.ds(pl.multiple_of(j * D, D), D)
        s.hidden[...] = mm(s.norm2[...], w_fc1[:, columns])
        s.grad_active[...] = mm_nt(s.cot[...], w_fc2[columns])

        def bend(_, rows):
            active, slope = gelu_both(s.hidden[rows])
            s.active[rows] = active.astype(BF16)
            s.grad_hidden[rows] = (slope * s.grad_active[rows]).astype(BF16)

        tiles(bend)
        s.mlp_out[...] += mm(s.active[...], w_fc2[columns])
        s.grad_norm[...] += mm_nt(s.grad_hidden[...], w_fc1[:, columns])
        grad_fc1 = mm_tn(s.norm2_z[...], s.grad_hidden[...]).astype(BF16)
        grad_b[:, :, :, pl.ds(pl.multiple_of(j * 16, 16), 16), :] = grad_fc1.reshape(2, 4, 4, 16, D)
        grad_fc2 = mm_tn(s.active[...], s.cot[...]).astype(BF16).reshape(2, 2, 4, 2, 16, D)
        for low in range(2):
            for high in range(2):
                for x in range(4):
                    for c in range(2):
                        grad_a[c, j, 2 * high + low, 16 * x : 16 * x + 16, :] = grad_fc2[
                            low, high, x, c
                        ]

    s.gain_sums[...] = jnp.zeros_like(s.gain_sums)

    def second_back(i, rows):
        grad, normal = s.grad_norm[rows], s.hat2[rows]
        s.gain_sums[1] += eight(grad * normal)
        grad_resid = s.cot[rows].astype(F32) + normalise_back(
            grad, normal, s.factor2[rows][:, 0:1], gain_mlp[...]
        )
        s.grad_resid[rows] = grad_resid
        s.grad_resid_low[rows] = grad_resid.astype(BF16)
        store_grid_tile(out_grid, i, s.resid[rows] + s.mlp_out[rows])

    tiles(second_back)


def attention_backward(s, gain_attn, w_qkv, w_proj, grad_grid, grad_a, grad_b, small):
    by_z = line_order(True)
    s.norm2_z[...] = mm(s.attended[...], by_z).astype(BF16)
    grad_proj = mm_tn(s.norm2_z[...], s.grad_resid_low[...]).astype(BF16)
    grad_b[:, :, :, 64:80, :] = grad_proj.reshape(2, 4, 4, 16, D)
    s.grad_attended[...] = mm_nt(s.grad_resid_low[...], w_proj[...]).astype(BF16)
    s.grad_bias[...] = jnp.zeros_like(s.grad_bias)

    @pl.loop(0, WINDOWS)
    def _(w):
        attend_back(w, s.qkv, s.probs, s.grad_attended, s.grad_bias, s.grad_rows)

    s.norm2_z[...] = mm(s.norm1[...], by_z).astype(BF16)
    grad_values = mm_tn(s.norm2_z[...], s.grad_rows[:, 2 * D : 3 * D]).astype(BF16)
    grad_b[:, :, :, 80:96, :] = grad_values.reshape(2, 4, 4, 16, D)
    s.norm2_z[...] = mm(s.norm1[...], line_order(False)).astype(BF16)
    for i in range(2):
        grad = mm_tn(s.norm2_z[...], s.grad_rows[:, D * i : D * i + D]).astype(BF16)
        grad_a[:, :, :, 64 + 16 * i : 80 + 16 * i, :] = grad.reshape(2, 4, 4, 16, D)
    s.grad_norm[...] = mm_nt(s.grad_rows[...], w_qkv[...])

    def first_back(i, rows):
        grad, normal = s.grad_norm[rows], s.hat1[rows]
        s.gain_sums[0] += eight(grad * normal)
        store_grid_tile(
            grad_grid,
            i,
            s.grad_resid[rows]
            + normalise_back(grad, normal, s.factor1[rows][:, 0:1], gain_attn[...]),
        )

    tiles(first_back)
    collect_table(s.grad_bias, s.shifted, s.table)
    small[...] = jnp.zeros_like(small)
    small[0, 0:1] = jnp.sum(s.gain_sums[0], axis=0, keepdims=True)
    small[0, 1:2] = jnp.sum(s.gain_sums[1], axis=0, keepdims=True)
    small[1, :, 0:256] = s.table[...]


def compute_kernel(
    x_grid, c_grid, gain_attn, w_qkv, w_proj, rel, gain_mlp, w_fc1, w_fc2,
    out_grid, grad_grid, grad_a, grad_b, small, *scratch
):
    s = Block(scratch)
    attention_forward(s, x_grid, gain_attn, w_qkv, rel, lax.axis_index("lat") == 0)
    mlp(s, x_grid, c_grid, w_proj, gain_mlp, w_fc1, w_fc2, out_grid, grad_a, grad_b)
    attention_backward(s, gain_attn, w_qkv, w_proj, grad_grid, grad_a, grad_b, small)


def compute(x_grid, c_grid, gain_attn, w_qkv, w_proj, rel, gain_mlp, w_fc1, w_fc2):
    vmem = pl.BlockSpec(memory_space=pltpu.VMEM)
    return pl.pallas_call(
        compute_kernel,
        out_shape=(
            jax.ShapeDtypeStruct((8, 48, D), F32),
            jax.ShapeDtypeStruct((8, 48, D), F32),
            jax.ShapeDtypeStruct((2, 4, 4, 96, D), BF16),
            jax.ShapeDtypeStruct((2, 4, 4, 96, D), BF16),
            jax.ShapeDtypeStruct((2, 8, D), F32),
        ),
        in_specs=[vmem] * 9,
        out_specs=[vmem] * 5,
        scratch_shapes=[pltpu.VMEM(shape, kind) for _, shape, kind in COMPUTE_SCRATCH],
        compiler_params=pltpu.CompilerParams(vmem_limit_bytes=56 * 2**20),
        name="block",
    )(x_grid, c_grid, gain_attn.reshape(1, D), w_qkv, w_proj, rel, gain_mlp.reshape(1, D), w_fc1, w_fc2)


def shards(tokens, cotangent, gain_attn, w_qkv, w_proj, rel_table, gain_mlp, w_fc1, w_fc2):
    x_grid, c_grid = shift_in(tokens, cotangent)
    out_grid, grad_grid, grad_a, grad_b, small = compute(
        x_grid, c_grid, gain_attn, w_qkv, w_proj, rel_table, gain_mlp, w_fc1, w_fc2
    )
    grad_qkv, grad_proj, grad_fc1, grad_fc2, small, output, grad_tokens = reduce_all(
        grad_a, grad_b, small, out_grid, grad_grid
    )
    return (
        output,
        grad_tokens,
        grad_qkv,
        grad_proj,
        small[1, :, :225],
        grad_fc1,
        grad_fc2,
        small[0, 0],
        small[0, 1],
    )


def solution(mesh):
    placed = (P("lat", "lon", None), P("lat", "lon", None), P(), P(), P(), P(), P(), P(), P())
    return jax.shard_map(
        shards,
        mesh=mesh,
        in_specs=placed,
        out_specs=(
            P("lat", "lon", None),
            P("lat", "lon", None),
            P(("lat", "lon"), None),
            P(("lat", "lon"), None),
            P(),
            P(("lat", "lon"), None),
            P(("lat", "lon"), None),
            P(),
            P(),
        ),
        check_vma=False,
    )
```

```python
import jax
import jax.numpy as jnp
from jax import lax
from jax.experimental import pallas as pl
from jax.experimental.pallas import tpu as pltpu
from jax.sharding import PartitionSpec as P

NORM_EPSILON = 1e-05
D = 512


MESH = pl.DeviceIdType.MESH
F32 = jnp.float32
BF16 = jnp.bfloat16


def place():
    lat = lax.axis_index("lat")
    lon = lax.axis_index("lon")
    return {
        "c": lax.rem(lon, 2),
        "x": lax.rem(lon // 2, 4),
        "y": lat // 2,
        "z": (lon // 8) * 2 + lax.rem(lat, 2),
    }


def moved(at, axis, step):
    size = 2 if axis == "c" else 4
    there = dict(at)
    there[axis] = lax.rem(at[axis] + step, size)
    lat = there["y"] * 2 + lax.rem(there["z"], 2)
    lon = (there["z"] // 2) * 8 + there["x"] * 2 + there["c"]
    return (lat, lon)


def neighbour(step_lat, step_lon):
    return (
        lax.rem(lax.axis_index("lat") + step_lat + 8, 8),
        lax.rem(lax.axis_index("lon") + step_lon + 16, 16),
    )


def greet(at):
    barrier = pltpu.get_barrier_semaphore()
    others = [moved(at, "c", 1)]
    others += [moved(at, axis, step) for axis in ("y", "z", "x") for step in (1, 2, 3)]
    steps = ((1, 0), (0, 1), (1, 1), (-1, 0), (0, -1), (-1, -1))
    others += [neighbour(*step) for step in steps]
    for other in others:
        pl.semaphore_signal(barrier, inc=1, device_id=other, device_id_type=MESH)
    pl.semaphore_wait(barrier, len(others))


class Copies:
    def __init__(self, send_sems, recv_sems):
        self.send_sems, self.recv_sems, self.used = send_sems, recv_sems, 0

    def reserve(self, count):
        self.used += count
        return self.used - count

    def make(self, index, src, dst, device):
        return pltpu.make_async_remote_copy(
            src_ref=src,
            dst_ref=dst,
            send_sem=self.send_sems.at[index],
            recv_sem=self.recv_sems.at[index],
            device_id=device,
            device_id_type=MESH,
        )

    def start(self, src, dst, device):
        copy = self.make(self.reserve(1), src, dst, device)
        copy.start()
        return copy


def add_into(target, other, count):
    @pl.loop(0, count)
    def _(i):
        target[i] = (target[i].astype(F32) + other[i].astype(F32)).astype(BF16)


class Part:
    def __init__(self, at, copies, axes, own, pair, half1, piece1, piece2):
        self.at, self.copies = at, copies
        self.first, self.second = axes
        self.own, self.pair = own, pair
        self.half1, self.piece1, self.piece2 = half1, piece1, piece2
        self.base = copies.reserve(4)

    def slot(self, step):
        return lax.rem(self.at[self.first] + step, 4)

    def pair_copy(self, i):
        j = self.slot(6 - i)
        return self.copies.make(
            self.base + i, self.own.at[1 - self.at["c"], j], self.pair.at[j], moved(self.at, "c", 1)
        )

    def begin(self):
        for i in range(4):
            self.pair_copy(i).start()

    def pair_sum(self, i):
        self.pair_copy(i).wait()
        j = self.slot(6 - i)
        add_into(self.pair.at[j], self.own.at[self.at["c"], j], 4)

    def first_halves(self):
        self.pair_sum(0)
        j = self.slot(2)
        self.up = self.copies.start(
            self.pair.at[j, 0:2], self.half1.at[0], moved(self.at, self.first, 1)
        )
        self.down = self.copies.start(
            self.pair.at[j, 2:4], self.half1.at[1], moved(self.at, self.first, 3)
        )
        self.pair_sum(1)
        self.pair_sum(3)

    def first_pieces(self):
        self.up.wait()
        add_into(self.pair.at[self.slot(1), 0:2], self.half1.at[0], 2)
        self.up = self.copies.start(
            self.pair.at[self.slot(1)], self.piece1.at[0], moved(self.at, self.first, 1)
        )
        self.down.wait()
        add_into(self.pair.at[self.slot(3), 2:4], self.half1.at[1], 2)
        self.down = self.copies.start(
            self.pair.at[self.slot(3)], self.piece1.at[1], moved(self.at, self.first, 3)
        )
        self.pair_sum(2)

    def second_send(self):
        self.up.wait()
        self.down.wait()
        mine = self.pair.at[self.slot(0)]

        @pl.loop(0, 4)
        def _(i):
            total = (
                mine[i].astype(F32)
                + self.piece1[0, i].astype(F32)
                + self.piece1[1, i].astype(F32)
            )
            mine[i] = total.astype(BF16)

        self.sent = [
            self.copies.start(
                mine.at[lax.rem(self.at[self.second] + step, 4)],
                self.piece2.at[step - 1],
                moved(self.at, self.second, step),
            )
            for step in (1, 2, 3)
        ]

    def finish(self):
        total = self.pair[self.slot(0), self.at[self.second]].astype(F32)
        for copy in self.sent:
            copy.wait()
        for i in range(3):
            total = total + self.piece2[i].astype(F32)
        return total


def part_scratch(rows, columns):
    return [
        pltpu.VMEM((2, 4, 4, rows, columns), BF16),
        pltpu.VMEM((4, 4, rows, columns), BF16),
        pltpu.VMEM((2, 2, rows, columns), BF16),
        pltpu.VMEM((2, 4, rows, columns), BF16),
        pltpu.VMEM((3, rows, columns), BF16),
    ]


def line_send(at, copies, lines, line_in):
    return [
        copies.start(
            lines.at[lax.rem(at["x"] + step, 4)], line_in.at[step - 1], moved(at, "x", step)
        )
        for step in (1, 2, 3)
    ]


def line_finish(at, started, lines, line_in):
    total = lines[at["x"]].astype(F32)
    for copy in started:
        copy.wait()
    for i in range(3):
        total = total + line_in[i].astype(F32)
    return total


def line_scratch(rows):
    return [pltpu.VMEM((4, rows, D), BF16), pltpu.VMEM((3, rows, D), BF16)]


def share_all(at, copies, axis, held, slots):
    size = 2 if axis == "c" else 4
    slots[at[axis]] = held[...]
    return [
        copies.start(held, slots.at[at[axis]], moved(at, axis, step)) for step in range(1, size)
    ]


def sum_shared(started, held, slots):
    for copy in started:
        copy.wait()
    total = slots[0]
    for i in range(1, slots.shape[0]):
        total = total + slots[i]
    held[...] = total


def shift_in_start(copies, source, rows_in, edge, edge_in):
    started = [copies.start(source.at[4:8], rows_in, neighbour(1, 0))]
    for half in range(2):
        ends = [source[4 * half + r, 32:48].astype(F32)[12:16] for r in range(4)]
        edge[half] = jnp.concatenate(ends, axis=0).astype(BF16)
    started.append(copies.start(edge.at[0], edge_in.at[0], neighbour(0, 1)))
    started.append(copies.start(edge.at[1], edge_in.at[1], neighbour(1, 1)))
    return started


def shift_in_finish(started, source, rows_in, edge_in, grid):
    for copy in started:
        copy.wait()
    for row in range(8):
        held = (rows_in[row] if row < 4 else source[row - 4]).astype(F32)
        turned = pltpu.roll(held, 4, 0)
        ends = edge_in[1 if row < 4 else 0].astype(F32)[4 * (row % 4) : 4 * (row % 4) + 4]
        grid[row] = jnp.concatenate(
            [jnp.concatenate([ends, turned[4:8]], axis=0), turned[8:48]], axis=0
        )


def shift_back_start(copies, grid, rows_out, rows_in, edge, edge_in):
    for row in range(4):
        rows_out[row] = pltpu.roll(grid[row], 44, 0).astype(BF16)
    started = [copies.start(rows_out, rows_in, neighbour(-1, 0))]
    for half in range(2):
        firsts = [grid[4 * half + r, 0:8][0:4] for r in range(4)]
        edge[half] = jnp.concatenate(firsts, axis=0).astype(BF16)
    started.append(copies.start(edge.at[1], edge_in.at[1], neighbour(0, -1)))
    started.append(copies.start(edge.at[0], edge_in.at[0], neighbour(-1, -1)))
    return started


def shift_back_finish(started, grid, rows_in, edge_in, result):
    for copy in started:
        copy.wait()
    for row in range(8):
        if row < 4:
            turned = pltpu.roll(grid[row + 4], 44, 0)
        else:
            turned = rows_in[row - 4].astype(F32)
        ends = edge_in[1 if row < 4 else 0].astype(F32)[4 * (row % 4) : 4 * (row % 4) + 4]
        whole = jnp.concatenate(
            [turned[0:40], jnp.concatenate([turned[40:44], ends], axis=0)], axis=0
        )
        result[row] = whole.astype(result.dtype)


SHIFT_SCRATCH = [
    pltpu.VMEM((4, 48, D), BF16),
    pltpu.VMEM((2, 16, D), BF16),
    pltpu.VMEM((2, 16, D), BF16),
]


TOKENS = 384
WINDOWS = 6
PAIRS = 4
TILE = 16


def mm(a, b):
    return lax.dot_general(a, b, (((1,), (0,)), ((), ())), preferred_element_type=F32)


def mm_nt(a, b):
    return lax.dot_general(a, b, (((1,), (1,)), ((), ())), preferred_element_type=F32)


def mm_tn(a, b):
    return lax.dot_general(a, b, (((0,), (0,)), ((), ())), preferred_element_type=F32)


def split_low(value):
    high = value.astype(BF16)
    return high, (value - high.astype(F32)).astype(BF16)


def iota(shape, dim):
    return lax.broadcasted_iota(jnp.int32, shape, dim)


def tiles(body):
    @pl.loop(0, TOKENS // TILE, unroll=8)
    def _(i):
        body(i, pl.ds(pl.multiple_of(i * TILE, TILE), TILE))


def grid_tile(grid, i):
    window, row = i // 4, lax.rem(i, 4) * 2
    columns = pl.ds(pl.multiple_of(window * 8, 8), 8)
    return jnp.concatenate([grid[row, columns], grid[row + 1, columns]], axis=0)


def store_grid_tile(grid, i, tile):
    window, row = i // 4, lax.rem(i, 4) * 2
    columns = pl.ds(pl.multiple_of(window * 8, 8), 8)
    grid[row, columns] = tile[0:8]
    grid[row + 1, columns] = tile[8:16]


def normalise(vectors):
    centred = vectors - jnp.mean(vectors, axis=-1, keepdims=True)
    factor = lax.rsqrt(jnp.mean(centred * centred, axis=-1, keepdims=True) + NORM_EPSILON)
    return centred * factor, factor


def normalise_back(grad_out, normal, factor, gain):
    grad_hat = grad_out * gain
    inner = (
        grad_hat
        - jnp.mean(grad_hat, axis=-1, keepdims=True)
        - normal * jnp.mean(grad_hat * normal, axis=-1, keepdims=True)
    )
    return factor * inner


def line_order(first_z):
    place_of = iota((1, D), 1)
    core, first, second = place_of >> 8, (place_of >> 6) & 3, (place_of >> 4) & 3
    x, r = (place_of >> 2) & 3, place_of & 3
    y, z = (second, first) if first_z else (first, second)
    feature = (y << 7) | ((z & 1) << 6) | ((z >> 1) << 5) | (x << 3) | (core << 2) | r
    return jnp.where(iota((D, D), 0) == feature, 1.0, 0.0).astype(BF16)


def pair_offsets():
    row, column = iota((256, 128), 0), iota((256, 128), 1)
    target = ((column >> 6) << 7) + 15 * ((column >> 3) & 7) + (column & 7)
    return jnp.where(row == target, 1.0, 0.0).astype(BF16)


def store_wide(halves, i, rows):
    halves[0, 8 * i : 8 * i + 8] = rows[:, 0:128]
    halves[1, 8 * i : 8 * i + 8] = rows[:, 128:256]


def load_strided(halves, first):
    return jnp.concatenate([halves[k, pl.ds(first, 8, stride=8), :] for k in range(2)], axis=1)


def expand_bias(rel, table, shifted, bias, masked):
    table[...] = jnp.zeros_like(table)
    table[:, 0:225] = rel[...]
    whole = table[...]
    for b in range(8):
        store_wide(shifted, b, pltpu.roll(whole, (256 - (7 - b)) % 256, 1))
    spread = pair_offsets()
    key, query = iota((64, 128), 0), iota((64, 128), 1) & 63
    apart = jnp.where((key >> 5) == (query >> 5), 0.0, -1e30)
    apart = jnp.where(masked, apart, 0.0)
    for p in range(PAIRS):
        heads = []
        for h in (2 * p, 2 * p + 1):
            rows = load_strided(shifted, h)
            turned = [pltpu.roll(rows, 256 - (105 - 15 * a), 1)[:, 0:128] for a in range(8)]
            heads.append(jnp.concatenate(turned, axis=0))
        high, low = split_low(jnp.concatenate(heads, axis=1))
        bias[p] = mm(high, spread) + mm(low, spread) + apart


def collect_table(grad_bias, collected, total):
    spread = pair_offsets()
    for p in range(PAIRS):
        high, low = split_low(grad_bias[p])
        both = mm_nt(high, spread) + mm_nt(low, spread)
        for k in range(2):
            one = both[:, 128 * k : 128 * k + 128]
            one = jnp.concatenate([one, jnp.zeros_like(one)], axis=1)
            rows = one[56:64]
            for a in range(7):
                rows = rows + pltpu.roll(one[8 * a : 8 * a + 8], 105 - 15 * a, 1)
            h = 2 * p + k
            store_wide(collected, h, rows)
    table = load_strided(collected, 7)
    for b in range(7):
        table = table + pltpu.roll(load_strided(collected, b), 7 - b, 1)
    total[...] = table


def both_heads(pair):
    left = iota(pair.shape, 1) < 64
    zero = jnp.zeros_like(pair)
    return jnp.concatenate([jnp.where(left, pair, zero), jnp.where(left, zero, pair)], axis=0)


def own_heads(crossed):
    return jnp.where(iota((64, 128), 1) < 64, crossed[0:64], crossed[64:128])


def window_rows(w):
    return pl.ds(pl.multiple_of(w * 64, 64), 64)


def attend(w, qkv, bias, probs, attended):
    rows = window_rows(w)
    for p in range(PAIRS):
        query = qkv[rows, 128 * p : 128 * p + 128]
        keys = qkv[rows, D + 128 * p : D + 128 * p + 128]
        values = qkv[rows, 2 * D + 128 * p : 2 * D + 128 * p + 128]
        scores = mm_nt(keys, both_heads(query)) + bias[p]
        powers = jnp.exp(scores - jnp.max(scores, axis=0, keepdims=True))
        each = powers / jnp.sum(powers, axis=0, keepdims=True)
        probs[w, p] = each
        crossed = mm_tn(each.astype(BF16), values)
        attended[rows, 128 * p : 128 * p + 128] = own_heads(crossed).astype(BF16)


def attend_back(w, qkv, probs, grad_attended, grad_bias, grad_rows):
    rows = window_rows(w)
    for p in range(PAIRS):
        query = both_heads(qkv[rows, 128 * p : 128 * p + 128])
        keys = qkv[rows, D + 128 * p : D + 128 * p + 128]
        values = qkv[rows, 2 * D + 128 * p : 2 * D + 128 * p + 128]
        grads = both_heads(grad_attended[rows, 128 * p : 128 * p + 128])
        each = probs[w, p]
        grad_probs = mm_nt(values, grads)
        grad_scores = each * (grad_probs - jnp.sum(each * grad_probs, axis=0, keepdims=True))
        grad_bias[p] += grad_scores
        low = grad_scores.astype(BF16)
        grad_query = own_heads(mm_tn(low, keys)) * 0.125
        grad_rows[rows, 128 * p : 128 * p + 128] = grad_query.astype(BF16)
        grad_rows[rows, D + 128 * p : D + 128 * p + 128] = mm(low, query).astype(BF16)
        grad_rows[rows, 2 * D + 128 * p : 2 * D + 128 * p + 128] = mm(
            each.astype(BF16), grads
        ).astype(BF16)


GELU_SCALE = 0.7978845608028654
GELU_CUBE = 0.044715


def gelu_both(hidden):
    square = hidden * hidden
    swing = jnp.tanh(GELU_SCALE * hidden * (1.0 + GELU_CUBE * square))
    half = 0.5 + 0.5 * swing
    slope = half + (0.5 * GELU_SCALE) * hidden * (1.0 - swing * swing) * (
        1.0 + 3.0 * GELU_CUBE * square
    )
    return hidden * half, slope


def eight(tile):
    return tile[0:8] + tile[8:16]


COMPUTE_SCRATCH = [
    ("hat1", (TOKENS, D), F32),
    ("factor1", (TOKENS, 128), F32),
    ("norm1", (TOKENS, D), BF16),
    ("qkv", (TOKENS, 3 * D), BF16),
    ("attended", (TOKENS, D), BF16),
    ("resid", (TOKENS, D), F32),
    ("hat2", (TOKENS, D), F32),
    ("factor2", (TOKENS, 128), F32),
    ("norm2", (TOKENS, D), BF16),
    ("norm2_z", (TOKENS, D), BF16),
    ("cot", (TOKENS, D), BF16),
    ("hidden", (TOKENS, D), F32),
    ("grad_active", (TOKENS, D), F32),
    ("active", (TOKENS, D), BF16),
    ("grad_hidden", (TOKENS, D), BF16),
    ("mlp_out", (TOKENS, D), F32),
    ("grad_norm", (TOKENS, D), F32),
    ("grad_resid", (TOKENS, D), F32),
    ("grad_resid_low", (TOKENS, D), BF16),
    ("grad_attended", (TOKENS, D), BF16),
    ("grad_rows", (TOKENS, 3 * D), BF16),
    ("probs", (WINDOWS, PAIRS, 64, 128), F32),
    ("bias", (PAIRS, 64, 128), F32),
    ("grad_bias", (PAIRS, 64, 128), F32),
    ("table", (8, 256), F32),
    ("shifted", (2, 64, 128), F32),
    ("gain_sums", (2, 8, D), F32),
]


class Block:
    def __init__(self, refs):
        for (name, _, _), ref in zip(COMPUTE_SCRATCH, refs):
            setattr(self, name, ref)


def attention_forward(s, x_grid, gain_attn, w_qkv):
    def first_norm(i, rows):
        normal, factor = normalise(grid_tile(x_grid, i))
        s.hat1[rows] = normal
        s.factor1[rows] = jnp.broadcast_to(factor, (TILE, 128))
        s.norm1[rows] = (normal * gain_attn[...]).astype(BF16)

    tiles(first_norm)
    for i in range(3):
        columns = slice(D * i, D * i + D)
        part = mm(s.norm1[...], w_qkv[:, columns])
        s.qkv[:, columns] = (part * 0.125 if i == 0 else part).astype(BF16)

    @pl.loop(0, WINDOWS, unroll=3)
    def _(w):
        attend(w, s.qkv, s.bias, s.probs, s.attended)


def before_mlp(s, x_grid, c_grid, gain_mlp):
    def second_norm(i, rows):
        resid = s.resid[rows] + grid_tile(x_grid, i)
        normal, factor = normalise(resid)
        s.resid[rows] = resid
        s.hat2[rows] = normal
        s.factor2[rows] = jnp.broadcast_to(factor, (TILE, 128))
        s.norm2[rows] = (normal * gain_mlp[...]).astype(BF16)
        s.cot[rows] = grid_tile(c_grid, i).astype(BF16)

    tiles(second_norm)
    s.norm2_z[...] = mm(s.norm2[...], line_order(True)).astype(BF16)
    s.mlp_out[...] = jnp.zeros_like(s.mlp_out)
    s.grad_norm[...] = jnp.zeros_like(s.grad_norm)


def mlp_step(s, j, w_fc1, w_fc2, own_fc2, own_fc1):
    columns = pl.ds(pl.multiple_of(j * D, D), D)
    s.hidden[...] = mm(s.norm2[...], w_fc1[:, columns])
    s.grad_active[...] = mm_nt(s.cot[...], w_fc2[columns])

    def bend(_, rows):
        active, slope = gelu_both(s.hidden[rows])
        s.active[rows] = active.astype(BF16)
        s.grad_hidden[rows] = (slope * s.grad_active[rows]).astype(BF16)

    tiles(bend)
    grad_fc2 = mm_tn(s.active[...], s.cot[...]).astype(BF16).reshape(2, 2, 4, 2, 16, D)
    for low in range(2):
        for high in range(2):
            for x in range(4):
                for c in range(2):
                    own_fc2[c, j, 2 * high + low, 16 * x : 16 * x + 16, :] = grad_fc2[
                        low, high, x, c
                    ]
    grad_fc1 = mm_tn(s.norm2_z[...], s.grad_hidden[...]).astype(BF16)
    own_fc1[:, :, :, pl.ds(pl.multiple_of(j * 16, 16), 16), :] = grad_fc1.reshape(2, 4, 4, 16, D)
    s.mlp_out[...] += mm(s.active[...], w_fc2[columns])
    s.grad_norm[...] += mm_nt(s.grad_hidden[...], w_fc1[:, columns])


def after_mlp(s, gain_mlp, out_grid):
    s.gain_sums[...] = jnp.zeros_like(s.gain_sums)

    def second_back(i, rows):
        grad, normal = s.grad_norm[rows], s.hat2[rows]
        s.gain_sums[1] += eight(grad * normal)
        grad_resid = s.cot[rows].astype(F32) + normalise_back(
            grad, normal, s.factor2[rows][:, 0:1], gain_mlp[...]
        )
        s.grad_resid[rows] = grad_resid
        s.grad_resid_low[rows] = grad_resid.astype(BF16)
        store_grid_tile(out_grid, i, s.resid[rows] + s.mlp_out[rows])

    tiles(second_back)


def attention_after(s, gain_attn, grad_grid, small):
    def first_back(i, rows):
        grad, normal = s.grad_norm[rows], s.hat1[rows]
        s.gain_sums[0] += eight(grad * normal)
        back = normalise_back(grad, normal, s.factor1[rows][:, 0:1], gain_attn[...])
        store_grid_tile(grad_grid, i, s.grad_resid[rows] + back)

    tiles(first_back)
    collect_table(s.grad_bias, s.shifted, s.table)
    small[...] = jnp.zeros_like(small)
    small[0, 0:1] = jnp.sum(s.gain_sums[0], axis=0, keepdims=True)
    small[0, 1:2] = jnp.sum(s.gain_sums[1], axis=0, keepdims=True)
    small[1, :, 0:256] = s.table[...]


def whole_kernel(
    tokens, cotangent, gain_attn, rel, gain_mlp, w_qkv_hbm, w_proj_hbm, w_fc1_hbm, w_fc2_hbm,
    output, grad_tokens, qkv_total, fc1_total, fc2_total, small_total, *scratch
):
    refs = list(scratch)

    def take(count):
        taken = refs[:count]
        del refs[:count]
        return taken

    s = Block(take(len(COMPUTE_SCRATCH)))
    weights, weight_sem = take(4), take(1)[0]
    w_qkv, w_proj, w_fc1, w_fc2 = weights
    x_grid, c_grid, out_grid, grad_grid, small = take(5)
    send_sems, recv_sems = take(2)
    at = place()
    copies = Copies(send_sems, recv_sems)
    fc2 = Part(at, copies, ("y", "z"), *take(5))
    fc1 = Part(at, copies, ("z", "y"), *take(5))
    qkv_y = Part(at, copies, ("y", "z"), *take(5))
    qkv_z = Part(at, copies, ("z", "y"), *take(5))
    fc2_lines, fc1_lines, qkv_lines = take(2), take(2), take(2)
    held, pair_slots, slots = take(3)
    in_tokens, in_cot = take(3), take(3)
    back_out, back_tokens = take(4), take(4)

    loads = []
    for i, source in enumerate((w_qkv_hbm, w_proj_hbm, w_fc1_hbm, w_fc2_hbm)):
        loads.append(pltpu.make_async_copy(source, weights[i], weight_sem.at[i]))
        loads[-1].start()
    greet(at)
    came_tokens = shift_in_start(copies, tokens, *in_tokens)
    came_cot = shift_in_start(copies, cotangent, *in_cot)
    expand_bias(rel, s.table, s.shifted, s.bias, lax.axis_index("lat") == 0)
    shift_in_finish(came_tokens, tokens, in_tokens[0], in_tokens[2], x_grid)
    loads[0].wait()
    attention_forward(s, x_grid, gain_attn, w_qkv)
    for load in loads[1:]:
        load.wait()
    s.resid[...] = mm(s.attended[...], w_proj[...])
    shift_in_finish(came_cot, cotangent, in_cot[0], in_cot[2], c_grid)
    before_mlp(s, x_grid, c_grid, gain_mlp)

    @pl.loop(0, 4)
    def _(i):
        mlp_step(s, fc2.slot(6 - i), w_fc1, w_fc2, fc2.own, fc1.own)
        fc2.pair_copy(i).start()

    after_mlp(s, gain_mlp, out_grid)
    went_out = shift_back_start(copies, out_grid, *back_out)
    by_z = line_order(True)
    s.norm2_z[...] = mm(s.attended[...], by_z).astype(BF16)
    grad_proj = mm_tn(s.norm2_z[...], s.grad_resid_low[...]).astype(BF16)
    fc1.own[:, :, :, 64:80, :] = grad_proj.reshape(2, 4, 4, 16, D)
    fc1.begin()
    fc2.first_halves()
    s.grad_attended[...] = mm_nt(s.grad_resid_low[...], w_proj[...]).astype(BF16)
    s.grad_bias[...] = jnp.zeros_like(s.grad_bias)

    def windows_back(first, last):
        @pl.loop(first, last, unroll=2)
        def _(w):
            attend_back(w, s.qkv, s.probs, s.grad_attended, s.grad_bias, s.grad_rows)

    windows_back(0, 2)
    fc2.first_pieces()
    fc1.first_halves()
    windows_back(2, 4)
    fc1.first_pieces()
    windows_back(4, 6)
    s.norm2_z[...] = mm(s.norm1[...], by_z).astype(BF16)
    s.norm2[...] = mm(s.norm1[...], line_order(False)).astype(BF16)
    for i in range(3):
        for left, turned, part in ((0, s.norm2, qkv_y), (256, s.norm2_z, qkv_z)):
            columns = slice(D * i + left, D * i + left + 256)
            grad = mm_tn(turned[...], s.grad_rows[:, columns]).astype(BF16)
            part.own[:, :, :, 16 * i : 16 * i + 16, :] = grad.reshape(2, 4, 4, 16, 256)
    qkv_y.begin()
    qkv_z.begin()
    fc2.second_send()
    s.grad_norm[...] = mm_nt(s.grad_rows[...], w_qkv[...])
    qkv_y.first_halves()
    qkv_z.first_halves()
    fc1.second_send()
    attention_after(s, gain_attn, grad_grid, small)
    went_tokens = shift_back_start(copies, grad_grid, *back_tokens)
    held[0] = small[...]
    shared = share_all(at, copies, "c", held.at[0], pair_slots)
    qkv_y.first_pieces()
    qkv_z.first_pieces()
    sum_shared(shared, held.at[1], pair_slots)
    shared = share_all(at, copies, "y", held.at[1], slots.at[0])
    fc2_lines[0][...] = fc2.finish().astype(BF16).reshape(4, 16, D)
    fc2_sent = line_send(at, copies, *fc2_lines)
    total = fc1.finish()
    for x in range(4):
        rows = [total[16 * i + 4 * x : 16 * i + 4 * x + 4] for i in range(5)]
        fc1_lines[0][x] = jnp.concatenate(rows + [jnp.zeros((12, D), F32)], axis=0).astype(BF16)
    fc1_sent = line_send(at, copies, *fc1_lines)
    qkv_y.second_send()
    qkv_z.second_send()
    sum_shared(shared, held.at[2], slots.at[0])
    shared = share_all(at, copies, "z", held.at[2], slots.at[1])
    shift_back_finish(went_out, out_grid, back_out[1], back_out[3], output)
    total = jnp.concatenate([qkv_y.finish(), qkv_z.finish()], axis=1)
    for x in range(4):
        rows = [total[16 * i + 4 * x : 16 * i + 4 * x + 4] for i in range(3)]
        qkv_lines[0][x] = jnp.concatenate(rows + [jnp.zeros((4, D), F32)], axis=0).astype(BF16)
    qkv_sent = line_send(at, copies, *qkv_lines)
    sum_shared(shared, held.at[3], slots.at[1])
    shared = share_all(at, copies, "x", held.at[3], slots.at[2])
    shift_back_finish(went_tokens, grad_grid, back_tokens[1], back_tokens[3], grad_tokens)
    fc2_total[...] = line_finish(at, fc2_sent, *fc2_lines)
    fc1_total[...] = line_finish(at, fc1_sent, *fc1_lines)
    qkv_total[...] = line_finish(at, qkv_sent, *qkv_lines)
    sum_shared(shared, small_total, slots.at[2])


def whole(tokens, cotangent, gain_attn, w_qkv, w_proj, rel, gain_mlp, w_fc1, w_fc2):
    vmem = pl.BlockSpec(memory_space=pltpu.VMEM)
    copies = 100
    return pl.pallas_call(
        whole_kernel,
        out_shape=(
            jax.ShapeDtypeStruct((8, 48, D), BF16),
            jax.ShapeDtypeStruct((8, 48, D), F32),
            jax.ShapeDtypeStruct((16, D), F32),
            jax.ShapeDtypeStruct((32, D), F32),
            jax.ShapeDtypeStruct((16, D), F32),
            jax.ShapeDtypeStruct((2, 8, D), F32),
        ),
        in_specs=[vmem] * 5 + [pl.BlockSpec(memory_space=pl.ANY)] * 4,
        out_specs=[vmem] * 6,
        scratch_shapes=[pltpu.VMEM(shape, kind) for _, shape, kind in COMPUTE_SCRATCH]
        + [pltpu.VMEM(w.shape, BF16) for w in (w_qkv, w_proj, w_fc1, w_fc2)]
        + [pltpu.SemaphoreType.DMA((4,))]
        + [pltpu.VMEM((8, 48, D), F32)] * 4
        + [pltpu.VMEM((2, 8, D), F32)]
        + [pltpu.SemaphoreType.DMA((copies,))] * 2
        + part_scratch(64, D)
        + part_scratch(80, D)
        + part_scratch(48, 256) * 2
        + line_scratch(16)
        + line_scratch(32)
        + line_scratch(16)
        + [
            pltpu.VMEM((4, 2, 8, D), F32),
            pltpu.VMEM((2, 2, 8, D), F32),
            pltpu.VMEM((3, 4, 2, 8, D), F32),
        ]
        + SHIFT_SCRATCH * 2
        + ([pltpu.VMEM((4, 48, D), BF16)] + SHIFT_SCRATCH) * 2,
        compiler_params=pltpu.CompilerParams(
            collective_id=0, has_side_effects=True, vmem_limit_bytes=56 * 2**20
        ),
        name="whole_block",
    )(tokens, cotangent, gain_attn.reshape(1, D), rel, gain_mlp.reshape(1, D), w_qkv, w_proj, w_fc1, w_fc2)


def deliver_kernel(
    output, grad_tokens, qkv_total, fc1_total, fc2_total, small,
    output_to, grad_tokens_to, grad_qkv, grad_proj, table, grad_fc1, grad_fc2, gain_attn, gain_mlp,
    sems
):
    first = pltpu.make_async_copy(grad_tokens, grad_tokens_to, sems.at[0])
    second = pltpu.make_async_copy(output, output_to, sems.at[1])
    first.start()
    second.start()
    for i in range(3):
        grad_qkv[:, D * i : D * i + D] = qkv_total[4 * i : 4 * i + 4]
    for i in range(4):
        grad_fc1[:, D * i : D * i + D] = fc1_total[4 * i : 4 * i + 4]
    grad_proj[...] = fc1_total[16:20]
    grad_fc2[...] = fc2_total[...]
    table[...] = small[1][:, 0:225]
    gain_attn[...] = small[0, 0]
    gain_mlp[...] = small[0, 1]
    first.wait()
    second.wait()


def deliver(*results):
    vmem, anywhere = pl.BlockSpec(memory_space=pltpu.VMEM), pl.BlockSpec(memory_space=pl.ANY)
    return pl.pallas_call(
        deliver_kernel,
        out_shape=(
            jax.ShapeDtypeStruct((8, 48, D), BF16),
            jax.ShapeDtypeStruct((8, 48, D), F32),
            jax.ShapeDtypeStruct((4, 3 * D), F32),
            jax.ShapeDtypeStruct((4, D), F32),
            jax.ShapeDtypeStruct((8, 225), F32),
            jax.ShapeDtypeStruct((4, 4 * D), F32),
            jax.ShapeDtypeStruct((16, D), F32),
            jax.ShapeDtypeStruct((D,), F32),
            jax.ShapeDtypeStruct((D,), F32),
        ),
        in_specs=[anywhere] * 2 + [vmem] * 4,
        out_specs=[anywhere] * 2 + [vmem] * 7,
        scratch_shapes=[pltpu.SemaphoreType.DMA((2,))],
        name="deliver",
    )(*results)


def shards(tokens, cotangent, gain_attn, w_qkv, w_proj, rel_table, gain_mlp, w_fc1, w_fc2):
    return deliver(
        *whole(tokens, cotangent, gain_attn, w_qkv, w_proj, rel_table, gain_mlp, w_fc1, w_fc2)
    )


def solution(mesh):
    placed = (P("lat", "lon", None), P("lat", "lon", None), P(), P(), P(), P(), P(), P(), P())
    return jax.shard_map(
        shards,
        mesh=mesh,
        in_specs=placed,
        out_specs=(
            P("lat", "lon", None),
            P("lat", "lon", None),
            P(("lat", "lon"), None),
            P(("lat", "lon"), None),
            P(),
            P(("lat", "lon"), None),
            P(("lat", "lon"), None),
            P(),
            P(),
        ),
        check_vma=False,
    )
```

```python
import jax
import jax.numpy as jnp
from jax import lax
from jax.experimental import pallas as pl
from jax.experimental.pallas import tpu as pltpu
from jax.sharding import PartitionSpec as P

NORM_EPSILON = 1e-05
D = 512


MESH = pl.DeviceIdType.MESH
F32 = jnp.float32
BF16 = jnp.bfloat16


def place():
    lat = lax.axis_index("lat")
    lon = lax.axis_index("lon")
    return {
        "c": lax.rem(lon, 2),
        "x": lax.rem(lon // 2, 4),
        "y": lat // 2,
        "z": (lon // 8) * 2 + lax.rem(lat, 2),
    }


def moved(at, axis, step):
    size = 2 if axis == "c" else 4
    there = dict(at)
    there[axis] = lax.rem(at[axis] + step, size)
    lat = there["y"] * 2 + lax.rem(there["z"], 2)
    lon = (there["z"] // 2) * 8 + there["x"] * 2 + there["c"]
    return (lat, lon)


def neighbour(step_lat, step_lon):
    return (
        lax.rem(lax.axis_index("lat") + step_lat + 8, 8),
        lax.rem(lax.axis_index("lon") + step_lon + 16, 16),
    )


def greet(at):
    barrier = pltpu.get_barrier_semaphore()
    others = [moved(at, "c", 1)]
    others += [moved(at, axis, step) for axis in ("y", "z", "x") for step in (1, 2, 3)]
    steps = ((1, 0), (0, 1), (1, 1), (-1, 0), (0, -1), (-1, -1))
    others += [neighbour(*step) for step in steps]
    for other in others:
        pl.semaphore_signal(barrier, inc=1, device_id=other, device_id_type=MESH)
    pl.semaphore_wait(barrier, len(others))


class Copies:
    def __init__(self, send_sems, recv_sems):
        self.send_sems, self.recv_sems, self.used = send_sems, recv_sems, 0

    def reserve(self, count):
        self.used += count
        return self.used - count

    def make(self, index, src, dst, device):
        return pltpu.make_async_remote_copy(
            src_ref=src,
            dst_ref=dst,
            send_sem=self.send_sems.at[index],
            recv_sem=self.recv_sems.at[index],
            device_id=device,
            device_id_type=MESH,
        )

    def start(self, src, dst, device):
        copy = self.make(self.reserve(1), src, dst, device)
        copy.start()
        return copy


def add_into(target, other, count):
    @pl.loop(0, count)
    def _(i):
        target[i] = target[i] + other[i]


class Part:
    def __init__(self, at, copies, axes, own, pair, half1, piece1, piece2):
        self.at, self.copies = at, copies
        self.first, self.second = axes
        self.own, self.pair = own, pair
        self.half1, self.piece1, self.piece2 = half1, piece1, piece2
        self.base = copies.reserve(4)

    def slot(self, step):
        return lax.rem(self.at[self.first] + step, 4)

    def pair_copy(self, i):
        j = self.slot(6 - i)
        return self.copies.make(
            self.base + i, self.own.at[1 - self.at["c"], j], self.pair.at[j], moved(self.at, "c", 1)
        )

    def begin(self):
        for i in range(4):
            self.pair_copy(i).start()

    def pair_sum(self, i):
        self.pair_copy(i).wait()
        j = self.slot(6 - i)
        add_into(self.pair.at[j], self.own.at[self.at["c"], j], 4)

    def first_halves(self):
        self.pair_sum(0)
        j = self.slot(2)
        self.up = self.copies.start(
            self.pair.at[j, 0:2], self.half1.at[0], moved(self.at, self.first, 1)
        )
        self.down = self.copies.start(
            self.pair.at[j, 2:4], self.half1.at[1], moved(self.at, self.first, 3)
        )
        self.pair_sum(1)
        self.pair_sum(3)

    def first_pieces(self):
        self.up.wait()
        add_into(self.pair.at[self.slot(1), 0:2], self.half1.at[0], 2)
        self.up = self.copies.start(
            self.pair.at[self.slot(1)], self.piece1.at[0], moved(self.at, self.first, 1)
        )
        self.down.wait()
        add_into(self.pair.at[self.slot(3), 2:4], self.half1.at[1], 2)
        self.down = self.copies.start(
            self.pair.at[self.slot(3)], self.piece1.at[1], moved(self.at, self.first, 3)
        )
        self.pair_sum(2)

    def second_send(self):
        self.up.wait()
        self.down.wait()
        mine = self.pair.at[self.slot(0)]

        @pl.loop(0, 4)
        def _(i):
            total = (
                mine[i].astype(F32)
                + self.piece1[0, i].astype(F32)
                + self.piece1[1, i].astype(F32)
            )
            mine[i] = total.astype(BF16)

        self.sent = [
            self.copies.start(
                mine.at[lax.rem(self.at[self.second] + step, 4)],
                self.piece2.at[step - 1],
                moved(self.at, self.second, step),
            )
            for step in (1, 2, 3)
        ]

    def finish(self):
        total = self.pair[self.slot(0), self.at[self.second]].astype(F32)
        for copy in self.sent:
            copy.wait()
        for i in range(3):
            total = total + self.piece2[i].astype(F32)
        return total


def part_scratch(rows, columns):
    return [
        pltpu.VMEM((2, 4, 4, rows, columns), BF16),
        pltpu.VMEM((4, 4, rows, columns), BF16),
        pltpu.VMEM((2, 2, rows, columns), BF16),
        pltpu.VMEM((2, 4, rows, columns), BF16),
        pltpu.VMEM((3, rows, columns), BF16),
    ]


def line_send(at, copies, lines, line_in):
    return [
        copies.start(
            lines.at[lax.rem(at["x"] + step, 4)], line_in.at[step - 1], moved(at, "x", step)
        )
        for step in (1, 2, 3)
    ]


def line_finish(at, started, lines, line_in):
    total = lines[at["x"]].astype(F32)
    for copy in started:
        copy.wait()
    for i in range(3):
        total = total + line_in[i].astype(F32)
    return total


def line_scratch(rows):
    return [pltpu.VMEM((4, rows, D), BF16), pltpu.VMEM((3, rows, D), BF16)]


def share_all(at, copies, axis, held, slots):
    size = 2 if axis == "c" else 4
    slots[at[axis]] = held[...]
    return [
        copies.start(held, slots.at[at[axis]], moved(at, axis, step)) for step in range(1, size)
    ]


def sum_shared(started, held, slots):
    for copy in started:
        copy.wait()
    total = slots[0]
    for i in range(1, slots.shape[0]):
        total = total + slots[i]
    held[...] = total


def shift_in_start(copies, source, rows_in, edge, edge_in):
    started = [copies.start(source.at[4:8], rows_in, neighbour(1, 0))]
    for half in range(2):
        ends = [source[4 * half + r, 32:48].astype(F32)[12:16] for r in range(4)]
        edge[half] = jnp.concatenate(ends, axis=0).astype(BF16)
    started.append(copies.start(edge.at[0], edge_in.at[0], neighbour(0, 1)))
    started.append(copies.start(edge.at[1], edge_in.at[1], neighbour(1, 1)))
    return started


def shift_in_finish(started, source, rows_in, edge_in, grid):
    for copy in started:
        copy.wait()
    for row in range(8):
        held = (rows_in[row] if row < 4 else source[row - 4]).astype(F32)
        turned = pltpu.roll(held, 4, 0)
        ends = edge_in[1 if row < 4 else 0].astype(F32)[4 * (row % 4) : 4 * (row % 4) + 4]
        grid[row] = jnp.concatenate(
            [jnp.concatenate([ends, turned[4:8]], axis=0), turned[8:48]], axis=0
        )


def shift_back_start(copies, grid, rows_out, rows_in, edge, edge_in):
    for row in range(4):
        rows_out[row] = pltpu.roll(grid[row], 44, 0).astype(BF16)
    started = [copies.start(rows_out, rows_in, neighbour(-1, 0))]
    for half in range(2):
        firsts = [grid[4 * half + r, 0:8][0:4] for r in range(4)]
        edge[half] = jnp.concatenate(firsts, axis=0).astype(BF16)
    started.append(copies.start(edge.at[1], edge_in.at[1], neighbour(0, -1)))
    started.append(copies.start(edge.at[0], edge_in.at[0], neighbour(-1, -1)))
    return started


def shift_back_finish(started, grid, rows_in, edge_in, result):
    for copy in started:
        copy.wait()
    for row in range(8):
        if row < 4:
            turned = pltpu.roll(grid[row + 4], 44, 0)
        else:
            turned = rows_in[row - 4].astype(F32)
        ends = edge_in[1 if row < 4 else 0].astype(F32)[4 * (row % 4) : 4 * (row % 4) + 4]
        whole = jnp.concatenate(
            [turned[0:40], jnp.concatenate([turned[40:44], ends], axis=0)], axis=0
        )
        result[row] = whole.astype(result.dtype)


SHIFT_SCRATCH = [
    pltpu.VMEM((4, 48, D), BF16),
    pltpu.VMEM((2, 16, D), BF16),
    pltpu.VMEM((2, 16, D), BF16),
]


TOKENS = 384
WINDOWS = 6
PAIRS = 4
TILE = 16


def mm(a, b):
    return lax.dot_general(a, b, (((1,), (0,)), ((), ())), preferred_element_type=F32)


def mm_nt(a, b):
    return lax.dot_general(a, b, (((1,), (1,)), ((), ())), preferred_element_type=F32)


def mm_tn(a, b):
    return lax.dot_general(a, b, (((0,), (0,)), ((), ())), preferred_element_type=F32)


def split_low(value):
    high = value.astype(BF16)
    return high, (value - high.astype(F32)).astype(BF16)


def iota(shape, dim):
    return lax.broadcasted_iota(jnp.int32, shape, dim)


def tiles(body):
    @pl.loop(0, TOKENS // TILE, unroll=8)
    def _(i):
        body(i, pl.ds(pl.multiple_of(i * TILE, TILE), TILE))


def grid_tile(grid, i):
    window, row = i // 4, lax.rem(i, 4) * 2
    columns = pl.ds(pl.multiple_of(window * 8, 8), 8)
    return jnp.concatenate([grid[row, columns], grid[row + 1, columns]], axis=0)


def store_grid_tile(grid, i, tile):
    window, row = i // 4, lax.rem(i, 4) * 2
    columns = pl.ds(pl.multiple_of(window * 8, 8), 8)
    grid[row, columns] = tile[0:8]
    grid[row + 1, columns] = tile[8:16]


def normalise(vectors):
    centred = vectors - jnp.mean(vectors, axis=-1, keepdims=True)
    factor = lax.rsqrt(jnp.mean(centred * centred, axis=-1, keepdims=True) + NORM_EPSILON)
    return centred * factor, factor


def normalise_back(grad_out, normal, factor, gain):
    grad_hat = grad_out * gain
    inner = (
        grad_hat
        - jnp.mean(grad_hat, axis=-1, keepdims=True)
        - normal * jnp.mean(grad_hat * normal, axis=-1, keepdims=True)
    )
    return factor * inner


def line_order(first_z):
    place_of = iota((1, D), 1)
    core, first, second = place_of >> 8, (place_of >> 6) & 3, (place_of >> 4) & 3
    x, r = (place_of >> 2) & 3, place_of & 3
    y, z = (second, first) if first_z else (first, second)
    feature = (y << 7) | ((z & 1) << 6) | ((z >> 1) << 5) | (x << 3) | (core << 2) | r
    return jnp.where(iota((D, D), 0) == feature, 1.0, 0.0).astype(BF16)


def pair_offsets():
    row, column = iota((256, 128), 0), iota((256, 128), 1)
    target = ((column >> 6) << 7) + 15 * ((column >> 3) & 7) + (column & 7)
    return jnp.where(row == target, 1.0, 0.0).astype(BF16)


def store_wide(halves, i, rows):
    halves[0, 8 * i : 8 * i + 8] = rows[:, 0:128]
    halves[1, 8 * i : 8 * i + 8] = rows[:, 128:256]


def load_strided(halves, first):
    return jnp.concatenate([halves[k, pl.ds(first, 8, stride=8), :] for k in range(2)], axis=1)


def expand_bias(rel, table, shifted, bias, masked):
    table[...] = jnp.zeros_like(table)
    table[:, 0:225] = rel[...]
    whole = table[...]
    for b in range(8):
        store_wide(shifted, b, pltpu.roll(whole, (256 - (7 - b)) % 256, 1))
    spread = pair_offsets()
    key, query = iota((64, 128), 0), iota((64, 128), 1) & 63
    apart = jnp.where((key >> 5) == (query >> 5), 0.0, -1e30)
    apart = jnp.where(masked, apart, 0.0)
    for p in range(PAIRS):
        heads = []
        for h in (2 * p, 2 * p + 1):
            rows = load_strided(shifted, h)
            turned = [pltpu.roll(rows, 256 - (105 - 15 * a), 1)[:, 0:128] for a in range(8)]
            heads.append(jnp.concatenate(turned, axis=0))
        high, low = split_low(jnp.concatenate(heads, axis=1))
        bias[p] = mm(high, spread) + mm(low, spread) + apart


def collect_table(grad_bias, collected, total):
    spread = pair_offsets()
    for p in range(PAIRS):
        high, low = split_low(grad_bias[p])
        both = mm_nt(high, spread) + mm_nt(low, spread)
        for k in range(2):
            one = both[:, 128 * k : 128 * k + 128]
            one = jnp.concatenate([one, jnp.zeros_like(one)], axis=1)
            rows = one[56:64]
            for a in range(7):
                rows = rows + pltpu.roll(one[8 * a : 8 * a + 8], 105 - 15 * a, 1)
            h = 2 * p + k
            store_wide(collected, h, rows)
    table = load_strided(collected, 7)
    for b in range(7):
        table = table + pltpu.roll(load_strided(collected, b), 7 - b, 1)
    total[...] = table


def both_heads(pair):
    left = iota(pair.shape, 1) < 64
    zero = jnp.zeros_like(pair)
    return jnp.concatenate([jnp.where(left, pair, zero), jnp.where(left, zero, pair)], axis=0)


def own_heads(crossed):
    return jnp.where(iota((64, 128), 1) < 64, crossed[0:64], crossed[64:128])


def window_rows(w):
    return pl.ds(pl.multiple_of(w * 64, 64), 64)


def attend(w, qkv, bias, probs, attended):
    rows = window_rows(w)
    for p in range(PAIRS):
        query = qkv[rows, 128 * p : 128 * p + 128]
        keys = qkv[rows, D + 128 * p : D + 128 * p + 128]
        values = qkv[rows, 2 * D + 128 * p : 2 * D + 128 * p + 128]
        scores = mm_nt(keys, both_heads(query)) + bias[p]
        powers = jnp.exp(scores - jnp.max(scores, axis=0, keepdims=True))
        each = powers / jnp.sum(powers, axis=0, keepdims=True)
        probs[w, p] = each
        crossed = mm_tn(each.astype(BF16), values)
        attended[rows, 128 * p : 128 * p + 128] = own_heads(crossed).astype(BF16)


def attend_back(w, qkv, probs, grad_attended, grad_bias, grad_rows):
    rows = window_rows(w)
    for p in range(PAIRS):
        query = both_heads(qkv[rows, 128 * p : 128 * p + 128])
        keys = qkv[rows, D + 128 * p : D + 128 * p + 128]
        values = qkv[rows, 2 * D + 128 * p : 2 * D + 128 * p + 128]
        grads = both_heads(grad_attended[rows, 128 * p : 128 * p + 128])
        each = probs[w, p]
        grad_probs = mm_nt(values, grads)
        grad_scores = each * (grad_probs - jnp.sum(each * grad_probs, axis=0, keepdims=True))
        grad_bias[p] += grad_scores
        low = grad_scores.astype(BF16)
        grad_query = own_heads(mm_tn(low, keys)) * 0.125
        grad_rows[rows, 128 * p : 128 * p + 128] = grad_query.astype(BF16)
        grad_rows[rows, D + 128 * p : D + 128 * p + 128] = mm(low, query).astype(BF16)
        grad_rows[rows, 2 * D + 128 * p : 2 * D + 128 * p + 128] = mm(
            each.astype(BF16), grads
        ).astype(BF16)


GELU_SCALE = 0.7978845608028654
GELU_CUBE = 0.044715


def gelu_both(hidden):
    square = hidden * hidden
    swing = jnp.tanh(GELU_SCALE * hidden * (1.0 + GELU_CUBE * square))
    half = 0.5 + 0.5 * swing
    slope = half + (0.5 * GELU_SCALE) * hidden * (1.0 - swing * swing) * (
        1.0 + 3.0 * GELU_CUBE * square
    )
    return hidden * half, slope


def eight(tile):
    return tile[0:8] + tile[8:16]


COMPUTE_SCRATCH = [
    ("hat1", (TOKENS, D), F32),
    ("factor1", (TOKENS, 128), F32),
    ("norm1", (TOKENS, D), BF16),
    ("qkv", (TOKENS, 3 * D), BF16),
    ("attended", (TOKENS, D), BF16),
    ("resid", (TOKENS, D), F32),
    ("hat2", (TOKENS, D), F32),
    ("factor2", (TOKENS, 128), F32),
    ("norm2", (TOKENS, D), BF16),
    ("norm2_z", (TOKENS, D), BF16),
    ("cot", (TOKENS, D), BF16),
    ("hidden", (TOKENS, D), F32),
    ("grad_active", (TOKENS, D), F32),
    ("active", (TOKENS, D), BF16),
    ("grad_hidden", (TOKENS, D), BF16),
    ("mlp_out", (TOKENS, D), F32),
    ("grad_norm", (TOKENS, D), F32),
    ("grad_resid", (TOKENS, D), F32),
    ("grad_resid_low", (TOKENS, D), BF16),
    ("grad_attended", (TOKENS, D), BF16),
    ("grad_rows", (TOKENS, 3 * D), BF16),
    ("probs", (WINDOWS, PAIRS, 64, 128), F32),
    ("bias", (PAIRS, 64, 128), F32),
    ("grad_bias", (PAIRS, 64, 128), F32),
    ("table", (8, 256), F32),
    ("shifted", (2, 64, 128), F32),
    ("gain_sums", (2, 8, D), F32),
]


class Block:
    def __init__(self, refs):
        for (name, _, _), ref in zip(COMPUTE_SCRATCH, refs):
            setattr(self, name, ref)


def attention_forward(s, x_grid, gain_attn, w_qkv):
    def first_norm(i, rows):
        normal, factor = normalise(grid_tile(x_grid, i))
        s.hat1[rows] = normal
        s.factor1[rows] = jnp.broadcast_to(factor, (TILE, 128))
        s.norm1[rows] = (normal * gain_attn[...]).astype(BF16)

    tiles(first_norm)
    for i in range(3):
        columns = slice(D * i, D * i + D)
        part = mm(s.norm1[...], w_qkv[:, columns])
        s.qkv[:, columns] = (part * 0.125 if i == 0 else part).astype(BF16)

    @pl.loop(0, WINDOWS, unroll=3)
    def _(w):
        attend(w, s.qkv, s.bias, s.probs, s.attended)


def before_mlp(s, x_grid, c_grid, gain_mlp):
    def second_norm(i, rows):
        resid = s.resid[rows] + grid_tile(x_grid, i)
        normal, factor = normalise(resid)
        s.resid[rows] = resid
        s.hat2[rows] = normal
        s.factor2[rows] = jnp.broadcast_to(factor, (TILE, 128))
        s.norm2[rows] = (normal * gain_mlp[...]).astype(BF16)
        s.cot[rows] = grid_tile(c_grid, i).astype(BF16)

    tiles(second_norm)
    s.norm2_z[...] = mm(s.norm2[...], line_order(True)).astype(BF16)
    s.mlp_out[...] = jnp.zeros_like(s.mlp_out)
    s.grad_norm[...] = jnp.zeros_like(s.grad_norm)


def mlp_step(s, j, w_fc1, w_fc2, own_fc2, own_fc1):
    columns = pl.ds(pl.multiple_of(j * D, D), D)
    s.hidden[...] = mm(s.norm2[...], w_fc1[:, columns])
    s.grad_active[...] = mm_nt(s.cot[...], w_fc2[columns])

    def bend(_, rows):
        active, slope = gelu_both(s.hidden[rows])
        s.active[rows] = active.astype(BF16)
        s.grad_hidden[rows] = (slope * s.grad_active[rows]).astype(BF16)

    tiles(bend)
    grad_fc2 = mm_tn(s.active[...], s.cot[...]).astype(BF16).reshape(2, 2, 4, 2, 16, D)
    for low in range(2):
        for high in range(2):
            for x in range(4):
                for c in range(2):
                    own_fc2[c, j, 2 * high + low, 16 * x : 16 * x + 16, :] = grad_fc2[
                        low, high, x, c
                    ]
    grad_fc1 = mm_tn(s.norm2_z[...], s.grad_hidden[...]).astype(BF16)
    own_fc1[:, :, :, pl.ds(pl.multiple_of(j * 16, 16), 16), :] = grad_fc1.reshape(2, 4, 4, 16, D)
    s.mlp_out[...] += mm(s.active[...], w_fc2[columns])
    s.grad_norm[...] += mm_nt(s.grad_hidden[...], w_fc1[:, columns])


def after_mlp(s, gain_mlp, out_grid):
    s.gain_sums[...] = jnp.zeros_like(s.gain_sums)

    def second_back(i, rows):
        grad, normal = s.grad_norm[rows], s.hat2[rows]
        s.gain_sums[1] += eight(grad * normal)
        grad_resid = s.cot[rows].astype(F32) + normalise_back(
            grad, normal, s.factor2[rows][:, 0:1], gain_mlp[...]
        )
        s.grad_resid[rows] = grad_resid
        s.grad_resid_low[rows] = grad_resid.astype(BF16)
        store_grid_tile(out_grid, i, s.resid[rows] + s.mlp_out[rows])

    tiles(second_back)


def attention_after(s, gain_attn, grad_grid, small):
    def first_back(i, rows):
        grad, normal = s.grad_norm[rows], s.hat1[rows]
        s.gain_sums[0] += eight(grad * normal)
        back = normalise_back(grad, normal, s.factor1[rows][:, 0:1], gain_attn[...])
        store_grid_tile(grad_grid, i, s.grad_resid[rows] + back)

    tiles(first_back)
    collect_table(s.grad_bias, s.shifted, s.table)
    small[...] = jnp.zeros_like(small)
    small[0, 0:1] = jnp.sum(s.gain_sums[0], axis=0, keepdims=True)
    small[0, 1:2] = jnp.sum(s.gain_sums[1], axis=0, keepdims=True)
    small[1, :, 0:256] = s.table[...]


def whole_kernel(
    tokens, cotangent, gain_attn, rel, gain_mlp, w_qkv_hbm, w_proj_hbm, w_fc1_hbm, w_fc2_hbm,
    output, grad_tokens, qkv_total, fc1_total, fc2_total, small_total, *scratch
):
    refs = list(scratch)

    def take(count):
        taken = refs[:count]
        del refs[:count]
        return taken

    s = Block(take(len(COMPUTE_SCRATCH)))
    weights, weight_sem = take(4), take(1)[0]
    w_qkv, w_proj, w_fc1, w_fc2 = weights
    x_grid, c_grid, out_grid, grad_grid, small = take(5)
    send_sems, recv_sems = take(2)
    at = place()
    copies = Copies(send_sems, recv_sems)
    fc2 = Part(at, copies, ("y", "z"), *take(5))
    fc1 = Part(at, copies, ("z", "y"), *take(5))
    qkv_y = Part(at, copies, ("y", "z"), *take(5))
    qkv_z = Part(at, copies, ("z", "y"), *take(5))
    fc2_lines, fc1_lines, qkv_lines = take(2), take(2), take(2)
    held, pair_slots, slots = take(3)
    in_tokens, in_cot = take(3), take(3)
    back_out, back_tokens = take(4), take(4)

    loads = []
    for i, source in enumerate((w_qkv_hbm, w_proj_hbm, w_fc1_hbm, w_fc2_hbm)):
        loads.append(pltpu.make_async_copy(source, weights[i], weight_sem.at[i]))
        loads[-1].start()
    greet(at)
    came_tokens = shift_in_start(copies, tokens, *in_tokens)
    expand_bias(rel, s.table, s.shifted, s.bias, lax.axis_index("lat") == 0)
    shift_in_finish(came_tokens, tokens, in_tokens[0], in_tokens[2], x_grid)
    came_cot = shift_in_start(copies, cotangent, *in_cot)
    loads[0].wait()
    attention_forward(s, x_grid, gain_attn, w_qkv)
    for load in loads[1:]:
        load.wait()
    s.resid[...] = mm(s.attended[...], w_proj[...])
    shift_in_finish(came_cot, cotangent, in_cot[0], in_cot[2], c_grid)
    before_mlp(s, x_grid, c_grid, gain_mlp)

    @pl.loop(0, 4)
    def _(i):
        mlp_step(s, fc2.slot(6 - i), w_fc1, w_fc2, fc2.own, fc1.own)
        fc2.pair_copy(i).start()

    after_mlp(s, gain_mlp, out_grid)
    went_out = shift_back_start(copies, out_grid, *back_out)
    by_z = line_order(True)
    s.norm2_z[...] = mm(s.attended[...], by_z).astype(BF16)
    grad_proj = mm_tn(s.norm2_z[...], s.grad_resid_low[...]).astype(BF16)
    fc1.own[:, :, :, 64:80, :] = grad_proj.reshape(2, 4, 4, 16, D)
    fc1.begin()
    fc2.first_halves()
    s.grad_attended[...] = mm_nt(s.grad_resid_low[...], w_proj[...]).astype(BF16)
    s.grad_bias[...] = jnp.zeros_like(s.grad_bias)

    def windows_back(first, last):
        @pl.loop(first, last, unroll=2)
        def _(w):
            attend_back(w, s.qkv, s.probs, s.grad_attended, s.grad_bias, s.grad_rows)

    windows_back(0, 2)
    fc2.first_pieces()
    fc1.first_halves()
    windows_back(2, 4)
    fc1.first_pieces()
    windows_back(4, 6)
    s.norm2_z[...] = mm(s.norm1[...], by_z).astype(BF16)
    s.norm2[...] = mm(s.norm1[...], line_order(False)).astype(BF16)
    for i in range(3):
        for left, turned, part in ((0, s.norm2, qkv_y), (256, s.norm2_z, qkv_z)):
            columns = slice(D * i + left, D * i + left + 256)
            grad = mm_tn(turned[...], s.grad_rows[:, columns]).astype(BF16)
            part.own[:, :, :, 16 * i : 16 * i + 16, :] = grad.reshape(2, 4, 4, 16, 256)
    qkv_y.begin()
    qkv_z.begin()
    fc2.second_send()
    s.grad_norm[...] = mm_nt(s.grad_rows[...], w_qkv[...])
    qkv_y.first_halves()
    qkv_z.first_halves()
    fc1.second_send()
    attention_after(s, gain_attn, grad_grid, small)
    went_tokens = shift_back_start(copies, grad_grid, *back_tokens)
    held[0] = small[...]
    shared = share_all(at, copies, "c", held.at[0], pair_slots)
    qkv_y.first_pieces()
    qkv_z.first_pieces()
    sum_shared(shared, held.at[1], pair_slots)
    shared = share_all(at, copies, "y", held.at[1], slots.at[0])
    fc2_lines[0][...] = fc2.finish().astype(BF16).reshape(4, 16, D)
    fc2_sent = line_send(at, copies, *fc2_lines)
    total = fc1.finish()
    for x in range(4):
        rows = [total[16 * i + 4 * x : 16 * i + 4 * x + 4] for i in range(5)]
        fc1_lines[0][x] = jnp.concatenate(rows + [jnp.zeros((12, D), F32)], axis=0).astype(BF16)
    fc1_sent = line_send(at, copies, *fc1_lines)
    qkv_y.second_send()
    qkv_z.second_send()
    sum_shared(shared, held.at[2], slots.at[0])
    shared = share_all(at, copies, "z", held.at[2], slots.at[1])
    shift_back_finish(went_out, out_grid, back_out[1], back_out[3], output)
    total = jnp.concatenate([qkv_y.finish(), qkv_z.finish()], axis=1)
    for x in range(4):
        rows = [total[16 * i + 4 * x : 16 * i + 4 * x + 4] for i in range(3)]
        qkv_lines[0][x] = jnp.concatenate(rows + [jnp.zeros((4, D), F32)], axis=0).astype(BF16)
    qkv_sent = line_send(at, copies, *qkv_lines)
    sum_shared(shared, held.at[3], slots.at[1])
    shared = share_all(at, copies, "x", held.at[3], slots.at[2])
    shift_back_finish(went_tokens, grad_grid, back_tokens[1], back_tokens[3], grad_tokens)
    fc2_total[...] = line_finish(at, fc2_sent, *fc2_lines)
    fc1_total[...] = line_finish(at, fc1_sent, *fc1_lines)
    qkv_total[...] = line_finish(at, qkv_sent, *qkv_lines)
    sum_shared(shared, small_total, slots.at[2])


def whole(tokens, cotangent, gain_attn, w_qkv, w_proj, rel, gain_mlp, w_fc1, w_fc2):
    vmem = pl.BlockSpec(memory_space=pltpu.VMEM)
    copies = 100
    return pl.pallas_call(
        whole_kernel,
        out_shape=(
            jax.ShapeDtypeStruct((8, 48, D), BF16),
            jax.ShapeDtypeStruct((8, 48, D), F32),
            jax.ShapeDtypeStruct((16, D), F32),
            jax.ShapeDtypeStruct((32, D), F32),
            jax.ShapeDtypeStruct((16, D), F32),
            jax.ShapeDtypeStruct((2, 8, D), F32),
        ),
        in_specs=[vmem] * 5 + [pl.BlockSpec(memory_space=pl.ANY)] * 4,
        out_specs=[vmem] * 6,
        scratch_shapes=[pltpu.VMEM(shape, kind) for _, shape, kind in COMPUTE_SCRATCH]
        + [pltpu.VMEM(w.shape, BF16) for w in (w_qkv, w_proj, w_fc1, w_fc2)]
        + [pltpu.SemaphoreType.DMA((4,))]
        + [pltpu.VMEM((8, 48, D), F32)] * 4
        + [pltpu.VMEM((2, 8, D), F32)]
        + [pltpu.SemaphoreType.DMA((copies,))] * 2
        + part_scratch(64, D)
        + part_scratch(80, D)
        + part_scratch(48, 256) * 2
        + line_scratch(16)
        + line_scratch(32)
        + line_scratch(16)
        + [
            pltpu.VMEM((4, 2, 8, D), F32),
            pltpu.VMEM((2, 2, 8, D), F32),
            pltpu.VMEM((3, 4, 2, 8, D), F32),
        ]
        + SHIFT_SCRATCH * 2
        + ([pltpu.VMEM((4, 48, D), BF16)] + SHIFT_SCRATCH) * 2,
        compiler_params=pltpu.CompilerParams(
            collective_id=0, has_side_effects=True, vmem_limit_bytes=56 * 2**20
        ),
        name="whole_block",
    )(tokens, cotangent, gain_attn.reshape(1, D), rel, gain_mlp.reshape(1, D), w_qkv, w_proj, w_fc1, w_fc2)


def deliver_kernel(
    output, grad_tokens, qkv_total, fc1_total, fc2_total, small,
    output_to, grad_tokens_to, grad_qkv, grad_proj, table, grad_fc1, grad_fc2, gain_attn, gain_mlp
):
    grad_tokens_to[...] = grad_tokens[...]
    output_to[...] = output[...]
    for i in range(3):
        grad_qkv[:, D * i : D * i + D] = qkv_total[4 * i : 4 * i + 4]
    for i in range(4):
        grad_fc1[:, D * i : D * i + D] = fc1_total[4 * i : 4 * i + 4]
    grad_proj[...] = fc1_total[16:20]
    grad_fc2[...] = fc2_total[...]
    table[...] = small[1][:, 0:225]
    gain_attn[...] = small[0, 0]
    gain_mlp[...] = small[0, 1]


def deliver(*results):
    vmem = pl.BlockSpec(memory_space=pltpu.VMEM)
    return pl.pallas_call(
        deliver_kernel,
        out_shape=(
            jax.ShapeDtypeStruct((8, 48, D), BF16),
            jax.ShapeDtypeStruct((8, 48, D), F32),
            jax.ShapeDtypeStruct((4, 3 * D), F32),
            jax.ShapeDtypeStruct((4, D), F32),
            jax.ShapeDtypeStruct((8, 225), F32),
            jax.ShapeDtypeStruct((4, 4 * D), F32),
            jax.ShapeDtypeStruct((16, D), F32),
            jax.ShapeDtypeStruct((D,), F32),
            jax.ShapeDtypeStruct((D,), F32),
        ),
        in_specs=[vmem] * 6,
        out_specs=[vmem] * 9,
        name="deliver",
    )(*results)


def shards(tokens, cotangent, gain_attn, w_qkv, w_proj, rel_table, gain_mlp, w_fc1, w_fc2):
    return deliver(
        *whole(tokens, cotangent, gain_attn, w_qkv, w_proj, rel_table, gain_mlp, w_fc1, w_fc2)
    )


def solution(mesh):
    placed = (P("lat", "lon", None), P("lat", "lon", None), P(), P(), P(), P(), P(), P(), P())
    return jax.shard_map(
        shards,
        mesh=mesh,
        in_specs=placed,
        out_specs=(
            P("lat", "lon", None),
            P("lat", "lon", None),
            P(("lat", "lon"), None),
            P(("lat", "lon"), None),
            P(),
            P(("lat", "lon"), None),
            P(("lat", "lon"), None),
            P(),
            P(),
        ),
        check_vma=False,
    )
```

```python
import jax
import jax.numpy as jnp
from jax import lax
from jax.experimental import pallas as pl
from jax.experimental.pallas import tpu as pltpu
from jax.sharding import PartitionSpec as P

NORM_EPSILON = 1e-05
D = 512


MESH = pl.DeviceIdType.MESH
F32 = jnp.float32
BF16 = jnp.bfloat16


def place():
    lat = lax.axis_index("lat")
    lon = lax.axis_index("lon")
    return {
        "c": lax.rem(lon, 2),
        "x": lax.rem(lon // 2, 4),
        "y": lat // 2,
        "z": (lon // 8) * 2 + lax.rem(lat, 2),
    }


def moved(at, *hops):
    there = dict(at)
    for axis, step in hops:
        there[axis] = lax.rem(at[axis] + step, 2 if axis == "c" else 4)
    lat = there["y"] * 2 + lax.rem(there["z"], 2)
    lon = (there["z"] // 2) * 8 + there["x"] * 2 + there["c"]
    return (lat, lon)


def neighbour(step_lat, step_lon):
    return (
        lax.rem(lax.axis_index("lat") + step_lat + 8, 8),
        lax.rem(lax.axis_index("lon") + step_lon + 16, 16),
    )


PLANE = [(i, j) for i in range(4) for j in range(4) if (i, j) != (0, 0)]


def greet(at):
    barrier = pltpu.get_barrier_semaphore()
    others = [moved(at, ("c", 1))]
    others += [moved(at, ("z", i), ("x", j)) for i, j in PLANE]
    others += [moved(at, ("y", i), ("x", j)) for i, j in PLANE if i]
    steps = ((1, 0), (0, 1), (1, 1), (-1, 0), (0, -1), (-1, -1))
    others += [neighbour(*step) for step in steps]
    for other in others:
        pl.semaphore_signal(barrier, inc=1, device_id=other, device_id_type=MESH)
    return len(others)


class Copies:
    def __init__(self, send_sems, recv_sems):
        self.send_sems, self.recv_sems, self.used = send_sems, recv_sems, 0

    def reserve(self, count):
        self.used += count
        return self.used - count

    def make(self, index, src, dst, device):
        return pltpu.make_async_remote_copy(
            src_ref=src,
            dst_ref=dst,
            send_sem=self.send_sems.at[index],
            recv_sem=self.recv_sems.at[index],
            device_id=device,
            device_id_type=MESH,
        )

    def start(self, src, dst, device):
        copy = self.make(self.reserve(1), src, dst, device)
        copy.start()
        return copy


class Part:
    def __init__(self, at, copies, axes, own, pair, piece1, piece2):
        self.at, self.copies = at, copies
        self.first, self.second = axes
        self.own, self.pair, self.piece1, self.piece2 = own, pair, piece1, piece2
        self.pairs, self.sent = {}, []

    def slot(self, step):
        return lax.rem(self.at[self.first] + step, 4)

    def place_start(self, step):
        j = self.slot(step)
        self.pairs[step] = self.copies.start(
            self.own.at[1 - self.at["c"], j], self.pair.at[j], moved(self.at, ("c", 1))
        )

    def place_send(self, step):
        self.pairs[step].wait()
        j, c = self.slot(step), self.at["c"]

        @pl.loop(0, 4)
        def _(i):
            self.pair[j, i] = self.pair[j, i] + self.own[c, j, i]

        if step:
            self.sent.append(
                self.copies.start(
                    self.pair.at[j], self.piece1.at[step - 1], moved(self.at, (self.first, step))
                )
            )

    def rows_start(self, key, rows):
        self.pairs[key] = self.copies.start(
            self.own.at[1 - self.at["c"], :, :, rows],
            self.pair.at[:, :, rows],
            moved(self.at, ("c", 1)),
        )

    def rows_send(self, key, rows):
        self.pairs[key].wait()
        c = self.at["c"]

        @pl.loop(0, 4)
        def _(j):
            self.pair[j, :, rows] = self.pair[j, :, rows] + self.own[c, j, :, rows]

        for step in (2, 1, 3):
            self.sent.append(
                self.copies.start(
                    self.pair.at[self.slot(step), :, rows],
                    self.piece1.at[step - 1, :, rows],
                    moved(self.at, (self.first, step)),
                )
            )

    def second_send(self):
        for copy in self.sent:
            copy.wait()
        mine = self.pair.at[self.slot(0)]

        @pl.loop(0, 4)
        def _(i):
            total = mine[i].astype(F32)
            for k in range(3):
                total = total + self.piece1[k, i].astype(F32)
            mine[i] = total.astype(BF16)

        self.sent = [
            self.copies.start(
                mine.at[lax.rem(self.at[self.second] + step, 4)],
                self.piece2.at[step - 1],
                moved(self.at, (self.second, step)),
            )
            for step in (2, 1, 3)
        ]

    def finish(self):
        total = self.pair[self.slot(0), self.at[self.second]].astype(F32)
        for copy in self.sent:
            copy.wait()
        for i in range(3):
            total = total + self.piece2[i].astype(F32)
        return total

    def plane_send(self, lines, lines_in):
        for copy in self.sent:
            copy.wait()
        mine = self.slot(0)
        for i in range(4):
            total = self.pair[mine, i].astype(F32)
            for k in range(3):
                total = total + self.piece1[k, i].astype(F32)
            for x in range(4):
                rows = [total[16 * k + 4 * x : 16 * k + 4 * x + 4] for k in range(3)]
                rows = rows + [jnp.zeros((4, total.shape[1]), F32)]
                lines[i, x] = jnp.concatenate(rows, axis=0).astype(BF16)
        at = self.at
        self.sent = [
            self.copies.start(
                lines.at[lax.rem(at[self.second] + i, 4), lax.rem(at["x"] + j, 4)],
                lines_in.at[4 * i + j - 1],
                moved(at, (self.second, i), ("x", j)),
            )
            for i, j in PLANE
        ]

    def plane_finish(self, lines, lines_in):
        total = lines[self.at[self.second], self.at["x"]].astype(F32)
        for copy in self.sent:
            copy.wait()
        for i in range(15):
            total = total + lines_in[i].astype(F32)
        return total


def part_scratch(rows, columns):
    return [
        pltpu.VMEM((2, 4, 4, rows, columns), BF16),
        pltpu.VMEM((4, 4, rows, columns), BF16),
        pltpu.VMEM((3, 4, rows, columns), BF16),
        pltpu.VMEM((3, rows, columns), BF16),
    ]


def line_send(at, copies, axis, lines, lines_in):
    return [
        copies.start(
            lines.at[lax.rem(at[axis] + step, 4)], lines_in.at[step - 1], moved(at, (axis, step))
        )
        for step in (2, 1, 3)
    ]


def line_finish(at, started, axis, lines, lines_in):
    total = lines[at[axis]].astype(F32)
    for copy in started:
        copy.wait()
    for i in range(3):
        total = total + lines_in[i].astype(F32)
    return total


def line_scratch(rows):
    return [pltpu.VMEM((4, rows, D), BF16), pltpu.VMEM((3, rows, D), BF16)]


def plane_scratch():
    return [pltpu.VMEM((4, 4, 16, 256), BF16), pltpu.VMEM((15, 16, 256), BF16)]


def share_line(at, copies, axis, held, slots):
    slots[at[axis]] = held[...]
    return [
        copies.start(held, slots.at[at[axis]], moved(at, (axis, step)))
        for step in range(1, slots.shape[0])
    ]


def share_plane(at, copies, held, slots):
    mine = at["z"] * 4 + at["x"]
    slots[mine] = held[...]
    return [copies.start(held, slots.at[mine], moved(at, ("z", i), ("x", j))) for i, j in PLANE]


def sum_shared(started, held, slots):
    for copy in started:
        copy.wait()
    total = slots[0]
    for i in range(1, slots.shape[0]):
        total = total + slots[i]
    held[...] = total


def shift_in_start(copies, source, rows_in, edge, edge_in):
    started = [copies.start(source.at[4:8], rows_in, neighbour(1, 0))]
    for half in range(2):
        ends = [source[4 * half + r, 32:48].astype(F32)[12:16] for r in range(4)]
        edge[half] = jnp.concatenate(ends, axis=0).astype(BF16)
    started.append(copies.start(edge.at[0], edge_in.at[0], neighbour(0, 1)))
    started.append(copies.start(edge.at[1], edge_in.at[1], neighbour(1, 1)))
    return started


def shift_in_finish(started, source, rows_in, edge_in, grid):
    for copy in started:
        copy.wait()
    for row in range(8):
        held = (rows_in[row] if row < 4 else source[row - 4]).astype(F32)
        turned = pltpu.roll(held, 4, 0)
        ends = edge_in[1 if row < 4 else 0].astype(F32)[4 * (row % 4) : 4 * (row % 4) + 4]
        grid[row] = jnp.concatenate(
            [jnp.concatenate([ends, turned[4:8]], axis=0), turned[8:48]], axis=0
        )


def shift_back_start(copies, grid, rows_out, rows_in, edge, edge_in):
    for row in range(4):
        rows_out[row] = pltpu.roll(grid[row], 44, 0).astype(BF16)
    started = [copies.start(rows_out, rows_in, neighbour(-1, 0))]
    for half in range(2):
        firsts = [grid[4 * half + r, 0:8][0:4] for r in range(4)]
        edge[half] = jnp.concatenate(firsts, axis=0).astype(BF16)
    started.append(copies.start(edge.at[1], edge_in.at[1], neighbour(0, -1)))
    started.append(copies.start(edge.at[0], edge_in.at[0], neighbour(-1, -1)))
    return started


def shift_back_finish(started, grid, rows_in, edge_in, result):
    for copy in started:
        copy.wait()
    for row in range(8):
        if row < 4:
            turned = pltpu.roll(grid[row + 4], 44, 0)
        else:
            turned = rows_in[row - 4].astype(F32)
        ends = edge_in[1 if row < 4 else 0].astype(F32)[4 * (row % 4) : 4 * (row % 4) + 4]
        whole = jnp.concatenate(
            [turned[0:40], jnp.concatenate([turned[40:44], ends], axis=0)], axis=0
        )
        result[row] = whole.astype(result.dtype)


SHIFT_SCRATCH = [
    pltpu.VMEM((4, 48, D), BF16),
    pltpu.VMEM((2, 16, D), BF16),
    pltpu.VMEM((2, 16, D), BF16),
]


TOKENS = 384
WINDOWS = 6
PAIRS = 4
TILE = 16


def mm(a, b):
    return lax.dot_general(a, b, (((1,), (0,)), ((), ())), preferred_element_type=F32)


def mm_nt(a, b):
    return lax.dot_general(a, b, (((1,), (1,)), ((), ())), preferred_element_type=F32)


def mm_tn(a, b):
    return lax.dot_general(a, b, (((0,), (0,)), ((), ())), preferred_element_type=F32)


def split_low(value):
    high = value.astype(BF16)
    return high, (value - high.astype(F32)).astype(BF16)


def iota(shape, dim):
    return lax.broadcasted_iota(jnp.int32, shape, dim)


def tiles(body):
    @pl.loop(0, TOKENS // TILE, unroll=8)
    def _(i):
        body(i, pl.ds(pl.multiple_of(i * TILE, TILE), TILE))


def grid_tile(grid, i):
    window, row = i // 4, lax.rem(i, 4) * 2
    columns = pl.ds(pl.multiple_of(window * 8, 8), 8)
    return jnp.concatenate([grid[row, columns], grid[row + 1, columns]], axis=0)


def store_grid_tile(grid, i, tile):
    window, row = i // 4, lax.rem(i, 4) * 2
    columns = pl.ds(pl.multiple_of(window * 8, 8), 8)
    grid[row, columns] = tile[0:8]
    grid[row + 1, columns] = tile[8:16]


def normalise(vectors):
    centred = vectors - jnp.mean(vectors, axis=-1, keepdims=True)
    factor = lax.rsqrt(jnp.mean(centred * centred, axis=-1, keepdims=True) + NORM_EPSILON)
    return centred * factor, factor


def normalise_back(grad_out, normal, factor, gain):
    grad_hat = grad_out * gain
    inner = (
        grad_hat
        - jnp.mean(grad_hat, axis=-1, keepdims=True)
        - normal * jnp.mean(grad_hat * normal, axis=-1, keepdims=True)
    )
    return factor * inner


def line_order(axes):
    place_of = iota((1, D), 1)
    core, r = place_of >> 8, place_of & 3
    at = {axis: (place_of >> shift) & 3 for axis, shift in zip(axes, (6, 4, 2))}
    z = ((at["z"] & 1) << 6) | ((at["z"] >> 1) << 5)
    feature = (at["y"] << 7) | z | (at["x"] << 3) | (core << 2) | r
    return jnp.where(iota((D, D), 0) == feature, 1.0, 0.0).astype(BF16)


def pair_offsets():
    row, column = iota((256, 128), 0), iota((256, 128), 1)
    target = ((column >> 6) << 7) + 15 * ((column >> 3) & 7) + (column & 7)
    return jnp.where(row == target, 1.0, 0.0).astype(BF16)


def store_wide(halves, i, rows):
    halves[0, 8 * i : 8 * i + 8] = rows[:, 0:128]
    halves[1, 8 * i : 8 * i + 8] = rows[:, 128:256]


def load_strided(halves, first):
    return jnp.concatenate([halves[k, pl.ds(first, 8, stride=8), :] for k in range(2)], axis=1)


def expand_bias(rel, table, shifted, bias, masked):
    table[...] = jnp.zeros_like(table)
    table[:, 0:225] = rel[...]
    whole = table[...]
    for b in range(8):
        store_wide(shifted, b, pltpu.roll(whole, (256 - (7 - b)) % 256, 1))
    spread = pair_offsets()
    key, query = iota((64, 128), 0), iota((64, 128), 1) & 63
    apart = jnp.where((key >> 5) == (query >> 5), 0.0, -1e30)
    apart = jnp.where(masked, apart, 0.0)
    for p in range(PAIRS):
        heads = []
        for h in (2 * p, 2 * p + 1):
            rows = load_strided(shifted, h)
            turned = [pltpu.roll(rows, 256 - (105 - 15 * a), 1)[:, 0:128] for a in range(8)]
            heads.append(jnp.concatenate(turned, axis=0))
        high, low = split_low(jnp.concatenate(heads, axis=1))
        bias[p] = mm(high, spread) + mm(low, spread) + apart


def collect_table(grad_bias, collected, total):
    spread = pair_offsets()
    for p in range(PAIRS):
        high, low = split_low(grad_bias[p])
        both = mm_nt(high, spread) + mm_nt(low, spread)
        for k in range(2):
            one = both[:, 128 * k : 128 * k + 128]
            one = jnp.concatenate([one, jnp.zeros_like(one)], axis=1)
            rows = one[56:64]
            for a in range(7):
                rows = rows + pltpu.roll(one[8 * a : 8 * a + 8], 105 - 15 * a, 1)
            h = 2 * p + k
            store_wide(collected, h, rows)
    table = load_strided(collected, 7)
    for b in range(7):
        table = table + pltpu.roll(load_strided(collected, b), 7 - b, 1)
    total[...] = table


def both_heads(pair):
    left = iota(pair.shape, 1) < 64
    zero = jnp.zeros_like(pair)
    return jnp.concatenate([jnp.where(left, pair, zero), jnp.where(left, zero, pair)], axis=0)


def own_heads(crossed):
    return jnp.where(iota((64, 128), 1) < 64, crossed[0:64], crossed[64:128])


def window_rows(w):
    return pl.ds(pl.multiple_of(w * 64, 64), 64)


def attend(w, qkv, bias, probs, attended):
    rows = window_rows(w)
    for p in range(PAIRS):
        query = qkv[rows, 128 * p : 128 * p + 128]
        keys = qkv[rows, D + 128 * p : D + 128 * p + 128]
        values = qkv[rows, 2 * D + 128 * p : 2 * D + 128 * p + 128]
        scores = mm_nt(keys, both_heads(query)) + bias[p]
        powers = jnp.exp(scores - jnp.max(scores, axis=0, keepdims=True))
        each = powers / jnp.sum(powers, axis=0, keepdims=True)
        probs[w, p] = each
        crossed = mm_tn(each.astype(BF16), values)
        attended[rows, 128 * p : 128 * p + 128] = own_heads(crossed).astype(BF16)


def attend_back(w, qkv, probs, grad_attended, grad_bias, grad_rows):
    rows = window_rows(w)
    for p in range(PAIRS):
        query = both_heads(qkv[rows, 128 * p : 128 * p + 128])
        keys = qkv[rows, D + 128 * p : D + 128 * p + 128]
        values = qkv[rows, 2 * D + 128 * p : 2 * D + 128 * p + 128]
        grads = both_heads(grad_attended[rows, 128 * p : 128 * p + 128])
        each = probs[w, p]
        grad_probs = mm_nt(values, grads)
        grad_scores = each * (grad_probs - jnp.sum(each * grad_probs, axis=0, keepdims=True))
        grad_bias[p] += grad_scores
        low = grad_scores.astype(BF16)
        grad_query = own_heads(mm_tn(low, keys)) * 0.125
        grad_rows[rows, 128 * p : 128 * p + 128] = grad_query.astype(BF16)
        grad_rows[rows, D + 128 * p : D + 128 * p + 128] = mm(low, query).astype(BF16)
        grad_rows[rows, 2 * D + 128 * p : 2 * D + 128 * p + 128] = mm(
            each.astype(BF16), grads
        ).astype(BF16)


GELU_SCALE = 0.7978845608028654
GELU_CUBE = 0.044715


def gelu_both(hidden):
    square = hidden * hidden
    swing = jnp.tanh(GELU_SCALE * hidden * (1.0 + GELU_CUBE * square))
    half = 0.5 + 0.5 * swing
    slope = half + (0.5 * GELU_SCALE) * hidden * (1.0 - swing * swing) * (
        1.0 + 3.0 * GELU_CUBE * square
    )
    return hidden * half, slope


def eight(tile):
    return tile[0:8] + tile[8:16]


COMPUTE_SCRATCH = [
    ("hat1", (TOKENS, D), F32),
    ("factor1", (TOKENS, 128), F32),
    ("norm1", (TOKENS, D), BF16),
    ("qkv", (TOKENS, 3 * D), BF16),
    ("attended", (TOKENS, D), BF16),
    ("resid", (TOKENS, D), F32),
    ("hat2", (TOKENS, D), F32),
    ("factor2", (TOKENS, 128), F32),
    ("norm2", (TOKENS, D), BF16),
    ("turned", (TOKENS, D), BF16),
    ("order_fc1", (D, D), BF16),
    ("order_y", (D, D), BF16),
    ("order_z", (D, D), BF16),
    ("cot", (TOKENS, D), BF16),
    ("hidden", (TOKENS, D), F32),
    ("grad_active", (TOKENS, D), F32),
    ("active", (TOKENS, D), BF16),
    ("grad_hidden", (TOKENS, D), BF16),
    ("mlp_out", (TOKENS, D), F32),
    ("grad_norm", (TOKENS, D), F32),
    ("grad_resid", (TOKENS, D), F32),
    ("grad_resid_low", (TOKENS, D), BF16),
    ("grad_attended", (TOKENS, D), BF16),
    ("grad_rows", (TOKENS, 3 * D), BF16),
    ("probs", (WINDOWS, PAIRS, 64, 128), F32),
    ("bias", (PAIRS, 64, 128), F32),
    ("grad_bias", (PAIRS, 64, 128), F32),
    ("table", (8, 256), F32),
    ("shifted", (2, 64, 128), F32),
    ("gain_sums", (2, 8, D), F32),
]


class Block:
    def __init__(self, refs):
        for (name, _, _), ref in zip(COMPUTE_SCRATCH, refs):
            setattr(self, name, ref)


def attention_forward(s, x_grid, gain_attn, w_qkv):
    def first_norm(i, rows):
        normal, factor = normalise(grid_tile(x_grid, i))
        s.hat1[rows] = normal
        s.factor1[rows] = jnp.broadcast_to(factor, (TILE, 128))
        s.norm1[rows] = (normal * gain_attn[...]).astype(BF16)

    tiles(first_norm)
    for i in range(3):
        columns = slice(D * i, D * i + D)
        part = mm(s.norm1[...], w_qkv[:, columns])
        s.qkv[:, columns] = (part * 0.125 if i == 0 else part).astype(BF16)

    @pl.loop(0, WINDOWS, unroll=3)
    def _(w):
        attend(w, s.qkv, s.bias, s.probs, s.attended)


def before_mlp(s, x_grid, c_grid, gain_mlp):
    def second_norm(i, rows):
        resid = s.resid[rows] + grid_tile(x_grid, i)
        normal, factor = normalise(resid)
        s.resid[rows] = resid
        s.hat2[rows] = normal
        s.factor2[rows] = jnp.broadcast_to(factor, (TILE, 128))
        s.norm2[rows] = (normal * gain_mlp[...]).astype(BF16)
        s.cot[rows] = grid_tile(c_grid, i).astype(BF16)

    tiles(second_norm)
    s.turned[...] = mm(s.norm2[...], s.order_fc1[...]).astype(BF16)
    s.mlp_out[...] = jnp.zeros_like(s.mlp_out)
    s.grad_norm[...] = jnp.zeros_like(s.grad_norm)


def mlp_step(s, j, block, w_fc1, w_fc2, own_fc2, own_fc1):
    columns = pl.ds(pl.multiple_of(j * D, D), D)
    s.hidden[...] = mm(s.norm2[...], w_fc1[:, columns])
    s.grad_active[...] = mm_nt(s.cot[...], w_fc2[columns])

    def bend(_, rows):
        active, slope = gelu_both(s.hidden[rows])
        s.active[rows] = active.astype(BF16)
        s.grad_hidden[rows] = (slope * s.grad_active[rows]).astype(BF16)

    tiles(bend)
    grad_fc2 = mm_tn(s.active[...], s.cot[...]).astype(BF16).reshape(2, 2, 4, 2, 16, D)
    for low in range(2):
        for high in range(2):
            for x in range(4):
                for c in range(2):
                    own_fc2[c, j, 2 * high + low, 16 * x : 16 * x + 16, :] = grad_fc2[
                        low, high, x, c
                    ]
    grad_fc1 = mm_tn(s.turned[...], s.grad_hidden[...]).astype(BF16)
    own_fc1[:, :, :, block, :] = grad_fc1.reshape(2, 4, 4, 16, D)
    s.mlp_out[...] += mm(s.active[...], w_fc2[columns])
    s.grad_norm[...] += mm_nt(s.grad_hidden[...], w_fc1[:, columns])


def after_mlp(s, gain_mlp, out_grid):
    s.gain_sums[...] = jnp.zeros_like(s.gain_sums)

    def second_back(i, rows):
        grad, normal = s.grad_norm[rows], s.hat2[rows]
        s.gain_sums[1] += eight(grad * normal)
        grad_resid = s.cot[rows].astype(F32) + normalise_back(
            grad, normal, s.factor2[rows][:, 0:1], gain_mlp[...]
        )
        s.grad_resid[rows] = grad_resid
        s.grad_resid_low[rows] = grad_resid.astype(BF16)
        store_grid_tile(out_grid, i, s.resid[rows] + s.mlp_out[rows])

    tiles(second_back)


def attention_after(s, gain_attn, grad_grid, small):
    def first_back(i, rows):
        grad, normal = s.grad_norm[rows], s.hat1[rows]
        s.gain_sums[0] += eight(grad * normal)
        back = normalise_back(grad, normal, s.factor1[rows][:, 0:1], gain_attn[...])
        store_grid_tile(grad_grid, i, s.grad_resid[rows] + back)

    tiles(first_back)
    small[:, 256:512] = jnp.zeros((8, 256), F32)
    for i in range(2):
        total = jnp.sum(s.gain_sums[i], axis=0, keepdims=True)
        small[2 * i : 2 * i + 1, 256:512] = total[:, 0:256]
        small[2 * i + 1 : 2 * i + 2, 256:512] = total[:, 256:512]


def whole_kernel(
    tokens, cotangent, gain_attn, rel, gain_mlp, w_qkv_hbm, w_proj_hbm, w_fc1_hbm, w_fc2_hbm,
    output, grad_tokens, qkv_total, fc1_total, fc2_total, small_total, *scratch
):
    refs = list(scratch)

    def take(count):
        taken = refs[:count]
        del refs[:count]
        return taken

    s = Block(take(len(COMPUTE_SCRATCH)))
    weights, weight_sem = take(4), take(1)[0]
    w_qkv, w_proj, w_fc1, w_fc2 = weights
    x_grid, c_grid, out_grid, grad_grid, small = take(5)
    send_sems, recv_sems = take(2)
    at = place()
    copies = Copies(send_sems, recv_sems)
    fc2 = Part(at, copies, ("y", "z"), *take(4))
    fc1 = Part(at, copies, ("x", "z"), *take(4))
    qkv_y = Part(at, copies, ("y", "z"), *take(4))
    qkv_z = Part(at, copies, ("z", "y"), *take(4))
    fc2_lines, fc1_lines, qkv_y_lines, qkv_z_lines = take(2), take(2), take(2), take(2)
    held, pair_slots, y_slots, plane_slots = take(4)
    in_tokens, in_cot = take(3), take(3)
    back_out, back_tokens = take(4), take(4)

    loads = []
    for i, source in enumerate((w_qkv_hbm, w_proj_hbm, w_fc1_hbm, w_fc2_hbm)):
        loads.append(pltpu.make_async_copy(source, weights[i], weight_sem.at[i]))
        loads[-1].start()
    partners = greet(at)
    expand_bias(rel, s.table, s.shifted, s.bias, lax.axis_index("lat") == 0)
    pl.semaphore_wait(pltpu.get_barrier_semaphore(), partners)
    came_tokens = shift_in_start(copies, tokens, *in_tokens)
    s.order_fc1[...] = line_order(("x", "z", "y"))
    s.order_y[...] = line_order(("y", "z", "x"))
    s.order_z[...] = line_order(("z", "y", "x"))
    shift_in_finish(came_tokens, tokens, in_tokens[0], in_tokens[2], x_grid)
    came_cot = shift_in_start(copies, cotangent, *in_cot)
    loads[0].wait()
    attention_forward(s, x_grid, gain_attn, w_qkv)
    for load in loads[1:]:
        load.wait()
    s.resid[...] = mm(s.attended[...], w_proj[...])
    shift_in_finish(came_cot, cotangent, in_cot[0], in_cot[2], c_grid)
    before_mlp(s, x_grid, c_grid, gain_mlp)

    steps = (2, 1, 3, 0)
    blocks = [pl.ds(pl.multiple_of(16 * fc2.slot(step), 16), 16) for step in steps]
    for i in range(4):
        mlp_step(s, fc2.slot(steps[i]), blocks[i], w_fc1, w_fc2, fc2.own, fc1.own)
        fc2.place_start(steps[i])
        fc1.rows_start(i, blocks[i])
        if i:
            fc2.place_send(steps[i - 1])
            fc1.rows_send(i - 1, blocks[i - 1])
    after_mlp(s, gain_mlp, out_grid)
    fc1.rows_send(3, blocks[3])
    fc2.place_send(0)
    went_out = shift_back_start(copies, out_grid, *back_out)
    s.turned[...] = mm(s.attended[...], s.order_fc1[...]).astype(BF16)
    grad_proj = mm_tn(s.turned[...], s.grad_resid_low[...]).astype(BF16)
    fc1.own[:, :, :, 64:80, :] = grad_proj.reshape(2, 4, 4, 16, D)
    fc1.rows_start(4, slice(64, 80))
    s.grad_attended[...] = mm_nt(s.grad_resid_low[...], w_proj[...]).astype(BF16)
    s.grad_bias[...] = jnp.zeros_like(s.grad_bias)
    fc1.rows_send(4, slice(64, 80))

    @pl.loop(0, WINDOWS, unroll=2)
    def _(w):
        attend_back(w, s.qkv, s.probs, s.grad_attended, s.grad_bias, s.grad_rows)

    for left, order, part in ((0, s.order_y, qkv_y), (256, s.order_z, qkv_z)):
        s.turned[...] = mm(s.norm1[...], order[...]).astype(BF16)
        for i in range(3):
            columns = slice(D * i + left, D * i + left + 256)
            grad = mm_tn(s.turned[...], s.grad_rows[:, columns]).astype(BF16)
            part.own[:, :, :, 16 * i : 16 * i + 16, :] = grad.reshape(2, 4, 4, 16, 256)
        part.rows_start(0, slice(0, 48))
    s.grad_norm[...] = mm_nt(s.grad_rows[...], w_qkv[...])
    qkv_y.rows_send(0, slice(0, 48))
    qkv_z.rows_send(0, slice(0, 48))
    collect_table(s.grad_bias, s.shifted, s.table)
    attention_after(s, gain_attn, grad_grid, small)
    small[:, 0:256] = s.table[...]
    held[0] = small[...]
    shared = share_line(at, copies, "c", held.at[0], pair_slots)
    fc2.second_send()
    sum_shared(shared, held.at[1], pair_slots)
    shared = share_line(at, copies, "y", held.at[1], y_slots)
    went_tokens = shift_back_start(copies, grad_grid, *back_tokens)
    fc1.second_send()
    sum_shared(shared, held.at[2], y_slots)
    shared = share_plane(at, copies, held.at[2], plane_slots)
    qkv_y.plane_send(*qkv_y_lines)
    qkv_z.plane_send(*qkv_z_lines)
    fc2_lines[0][...] = fc2.finish().astype(BF16).reshape(4, 16, D)
    fc2_sent = line_send(at, copies, "x", *fc2_lines)
    total = fc1.finish()
    for y in range(4):
        rows = [total[16 * i + 4 * y : 16 * i + 4 * y + 4] for i in range(5)]
        fc1_lines[0][y] = jnp.concatenate(rows + [jnp.zeros((12, D), F32)], axis=0).astype(BF16)
    fc1_sent = line_send(at, copies, "y", *fc1_lines)
    shift_back_finish(went_out, out_grid, back_out[1], back_out[3], output)
    shift_back_finish(went_tokens, grad_grid, back_tokens[1], back_tokens[3], grad_tokens)
    sum_shared(shared, small_total, plane_slots)
    qkv_total[:, 0:256] = qkv_y.plane_finish(*qkv_y_lines)
    qkv_total[:, 256:512] = qkv_z.plane_finish(*qkv_z_lines)
    fc2_total[...] = line_finish(at, fc2_sent, "x", *fc2_lines)
    fc1_total[...] = line_finish(at, fc1_sent, "y", *fc1_lines)


def whole(tokens, cotangent, gain_attn, w_qkv, w_proj, rel, gain_mlp, w_fc1, w_fc2):
    vmem = pl.BlockSpec(memory_space=pltpu.VMEM)
    copies = 120
    return pl.pallas_call(
        whole_kernel,
        out_shape=(
            jax.ShapeDtypeStruct((8, 48, D), BF16),
            jax.ShapeDtypeStruct((8, 48, D), F32),
            jax.ShapeDtypeStruct((16, D), F32),
            jax.ShapeDtypeStruct((32, D), F32),
            jax.ShapeDtypeStruct((16, D), F32),
            jax.ShapeDtypeStruct((8, D), F32),
        ),
        in_specs=[vmem] * 5 + [pl.BlockSpec(memory_space=pl.ANY)] * 4,
        out_specs=[vmem] * 6,
        scratch_shapes=[pltpu.VMEM(shape, kind) for _, shape, kind in COMPUTE_SCRATCH]
        + [pltpu.VMEM(w.shape, BF16) for w in (w_qkv, w_proj, w_fc1, w_fc2)]
        + [pltpu.SemaphoreType.DMA((4,))]
        + [pltpu.VMEM((8, 48, D), F32)] * 4
        + [pltpu.VMEM((8, D), F32)]
        + [pltpu.SemaphoreType.DMA((copies,))] * 2
        + part_scratch(64, D)
        + part_scratch(80, D)
        + part_scratch(48, 256) * 2
        + line_scratch(16)
        + line_scratch(32)
        + plane_scratch() * 2
        + [
            pltpu.VMEM((3, 8, D), F32),
            pltpu.VMEM((2, 8, D), F32),
            pltpu.VMEM((4, 8, D), F32),
            pltpu.VMEM((16, 8, D), F32),
        ]
        + SHIFT_SCRATCH * 2
        + ([pltpu.VMEM((4, 48, D), BF16)] + SHIFT_SCRATCH) * 2,
        compiler_params=pltpu.CompilerParams(
            collective_id=0, has_side_effects=True, vmem_limit_bytes=56 * 2**20
        ),
        name="whole_block",
    )(tokens, cotangent, gain_attn.reshape(1, D), rel, gain_mlp.reshape(1, D), w_qkv, w_proj, w_fc1, w_fc2)


def deliver_kernel(
    output, grad_tokens, qkv_total, fc1_total, fc2_total, small,
    output_to, grad_tokens_to, grad_qkv, grad_proj, table, grad_fc1, grad_fc2, gain_attn, gain_mlp
):
    grad_tokens_to[...] = grad_tokens[...]
    output_to[...] = output[...]
    for i in range(3):
        grad_qkv[:, D * i : D * i + D] = qkv_total[4 * i : 4 * i + 4]
    for i in range(4):
        grad_fc1[:, D * i : D * i + D] = fc1_total[4 * i : 4 * i + 4]
    grad_proj[...] = fc1_total[16:20]
    grad_fc2[...] = fc2_total[...]
    table[...] = small[:, 0:225]
    for i in range(2):
        gain_attn[256 * i : 256 * i + 256] = small[i, 256:512]
        gain_mlp[256 * i : 256 * i + 256] = small[2 + i, 256:512]


def deliver(*results):
    vmem = pl.BlockSpec(memory_space=pltpu.VMEM)
    return pl.pallas_call(
        deliver_kernel,
        out_shape=(
            jax.ShapeDtypeStruct((8, 48, D), BF16),
            jax.ShapeDtypeStruct((8, 48, D), F32),
            jax.ShapeDtypeStruct((4, 3 * D), F32),
            jax.ShapeDtypeStruct((4, D), F32),
            jax.ShapeDtypeStruct((8, 225), F32),
            jax.ShapeDtypeStruct((4, 4 * D), F32),
            jax.ShapeDtypeStruct((16, D), F32),
            jax.ShapeDtypeStruct((D,), F32),
            jax.ShapeDtypeStruct((D,), F32),
        ),
        in_specs=[vmem] * 6,
        out_specs=[vmem] * 9,
        name="deliver",
    )(*results)


def shards(tokens, cotangent, gain_attn, w_qkv, w_proj, rel_table, gain_mlp, w_fc1, w_fc2):
    return deliver(
        *whole(tokens, cotangent, gain_attn, w_qkv, w_proj, rel_table, gain_mlp, w_fc1, w_fc2)
    )


def solution(mesh):
    placed = (P("lat", "lon", None), P("lat", "lon", None), P(), P(), P(), P(), P(), P(), P())
    return jax.shard_map(
        shards,
        mesh=mesh,
        in_specs=placed,
        out_specs=(
            P("lat", "lon", None),
            P("lat", "lon", None),
            P(("lat", "lon"), None),
            P(("lat", "lon"), None),
            P(),
            P(("lat", "lon"), None),
            P(("lat", "lon"), None),
            P(),
            P(),
        ),
        check_vma=False,
    )
```

```python
import jax
import jax.numpy as jnp
from jax import lax
from jax.experimental import pallas as pl
from jax.experimental.pallas import tpu as pltpu
from jax.sharding import PartitionSpec as P

NORM_EPSILON = 1e-05
D = 512


MESH = pl.DeviceIdType.MESH
F32 = jnp.float32
BF16 = jnp.bfloat16


def place():
    lat = lax.axis_index("lat")
    lon = lax.axis_index("lon")
    return {
        "c": lax.rem(lon, 2),
        "x": lax.rem(lon // 2, 4),
        "y": lat // 2,
        "z": (lon // 8) * 2 + lax.rem(lat, 2),
    }


def moved(at, *hops):
    there = dict(at)
    for axis, step in hops:
        there[axis] = lax.rem(at[axis] + step, 2 if axis == "c" else 4)
    lat = there["y"] * 2 + lax.rem(there["z"], 2)
    lon = (there["z"] // 2) * 8 + there["x"] * 2 + there["c"]
    return (lat, lon)


def neighbour(step_lat, step_lon):
    return (
        lax.rem(lax.axis_index("lat") + step_lat + 8, 8),
        lax.rem(lax.axis_index("lon") + step_lon + 16, 16),
    )


PLANE = [(i, j) for i in range(4) for j in range(4) if (i, j) != (0, 0)]


def greet(at):
    barrier = pltpu.get_barrier_semaphore()
    others = [moved(at, ("c", 1))]
    others += [moved(at, ("z", i), ("x", j)) for i, j in PLANE]
    others += [moved(at, ("z", i), ("y", j)) for i, j in PLANE if j]
    others += [moved(at, ("c", 1), ("x", j)) for j in (1, 2, 3)]
    steps = ((1, 0), (0, 1), (1, 1), (-1, 0), (0, -1), (-1, -1))
    others += [neighbour(*step) for step in steps]
    for other in others:
        pl.semaphore_signal(barrier, inc=1, device_id=other, device_id_type=MESH)
    return len(others)


class Copies:
    def __init__(self, send_sems, recv_sems):
        self.send_sems, self.recv_sems, self.used = send_sems, recv_sems, 0

    def reserve(self, count):
        self.used += count
        return self.used - count

    def make(self, index, src, dst, device):
        return pltpu.make_async_remote_copy(
            src_ref=src,
            dst_ref=dst,
            send_sem=self.send_sems.at[index],
            recv_sem=self.recv_sems.at[index],
            device_id=device,
            device_id_type=MESH,
        )

    def start(self, src, dst, device):
        copy = self.make(self.reserve(1), src, dst, device)
        copy.start()
        return copy


class Part:
    def __init__(self, at, copies, axes, fours, own, pair, piece1, lines, lines_in):
        self.at, self.copies, self.fours = at, copies, fours
        self.first, self.second, self.third = axes
        self.own, self.pair, self.piece1 = own, pair, piece1
        self.lines, self.lines_in = lines, lines_in
        self.pairs, self.sent = {}, []

    def slot(self, step):
        return lax.rem(self.at[self.first] + step, 4)

    def place_start(self, step):
        j = self.slot(step)
        self.pairs[step] = self.copies.start(
            self.own.at[1 - self.at["c"], j], self.pair.at[j], moved(self.at, ("c", 1))
        )

    def place_send(self, step):
        self.pairs[step].wait()
        j, c = self.slot(step), self.at["c"]

        @pl.loop(0, 4)
        def _(i):
            self.pair[j, i] = self.pair[j, i] + self.own[c, j, i]

        if step:
            self.sent.append(
                self.copies.start(
                    self.pair.at[j], self.piece1.at[step - 1], moved(self.at, (self.first, step))
                )
            )

    def rows_start(self, key, rows):
        self.pairs[key] = self.copies.start(
            self.own.at[1 - self.at["c"], :, :, rows],
            self.pair.at[:, :, rows],
            moved(self.at, ("c", 1)),
        )

    def rows_send(self, key, rows):
        self.pairs[key].wait()
        c = self.at["c"]

        @pl.loop(0, 4)
        def _(j):
            self.pair[j, :, rows] = self.pair[j, :, rows] + self.own[c, j, :, rows]

        for step in (2, 1, 3):
            self.sent.append(
                self.copies.start(
                    self.pair.at[self.slot(step), :, rows],
                    self.piece1.at[step - 1, :, rows],
                    moved(self.at, (self.first, step)),
                )
            )

    def plane_send(self):
        for copy in self.sent:
            copy.wait()
        mine, lines = self.slot(0), self.lines
        for i in range(4):
            total = self.pair[mine, i].astype(F32)
            for k in range(3):
                total = total + self.piece1[k, i].astype(F32)
            for k in range(4):
                rows = total[16 * k : 16 * k + 16]
                if self.fours:
                    fours = [total[16 * m + 4 * k : 16 * m + 4 * k + 4] for m in range(4)]
                    rows = jnp.concatenate(fours, axis=0)
                lines[i, k] = rows.astype(BF16)
        at = self.at
        self.sent = [
            self.copies.start(
                lines.at[lax.rem(at[self.second] + i, 4), lax.rem(at[self.third] + j, 4)],
                self.lines_in.at[4 * i + j - 1],
                moved(at, (self.second, i), (self.third, j)),
            )
            for i, j in PLANE
        ]

    def finish(self):
        total = self.lines[self.at[self.second], self.at[self.third]].astype(F32)
        for copy in self.sent:
            copy.wait()
        for i in range(15):
            total = total + self.lines_in[i].astype(F32)
        return total


def part_scratch(columns):
    return [
        pltpu.VMEM((2, 4, 4, 64, columns), BF16),
        pltpu.VMEM((4, 4, 64, columns), BF16),
        pltpu.VMEM((3, 4, 64, columns), BF16),
        pltpu.VMEM((4, 4, 16, columns), BF16),
        pltpu.VMEM((15, 16, columns), BF16),
    ]


def share(at, copies, axes, held, slots):
    outer, inner = axes
    mine = at[outer] * 4 + at[inner]
    slots[mine] = held[...]
    return [
        copies.start(held, slots.at[mine], moved(at, (outer, i), (inner, j)))
        for i, j in PLANE
        if i < slots.shape[0] // 4
    ]


def sum_shared(started, held, slots):
    for copy in started:
        copy.wait()
    total = slots[0].astype(F32)
    for i in range(1, slots.shape[0]):
        total = total + slots[i].astype(F32)
    held[...] = total.astype(held.dtype)


def shift_in_start(copies, source, rows_in, edge, edge_in):
    started = [copies.start(source.at[4:8], rows_in, neighbour(1, 0))]
    for half in range(2):
        ends = [source[4 * half + r, 32:48].astype(F32)[12:16] for r in range(4)]
        edge[half] = jnp.concatenate(ends, axis=0).astype(BF16)
    started.append(copies.start(edge.at[0], edge_in.at[0], neighbour(0, 1)))
    started.append(copies.start(edge.at[1], edge_in.at[1], neighbour(1, 1)))
    return started


def shift_in_finish(started, source, rows_in, edge_in, grid):
    for copy in started:
        copy.wait()
    for row in range(8):
        held = (rows_in[row] if row < 4 else source[row - 4]).astype(F32)
        turned = pltpu.roll(held, 4, 0)
        ends = edge_in[1 if row < 4 else 0].astype(F32)[4 * (row % 4) : 4 * (row % 4) + 4]
        grid[row] = jnp.concatenate(
            [jnp.concatenate([ends, turned[4:8]], axis=0), turned[8:48]], axis=0
        )


def shift_back_start(copies, grid, rows_out, rows_in, edge, edge_in):
    for row in range(4):
        rows_out[row] = pltpu.roll(grid[row], 44, 0).astype(BF16)
    started = [copies.start(rows_out, rows_in, neighbour(-1, 0))]
    for half in range(2):
        firsts = [grid[4 * half + r, 0:8][0:4] for r in range(4)]
        edge[half] = jnp.concatenate(firsts, axis=0).astype(BF16)
    started.append(copies.start(edge.at[1], edge_in.at[1], neighbour(0, -1)))
    started.append(copies.start(edge.at[0], edge_in.at[0], neighbour(-1, -1)))
    return started


def shift_back_finish(started, grid, rows_in, edge_in, result):
    for copy in started:
        copy.wait()
    for row in range(8):
        if row < 4:
            turned = pltpu.roll(grid[row + 4], 44, 0)
        else:
            turned = rows_in[row - 4].astype(F32)
        ends = edge_in[1 if row < 4 else 0].astype(F32)[4 * (row % 4) : 4 * (row % 4) + 4]
        whole = jnp.concatenate(
            [turned[0:40], jnp.concatenate([turned[40:44], ends], axis=0)], axis=0
        )
        result[row] = whole.astype(result.dtype)


SHIFT_SCRATCH = [
    pltpu.VMEM((4, 48, D), BF16),
    pltpu.VMEM((2, 16, D), BF16),
    pltpu.VMEM((2, 16, D), BF16),
]


TOKENS = 384
WINDOWS = 6
PAIRS = 4
TILE = 16


def mm(a, b):
    return lax.dot_general(a, b, (((1,), (0,)), ((), ())), preferred_element_type=F32)


def mm_nt(a, b):
    return lax.dot_general(a, b, (((1,), (1,)), ((), ())), preferred_element_type=F32)


def mm_tn(a, b):
    return lax.dot_general(a, b, (((0,), (0,)), ((), ())), preferred_element_type=F32)


def split_low(value):
    high = value.astype(BF16)
    return high, (value - high.astype(F32)).astype(BF16)


def iota(shape, dim):
    return lax.broadcasted_iota(jnp.int32, shape, dim)


def tiles(body):
    @pl.loop(0, TOKENS // TILE, unroll=8)
    def _(i):
        body(i, pl.ds(pl.multiple_of(i * TILE, TILE), TILE))


def grid_tile(grid, i):
    window, row = i // 4, lax.rem(i, 4) * 2
    columns = pl.ds(pl.multiple_of(window * 8, 8), 8)
    return jnp.concatenate([grid[row, columns], grid[row + 1, columns]], axis=0)


def store_grid_tile(grid, i, tile):
    window, row = i // 4, lax.rem(i, 4) * 2
    columns = pl.ds(pl.multiple_of(window * 8, 8), 8)
    grid[row, columns] = tile[0:8]
    grid[row + 1, columns] = tile[8:16]


def normalise(vectors):
    centred = vectors - jnp.mean(vectors, axis=-1, keepdims=True)
    factor = lax.rsqrt(jnp.mean(centred * centred, axis=-1, keepdims=True) + NORM_EPSILON)
    return centred * factor, factor


def normalise_back(grad_out, normal, factor, gain):
    grad_hat = grad_out * gain
    inner = (
        grad_hat
        - jnp.mean(grad_hat, axis=-1, keepdims=True)
        - normal * jnp.mean(grad_hat * normal, axis=-1, keepdims=True)
    )
    return factor * inner


def line_order(axes):
    place_of = iota((D, 1), 0)
    core, r = place_of >> 8, place_of & 3
    at = {axis: (place_of >> shift) & 3 for axis, shift in zip(axes, (6, 4, 2))}
    z = ((at["z"] & 1) << 6) | ((at["z"] >> 1) << 5)
    feature = (at["y"] << 7) | z | (at["x"] << 3) | (core << 2) | r
    return jnp.where(iota((D, D), 1) == feature, 1.0, 0.0).astype(BF16)


def pair_offsets():
    row, column = iota((256, 128), 0), iota((256, 128), 1)
    target = ((column >> 6) << 7) + 15 * ((column >> 3) & 7) + (column & 7)
    return jnp.where(row == target, 1.0, 0.0).astype(BF16)


def store_wide(halves, i, rows):
    halves[0, 8 * i : 8 * i + 8] = rows[:, 0:128]
    halves[1, 8 * i : 8 * i + 8] = rows[:, 128:256]


def load_strided(halves, first):
    return jnp.concatenate([halves[k, pl.ds(first, 8, stride=8), :] for k in range(2)], axis=1)


def expand_bias(rel, table, shifted, bias, masked):
    table[...] = jnp.zeros_like(table)
    table[:, 0:225] = rel[...]
    whole = table[...]
    for b in range(8):
        store_wide(shifted, b, pltpu.roll(whole, (256 - (7 - b)) % 256, 1))
    spread = pair_offsets()
    key, query = iota((64, 128), 0), iota((64, 128), 1) & 63
    apart = jnp.where((key >> 5) == (query >> 5), 0.0, -1e30)
    apart = jnp.where(masked, apart, 0.0)
    for p in range(PAIRS):
        heads = []
        for h in (2 * p, 2 * p + 1):
            rows = load_strided(shifted, h)
            turned = [pltpu.roll(rows, 256 - (105 - 15 * a), 1)[:, 0:128] for a in range(8)]
            heads.append(jnp.concatenate(turned, axis=0))
        high, low = split_low(jnp.concatenate(heads, axis=1))
        bias[p] = mm(high, spread) + mm(low, spread) + apart


def collect_table(grad_bias, collected, total):
    spread = pair_offsets()
    for p in range(PAIRS):
        high, low = split_low(grad_bias[p])
        both = mm_nt(high, spread) + mm_nt(low, spread)
        for k in range(2):
            one = both[:, 128 * k : 128 * k + 128]
            one = jnp.concatenate([one, jnp.zeros_like(one)], axis=1)
            rows = one[56:64]
            for a in range(7):
                rows = rows + pltpu.roll(one[8 * a : 8 * a + 8], 105 - 15 * a, 1)
            h = 2 * p + k
            store_wide(collected, h, rows)
    table = load_strided(collected, 7)
    for b in range(7):
        table = table + pltpu.roll(load_strided(collected, b), 7 - b, 1)
    total[...] = table


def both_heads(pair):
    left = iota(pair.shape, 1) < 64
    zero = jnp.zeros_like(pair)
    return jnp.concatenate([jnp.where(left, pair, zero), jnp.where(left, zero, pair)], axis=0)


def own_heads(crossed):
    return jnp.where(iota((64, 128), 1) < 64, crossed[0:64], crossed[64:128])


def window_rows(w):
    return pl.ds(pl.multiple_of(w * 64, 64), 64)


def attend(w, qkv, bias, probs, attended):
    rows = window_rows(w)
    for p in range(PAIRS):
        query = qkv[rows, 128 * p : 128 * p + 128]
        keys = qkv[rows, D + 128 * p : D + 128 * p + 128]
        values = qkv[rows, 2 * D + 128 * p : 2 * D + 128 * p + 128]
        scores = mm_nt(keys, both_heads(query)) + bias[p]
        powers = jnp.exp(scores - jnp.max(scores, axis=0, keepdims=True))
        each = powers / jnp.sum(powers, axis=0, keepdims=True)
        probs[w, p] = each
        crossed = mm_tn(each.astype(BF16), values)
        attended[rows, 128 * p : 128 * p + 128] = own_heads(crossed).astype(BF16)


def attend_back(w, qkv, probs, grad_attended, grad_bias, grad_rows):
    rows = window_rows(w)
    for p in range(PAIRS):
        query = both_heads(qkv[rows, 128 * p : 128 * p + 128])
        keys = qkv[rows, D + 128 * p : D + 128 * p + 128]
        values = qkv[rows, 2 * D + 128 * p : 2 * D + 128 * p + 128]
        grads = both_heads(grad_attended[rows, 128 * p : 128 * p + 128])
        each = probs[w, p]
        grad_probs = mm_nt(values, grads)
        grad_scores = each * (grad_probs - jnp.sum(each * grad_probs, axis=0, keepdims=True))
        grad_bias[p] += grad_scores
        low = grad_scores.astype(BF16)
        grad_query = own_heads(mm_tn(low, keys)) * 0.125
        grad_rows[rows, 128 * p : 128 * p + 128] = grad_query.astype(BF16)
        grad_rows[rows, D + 128 * p : D + 128 * p + 128] = mm(low, query).astype(BF16)
        grad_rows[rows, 2 * D + 128 * p : 2 * D + 128 * p + 128] = mm(
            each.astype(BF16), grads
        ).astype(BF16)


GELU_SCALE = 0.7978845608028654
GELU_CUBE = 0.044715


def gelu_both(hidden):
    square = hidden * hidden
    swing = jnp.tanh(GELU_SCALE * hidden * (1.0 + GELU_CUBE * square))
    half = 0.5 + 0.5 * swing
    slope = half + (0.5 * GELU_SCALE) * hidden * (1.0 - swing * swing) * (
        1.0 + 3.0 * GELU_CUBE * square
    )
    return hidden * half, slope


def eight(tile):
    return tile[0:8] + tile[8:16]


COMPUTE_SCRATCH = [
    ("hat1", (TOKENS, D), F32),
    ("factor1", (TOKENS, 128), F32),
    ("norm1", (TOKENS, D), BF16),
    ("qkv", (TOKENS, 3 * D), BF16),
    ("attended", (TOKENS, D), BF16),
    ("resid", (TOKENS, D), F32),
    ("hat2", (TOKENS, D), F32),
    ("factor2", (TOKENS, 128), F32),
    ("norm2", (TOKENS, D), BF16),
    ("turned", (D, TOKENS), BF16),
    ("order_y", (D, D), BF16),
    ("order_x", (D, D), BF16),
    ("cot", (TOKENS, D), BF16),
    ("hidden", (TOKENS, D), F32),
    ("grad_active", (TOKENS, D), F32),
    ("active", (TOKENS, D), BF16),
    ("grad_hidden", (TOKENS, D), BF16),
    ("mlp_out", (TOKENS, D), F32),
    ("grad_norm", (TOKENS, D), F32),
    ("grad_resid", (TOKENS, D), F32),
    ("grad_resid_low", (TOKENS, D), BF16),
    ("grad_attended", (TOKENS, D), BF16),
    ("grad_rows", (TOKENS, 3 * D), BF16),
    ("probs", (WINDOWS, PAIRS, 64, 128), F32),
    ("bias", (PAIRS, 64, 128), F32),
    ("grad_bias", (PAIRS, 64, 128), F32),
    ("table", (8, 256), F32),
    ("shifted", (2, 64, 128), F32),
    ("gain_sums", (2, 8, D), F32),
]


class Block:
    def __init__(self, refs):
        for (name, _, _), ref in zip(COMPUTE_SCRATCH, refs):
            setattr(self, name, ref)


def attention_forward(s, x_grid, gain_attn, w_qkv):
    def first_norm(i, rows):
        normal, factor = normalise(grid_tile(x_grid, i))
        s.hat1[rows] = normal
        s.factor1[rows] = jnp.broadcast_to(factor, (TILE, 128))
        s.norm1[rows] = (normal * gain_attn[...]).astype(BF16)

    tiles(first_norm)
    for i in range(3):
        columns = slice(D * i, D * i + D)
        part = mm(s.norm1[...], w_qkv[:, columns])
        s.qkv[:, columns] = (part * 0.125 if i == 0 else part).astype(BF16)

    @pl.loop(0, WINDOWS, unroll=3)
    def _(w):
        attend(w, s.qkv, s.bias, s.probs, s.attended)


def before_mlp(s, x_grid, c_grid, gain_mlp):
    def second_norm(i, rows):
        resid = s.resid[rows] + grid_tile(x_grid, i)
        normal, factor = normalise(resid)
        s.resid[rows] = resid
        s.hat2[rows] = normal
        s.factor2[rows] = jnp.broadcast_to(factor, (TILE, 128))
        s.norm2[rows] = (normal * gain_mlp[...]).astype(BF16)
        s.cot[rows] = grid_tile(c_grid, i).astype(BF16)

    tiles(second_norm)
    s.turned[...] = mm_nt(s.order_x[...], s.norm2[...]).astype(BF16)
    s.mlp_out[...] = jnp.zeros_like(s.mlp_out)
    s.grad_norm[...] = jnp.zeros_like(s.grad_norm)


def mlp_step(s, j, block, w_fc1, w_fc2, own_fc2, own_fc1):
    columns = pl.ds(pl.multiple_of(j * D, D), D)
    s.hidden[...] = mm(s.norm2[...], w_fc1[:, columns])
    s.grad_active[...] = mm_nt(s.cot[...], w_fc2[columns])

    def bend(_, rows):
        active, slope = gelu_both(s.hidden[rows])
        s.active[rows] = active.astype(BF16)
        s.grad_hidden[rows] = (slope * s.grad_active[rows]).astype(BF16)

    tiles(bend)
    grad_fc2 = mm_tn(s.active[...], s.cot[...]).astype(BF16).reshape(2, 2, 4, 2, 16, D)
    for low in range(2):
        for high in range(2):
            for x in range(4):
                for c in range(2):
                    own_fc2[c, j, 2 * high + low, 16 * x : 16 * x + 16, :] = grad_fc2[
                        low, high, x, c
                    ]
    grad_fc1 = mm(s.turned[...], s.grad_hidden[...]).astype(BF16)
    own_fc1[:, :, :, block, :] = grad_fc1.reshape(2, 4, 4, 16, D)
    s.mlp_out[...] += mm(s.active[...], w_fc2[columns])
    s.grad_norm[...] += mm_nt(s.grad_hidden[...], w_fc1[:, columns])


def after_mlp(s, gain_mlp, out_grid):
    s.gain_sums[...] = jnp.zeros_like(s.gain_sums)

    def second_back(i, rows):
        grad, normal = s.grad_norm[rows], s.hat2[rows]
        s.gain_sums[1] += eight(grad * normal)
        grad_resid = s.cot[rows].astype(F32) + normalise_back(
            grad, normal, s.factor2[rows][:, 0:1], gain_mlp[...]
        )
        s.grad_resid[rows] = grad_resid
        s.grad_resid_low[rows] = grad_resid.astype(BF16)
        store_grid_tile(out_grid, i, s.resid[rows] + s.mlp_out[rows])

    tiles(second_back)


def attention_after(s, gain_attn, grad_grid, small):
    def first_back(i, rows):
        grad, normal = s.grad_norm[rows], s.hat1[rows]
        s.gain_sums[0] += eight(grad * normal)
        back = normalise_back(grad, normal, s.factor1[rows][:, 0:1], gain_attn[...])
        store_grid_tile(grad_grid, i, s.grad_resid[rows] + back)

    tiles(first_back)
    gains = [jnp.sum(s.gain_sums[i], axis=0, keepdims=True) for i in range(2)]
    rows = [gain[:, 256 * k : 256 * k + 256] for gain in gains for k in range(2)]
    small[...] = jnp.concatenate([s.table[...]] + rows + [jnp.zeros((4, 256), F32)], axis=0)


def whole_kernel(
    tokens, cotangent, gain_attn, rel, gain_mlp, w_qkv_hbm, w_proj_hbm, w_fc1_hbm, w_fc2_hbm,
    output, grad_tokens, qkv_total, fc1_total, fc2_total, small_total, *scratch
):
    refs = list(scratch)

    def take(count):
        taken = refs[:count]
        del refs[:count]
        return taken

    s = Block(take(len(COMPUTE_SCRATCH)))
    weights, weight_sem = take(4), take(1)[0]
    w_qkv, w_proj, w_fc1, w_fc2 = weights
    x_grid, c_grid, out_grid, grad_grid, small = take(5)
    send_sems, recv_sems = take(2)
    at = place()
    copies = Copies(send_sems, recv_sems)
    fc2 = Part(at, copies, ("y", "z", "x"), False, *take(5))
    fc1 = Part(at, copies, ("x", "z", "y"), True, *take(5))
    rest_y = Part(at, copies, ("y", "z", "x"), True, *take(5))
    rest_x = Part(at, copies, ("x", "z", "y"), True, *take(5))
    halves = ((slice(0, 256), s.order_y, rest_y), (slice(256, 512), s.order_x, rest_x))
    held, pair_slots, plane_slots = take(3)
    in_tokens, in_cot = take(3), take(3)
    back_out, back_tokens = take(4), take(4)

    loads = []
    for i, source in enumerate((w_qkv_hbm, w_proj_hbm, w_fc1_hbm, w_fc2_hbm)):
        loads.append(pltpu.make_async_copy(source, weights[i], weight_sem.at[i]))
        loads[-1].start()
    partners = greet(at)
    expand_bias(rel, s.table, s.shifted, s.bias, lax.axis_index("lat") == 0)
    pl.semaphore_wait(pltpu.get_barrier_semaphore(), partners)
    came_tokens = shift_in_start(copies, tokens, *in_tokens)
    s.order_y[...] = line_order(("y", "z", "x"))
    s.order_x[...] = line_order(("x", "z", "y"))
    shift_in_finish(came_tokens, tokens, in_tokens[0], in_tokens[2], x_grid)
    came_cot = shift_in_start(copies, cotangent, *in_cot)
    loads[0].wait()
    attention_forward(s, x_grid, gain_attn, w_qkv)
    for load in loads[1:]:
        load.wait()
    s.resid[...] = mm(s.attended[...], w_proj[...])
    shift_in_finish(came_cot, cotangent, in_cot[0], in_cot[2], c_grid)
    before_mlp(s, x_grid, c_grid, gain_mlp)

    steps = (2, 1, 3, 0)
    blocks = [pl.ds(pl.multiple_of(16 * fc2.slot(step), 16), 16) for step in steps]
    for i in range(4):
        mlp_step(s, fc2.slot(steps[i]), blocks[i], w_fc1, w_fc2, fc2.own, fc1.own)
        fc2.place_start(steps[i])
        fc1.rows_start(i, blocks[i])
        if i:
            fc2.place_send(steps[i - 1])
            fc1.rows_send(i - 1, blocks[i - 1])
    after_mlp(s, gain_mlp, out_grid)
    fc1.rows_send(3, blocks[3])
    fc2.place_send(0)
    went_out = shift_back_start(copies, out_grid, *back_out)
    for columns, order, part in halves:
        s.turned[...] = mm_nt(order[...], s.attended[...]).astype(BF16)
        grad_proj = mm(s.turned[...], s.grad_resid_low[:, columns]).astype(BF16)
        part.own[:, :, :, 48:64, :] = grad_proj.reshape(2, 4, 4, 16, 256)
        part.rows_start(1, slice(48, 64))
    s.grad_attended[...] = mm_nt(s.grad_resid_low[...], w_proj[...]).astype(BF16)
    s.grad_bias[...] = jnp.zeros_like(s.grad_bias)
    rest_y.rows_send(1, slice(48, 64))
    rest_x.rows_send(1, slice(48, 64))

    @pl.loop(0, WINDOWS, unroll=2)
    def _(w):
        attend_back(w, s.qkv, s.probs, s.grad_attended, s.grad_bias, s.grad_rows)

    for columns, order, part in halves:
        s.turned[...] = mm_nt(order[...], s.norm1[...]).astype(BF16)
        for i in range(3):
            grad_rows = s.grad_rows[:, D * i + columns.start : D * i + columns.stop]
            grad = mm(s.turned[...], grad_rows).astype(BF16)
            part.own[:, :, :, 16 * i : 16 * i + 16, :] = grad.reshape(2, 4, 4, 16, 256)
        part.rows_start(0, slice(0, 48))
    fc2.plane_send()
    s.grad_norm[...] = mm_nt(s.grad_rows[...], w_qkv[...])
    rest_y.rows_send(0, slice(0, 48))
    rest_x.rows_send(0, slice(0, 48))
    fc1.plane_send()
    collect_table(s.grad_bias, s.shifted, s.table)
    attention_after(s, gain_attn, grad_grid, small)
    held[0] = small[...].astype(BF16)
    shared = share(at, copies, ("c", "x"), held.at[0], pair_slots)
    went_tokens = shift_back_start(copies, grad_grid, *back_tokens)
    sum_shared(shared, held.at[1], pair_slots)
    shared = share(at, copies, ("z", "y"), held.at[1], plane_slots)
    rest_y.plane_send()
    rest_x.plane_send()
    shift_back_finish(went_out, out_grid, back_out[1], back_out[3], output)
    fc2_total[...] = fc2.finish()
    shift_back_finish(went_tokens, grad_grid, back_tokens[1], back_tokens[3], grad_tokens)
    fc1_total[...] = fc1.finish()
    sum_shared(shared, small_total, plane_slots)
    qkv_total[:, 0:256] = rest_y.finish()
    qkv_total[:, 256:512] = rest_x.finish()


def whole(tokens, cotangent, gain_attn, w_qkv, w_proj, rel, gain_mlp, w_fc1, w_fc2):
    vmem = pl.BlockSpec(memory_space=pltpu.VMEM)
    copies = 140
    return pl.pallas_call(
        whole_kernel,
        out_shape=(
            jax.ShapeDtypeStruct((8, 48, D), BF16),
            jax.ShapeDtypeStruct((8, 48, D), F32),
            jax.ShapeDtypeStruct((16, D), F32),
            jax.ShapeDtypeStruct((16, D), F32),
            jax.ShapeDtypeStruct((16, D), F32),
            jax.ShapeDtypeStruct((16, 256), F32),
        ),
        in_specs=[vmem] * 5 + [pl.BlockSpec(memory_space=pl.ANY)] * 4,
        out_specs=[vmem] * 6,
        scratch_shapes=[pltpu.VMEM(shape, kind) for _, shape, kind in COMPUTE_SCRATCH]
        + [pltpu.VMEM(w.shape, BF16) for w in (w_qkv, w_proj, w_fc1, w_fc2)]
        + [pltpu.SemaphoreType.DMA((4,))]
        + [pltpu.VMEM((8, 48, D), F32)] * 4
        + [pltpu.VMEM((16, 256), F32)]
        + [pltpu.SemaphoreType.DMA((copies,))] * 2
        + part_scratch(D) * 2
        + part_scratch(256) * 2
        + [
            pltpu.VMEM((2, 16, 256), BF16),
            pltpu.VMEM((8, 16, 256), BF16),
            pltpu.VMEM((16, 16, 256), BF16),
        ]
        + SHIFT_SCRATCH * 2
        + ([pltpu.VMEM((4, 48, D), BF16)] + SHIFT_SCRATCH) * 2,
        compiler_params=pltpu.CompilerParams(
            collective_id=0, has_side_effects=True, vmem_limit_bytes=56 * 2**20
        ),
        name="whole_block",
    )(tokens, cotangent, gain_attn.reshape(1, D), rel, gain_mlp.reshape(1, D), w_qkv, w_proj, w_fc1, w_fc2)


def deliver_kernel(
    output, grad_tokens, qkv_total, fc1_total, fc2_total, small,
    output_to, grad_tokens_to, grad_qkv, grad_proj, table, grad_fc1, grad_fc2, gain_attn, gain_mlp
):
    grad_tokens_to[...] = grad_tokens[...]
    output_to[...] = output[...]
    for i in range(3):
        grad_qkv[:, D * i : D * i + D] = qkv_total[4 * i : 4 * i + 4]
    for i in range(4):
        grad_fc1[:, D * i : D * i + D] = fc1_total[4 * i : 4 * i + 4]
    grad_proj[...] = qkv_total[12:16]
    grad_fc2[...] = fc2_total[...]
    table[...] = small[0:8, 0:225]
    for i in range(2):
        gain_attn[256 * i : 256 * i + 256] = small[8 + i]
        gain_mlp[256 * i : 256 * i + 256] = small[10 + i]


def deliver(*results):
    vmem = pl.BlockSpec(memory_space=pltpu.VMEM)
    return pl.pallas_call(
        deliver_kernel,
        out_shape=(
            jax.ShapeDtypeStruct((8, 48, D), BF16),
            jax.ShapeDtypeStruct((8, 48, D), F32),
            jax.ShapeDtypeStruct((4, 3 * D), F32),
            jax.ShapeDtypeStruct((4, D), F32),
            jax.ShapeDtypeStruct((8, 225), F32),
            jax.ShapeDtypeStruct((4, 4 * D), F32),
            jax.ShapeDtypeStruct((16, D), F32),
            jax.ShapeDtypeStruct((D,), F32),
            jax.ShapeDtypeStruct((D,), F32),
        ),
        in_specs=[vmem] * 6,
        out_specs=[vmem] * 9,
        name="deliver",
    )(*results)


def shards(tokens, cotangent, gain_attn, w_qkv, w_proj, rel_table, gain_mlp, w_fc1, w_fc2):
    return deliver(
        *whole(tokens, cotangent, gain_attn, w_qkv, w_proj, rel_table, gain_mlp, w_fc1, w_fc2)
    )


def solution(mesh):
    placed = (P("lat", "lon", None), P("lat", "lon", None), P(), P(), P(), P(), P(), P(), P())
    return jax.shard_map(
        shards,
        mesh=mesh,
        in_specs=placed,
        out_specs=(
            P("lat", "lon", None),
            P("lat", "lon", None),
            P(("lat", "lon"), None),
            P(("lat", "lon"), None),
            P(),
            P(("lat", "lon"), None),
            P(("lat", "lon"), None),
            P(),
            P(),
        ),
        check_vma=False,
    )
```

```python
import jax
import jax.numpy as jnp
from jax import lax
from jax.experimental import pallas as pl
from jax.experimental.pallas import tpu as pltpu
from jax.sharding import PartitionSpec as P

NORM_EPSILON = 1e-05
D = 512


MESH = pl.DeviceIdType.MESH
F32 = jnp.float32
BF16 = jnp.bfloat16


def place():
    lat = lax.axis_index("lat")
    lon = lax.axis_index("lon")
    return {
        "c": lax.rem(lon, 2),
        "x": lax.rem(lon // 2, 4),
        "y": lat // 2,
        "z": (lon // 8) * 2 + lax.rem(lat, 2),
    }


def moved(at, *hops):
    there = dict(at)
    for axis, step in hops:
        there[axis] = lax.rem(at[axis] + step, 2 if axis == "c" else 4)
    lat = there["y"] * 2 + lax.rem(there["z"], 2)
    lon = (there["z"] // 2) * 8 + there["x"] * 2 + there["c"]
    return (lat, lon)


def neighbour(step_lat, step_lon):
    return (
        lax.rem(lax.axis_index("lat") + step_lat + 8, 8),
        lax.rem(lax.axis_index("lon") + step_lon + 16, 16),
    )


PLANE = [(i, j) for i in range(4) for j in range(4) if (i, j) != (0, 0)]


def greet(at):
    barrier = pltpu.get_barrier_semaphore()
    others = [moved(at, ("c", 1))]
    others += [moved(at, ("z", i), ("x", j)) for i, j in PLANE]
    others += [moved(at, ("z", i), ("y", j)) for i, j in PLANE if j]
    others += [moved(at, ("c", 1), ("x", j)) for j in (1, 2, 3)]
    steps = ((1, 0), (0, 1), (1, 1), (-1, 0), (0, -1), (-1, -1))
    others += [neighbour(*step) for step in steps]
    for other in others:
        pl.semaphore_signal(barrier, inc=1, device_id=other, device_id_type=MESH)
    return len(others)


class Copies:
    def __init__(self, send_sems, recv_sems):
        self.send_sems, self.recv_sems, self.used = send_sems, recv_sems, 0

    def reserve(self, count):
        self.used += count
        return self.used - count

    def make(self, index, src, dst, device):
        return pltpu.make_async_remote_copy(
            src_ref=src,
            dst_ref=dst,
            send_sem=self.send_sems.at[index],
            recv_sem=self.recv_sems.at[index],
            device_id=device,
            device_id_type=MESH,
        )

    def start(self, src, dst, device):
        copy = self.make(self.reserve(1), src, dst, device)
        copy.start()
        return copy


class Part:
    def __init__(self, at, copies, axes, fours, own, pair, piece1, lines, lines_in):
        self.at, self.copies, self.fours = at, copies, fours
        self.first, self.second, self.third = axes
        self.own, self.pair, self.piece1 = own, pair, piece1
        self.lines, self.lines_in = lines, lines_in
        self.pairs, self.sent = {}, []

    def slot(self, step):
        return lax.rem(self.at[self.first] + step, 4)

    def place_start(self, step):
        j = self.slot(step)
        self.pairs[step] = self.copies.start(
            self.own.at[1 - self.at["c"], j], self.pair.at[j], moved(self.at, ("c", 1))
        )

    def place_send(self, step):
        self.pairs[step].wait()
        j, c = self.slot(step), self.at["c"]

        @pl.loop(0, 4)
        def _(i):
            self.pair[j, i] = self.pair[j, i] + self.own[c, j, i]

        if step:
            self.sent.append(
                self.copies.start(
                    self.pair.at[j], self.piece1.at[step - 1], moved(self.at, (self.first, step))
                )
            )

    def rows_start(self, key, rows):
        self.pairs[key] = self.copies.start(
            self.own.at[1 - self.at["c"], :, :, rows],
            self.pair.at[:, :, rows],
            moved(self.at, ("c", 1)),
        )

    def rows_send(self, key, rows):
        self.pairs[key].wait()
        c = self.at["c"]

        @pl.loop(0, 4)
        def _(j):
            self.pair[j, :, rows] = self.pair[j, :, rows] + self.own[c, j, :, rows]

        for step in (2, 1, 3):
            self.sent.append(
                self.copies.start(
                    self.pair.at[self.slot(step), :, rows],
                    self.piece1.at[step - 1, :, rows],
                    moved(self.at, (self.first, step)),
                )
            )

    def plane_send(self):
        for copy in self.sent:
            copy.wait()
        mine, lines = self.slot(0), self.lines
        for i in range(4):
            total = self.pair[mine, i].astype(F32)
            for k in range(3):
                total = total + self.piece1[k, i].astype(F32)
            for k in range(4):
                rows = total[16 * k : 16 * k + 16]
                if self.fours:
                    fours = [total[16 * m + 4 * k : 16 * m + 4 * k + 4] for m in range(4)]
                    rows = jnp.concatenate(fours, axis=0)
                lines[i, k] = rows.astype(BF16)
        at = self.at
        self.sent = [
            self.copies.start(
                lines.at[lax.rem(at[self.second] + i, 4), lax.rem(at[self.third] + j, 4)],
                self.lines_in.at[4 * i + j - 1],
                moved(at, (self.second, i), (self.third, j)),
            )
            for i, j in PLANE
        ]

    def finish(self):
        total = self.lines[self.at[self.second], self.at[self.third]].astype(F32)
        for copy in self.sent:
            copy.wait()
        for i in range(15):
            total = total + self.lines_in[i].astype(F32)
        return total


def part_scratch(columns):
    return [
        pltpu.VMEM((2, 4, 4, 64, columns), BF16),
        pltpu.VMEM((4, 4, 64, columns), BF16),
        pltpu.VMEM((3, 4, 64, columns), BF16),
        pltpu.VMEM((4, 4, 16, columns), BF16),
        pltpu.VMEM((15, 16, columns), BF16),
    ]


def share(at, copies, axes, held, slots):
    outer, inner = axes
    mine = at[outer] * 4 + at[inner]
    slots[mine] = held[...]
    return [
        copies.start(held, slots.at[mine], moved(at, (outer, i), (inner, j)))
        for i, j in PLANE
        if i < slots.shape[0] // 4
    ]


def sum_shared(started, held, slots):
    for copy in started:
        copy.wait()
    total = slots[0].astype(F32)
    for i in range(1, slots.shape[0]):
        total = total + slots[i].astype(F32)
    held[...] = total.astype(held.dtype)


def shift_in_start(copies, source, rows_in, edge, edge_in):
    started = [copies.start(source.at[4:8], rows_in, neighbour(1, 0))]
    for half in range(2):
        ends = [source[4 * half + r, 32:48].astype(F32)[12:16] for r in range(4)]
        edge[half] = jnp.concatenate(ends, axis=0).astype(BF16)
    started.append(copies.start(edge.at[0], edge_in.at[0], neighbour(0, 1)))
    started.append(copies.start(edge.at[1], edge_in.at[1], neighbour(1, 1)))
    return started


def shift_in_finish(started, source, rows_in, edge_in, grid):
    for copy in started:
        copy.wait()
    for row in range(8):
        held = (rows_in[row] if row < 4 else source[row - 4]).astype(F32)
        turned = pltpu.roll(held, 4, 0)
        ends = edge_in[1 if row < 4 else 0].astype(F32)[4 * (row % 4) : 4 * (row % 4) + 4]
        grid[row] = jnp.concatenate(
            [jnp.concatenate([ends, turned[4:8]], axis=0), turned[8:48]], axis=0
        )


def shift_back_start(copies, grid, rows_out, rows_in, edge, edge_in):
    for row in range(4):
        rows_out[row] = pltpu.roll(grid[row], 44, 0).astype(BF16)
    started = [copies.start(rows_out, rows_in, neighbour(-1, 0))]
    for half in range(2):
        firsts = [grid[4 * half + r, 0:8][0:4] for r in range(4)]
        edge[half] = jnp.concatenate(firsts, axis=0).astype(BF16)
    started.append(copies.start(edge.at[1], edge_in.at[1], neighbour(0, -1)))
    started.append(copies.start(edge.at[0], edge_in.at[0], neighbour(-1, -1)))
    return started


def shift_back_finish(started, grid, rows_in, edge_in, result):
    for copy in started:
        copy.wait()
    for row in range(8):
        if row < 4:
            turned = pltpu.roll(grid[row + 4], 44, 0)
        else:
            turned = rows_in[row - 4].astype(F32)
        ends = edge_in[1 if row < 4 else 0].astype(F32)[4 * (row % 4) : 4 * (row % 4) + 4]
        whole = jnp.concatenate(
            [turned[0:40], jnp.concatenate([turned[40:44], ends], axis=0)], axis=0
        )
        result[row] = whole.astype(result.dtype)


SHIFT_SCRATCH = [
    pltpu.VMEM((4, 48, D), BF16),
    pltpu.VMEM((2, 16, D), BF16),
    pltpu.VMEM((2, 16, D), BF16),
]


TOKENS = 384
WINDOWS = 6
PAIRS = 4
TILE = 16


def mm(a, b):
    return lax.dot_general(a, b, (((1,), (0,)), ((), ())), preferred_element_type=F32)


def mm_nt(a, b):
    return lax.dot_general(a, b, (((1,), (1,)), ((), ())), preferred_element_type=F32)


def mm_tn(a, b):
    return lax.dot_general(a, b, (((0,), (0,)), ((), ())), preferred_element_type=F32)


def split_low(value):
    high = value.astype(BF16)
    return high, (value - high.astype(F32)).astype(BF16)


def iota(shape, dim):
    return lax.broadcasted_iota(jnp.int32, shape, dim)


def tiles(body):
    @pl.loop(0, TOKENS // TILE, unroll=8)
    def _(i):
        body(i, pl.ds(pl.multiple_of(i * TILE, TILE), TILE))


def grid_tile(grid, i):
    window, row = i // 4, lax.rem(i, 4) * 2
    columns = pl.ds(pl.multiple_of(window * 8, 8), 8)
    return jnp.concatenate([grid[row, columns], grid[row + 1, columns]], axis=0)


def store_grid_tile(grid, i, tile):
    window, row = i // 4, lax.rem(i, 4) * 2
    columns = pl.ds(pl.multiple_of(window * 8, 8), 8)
    grid[row, columns] = tile[0:8]
    grid[row + 1, columns] = tile[8:16]


def normalise(vectors):
    centred = vectors - jnp.mean(vectors, axis=-1, keepdims=True)
    factor = lax.rsqrt(jnp.mean(centred * centred, axis=-1, keepdims=True) + NORM_EPSILON)
    return centred * factor, factor


def normalise_back(grad_out, normal, factor, gain):
    grad_hat = grad_out * gain
    inner = (
        grad_hat
        - jnp.mean(grad_hat, axis=-1, keepdims=True)
        - normal * jnp.mean(grad_hat * normal, axis=-1, keepdims=True)
    )
    return factor * inner


def line_order(axes):
    place_of = iota((D, 1), 0)
    core, r = place_of >> 8, place_of & 3
    at = {axis: (place_of >> shift) & 3 for axis, shift in zip(axes, (6, 4, 2))}
    z = ((at["z"] & 1) << 6) | ((at["z"] >> 1) << 5)
    feature = (at["y"] << 7) | z | (at["x"] << 3) | (core << 2) | r
    return jnp.where(iota((D, D), 1) == feature, 1.0, 0.0).astype(BF16)


def pair_offsets():
    row, column = iota((256, 128), 0), iota((256, 128), 1)
    target = ((column >> 6) << 7) + 15 * ((column >> 3) & 7) + (column & 7)
    return jnp.where(row == target, 1.0, 0.0).astype(BF16)


def store_wide(halves, i, rows):
    halves[0, 8 * i : 8 * i + 8] = rows[:, 0:128]
    halves[1, 8 * i : 8 * i + 8] = rows[:, 128:256]


def load_strided(halves, first):
    return jnp.concatenate([halves[k, pl.ds(first, 8, stride=8), :] for k in range(2)], axis=1)


def expand_bias(rel, table, shifted, bias, masked):
    table[...] = jnp.zeros_like(table)
    table[:, 0:225] = rel[...]
    whole = table[...]
    for b in range(8):
        store_wide(shifted, b, pltpu.roll(whole, (256 - (7 - b)) % 256, 1))
    spread = pair_offsets()
    key, query = iota((64, 128), 0), iota((64, 128), 1) & 63
    apart = jnp.where((key >> 5) == (query >> 5), 0.0, -1e30)
    apart = jnp.where(masked, apart, 0.0)
    for p in range(PAIRS):
        heads = []
        for h in (2 * p, 2 * p + 1):
            rows = load_strided(shifted, h)
            turned = [pltpu.roll(rows, 256 - (105 - 15 * a), 1)[:, 0:128] for a in range(8)]
            heads.append(jnp.concatenate(turned, axis=0))
        high, low = split_low(jnp.concatenate(heads, axis=1))
        bias[p] = mm(high, spread) + mm(low, spread) + apart


def collect_table(grad_bias, collected, total):
    spread = pair_offsets()
    for p in range(PAIRS):
        high, low = split_low(grad_bias[p])
        both = mm_nt(high, spread) + mm_nt(low, spread)
        for k in range(2):
            one = both[:, 128 * k : 128 * k + 128]
            one = jnp.concatenate([one, jnp.zeros_like(one)], axis=1)
            rows = one[56:64]
            for a in range(7):
                rows = rows + pltpu.roll(one[8 * a : 8 * a + 8], 105 - 15 * a, 1)
            h = 2 * p + k
            store_wide(collected, h, rows)
    table = load_strided(collected, 7)
    for b in range(7):
        table = table + pltpu.roll(load_strided(collected, b), 7 - b, 1)
    total[...] = table


def both_heads(pair):
    left = iota(pair.shape, 1) < 64
    zero = jnp.zeros_like(pair)
    return jnp.concatenate([jnp.where(left, pair, zero), jnp.where(left, zero, pair)], axis=0)


def own_heads(crossed):
    return jnp.where(iota((64, 128), 1) < 64, crossed[0:64], crossed[64:128])


def window_rows(w):
    return pl.ds(pl.multiple_of(w * 64, 64), 64)


def attend(w, qkv, bias, probs, attended):
    rows = window_rows(w)
    for p in range(PAIRS):
        query = qkv[rows, 128 * p : 128 * p + 128]
        keys = qkv[rows, D + 128 * p : D + 128 * p + 128]
        values = qkv[rows, 2 * D + 128 * p : 2 * D + 128 * p + 128]
        scores = mm_nt(keys, both_heads(query)) + bias[p]
        powers = jnp.exp(scores - jnp.max(scores, axis=0, keepdims=True))
        each = powers / jnp.sum(powers, axis=0, keepdims=True)
        probs[w, p] = each
        crossed = mm_tn(each.astype(BF16), values)
        attended[rows, 128 * p : 128 * p + 128] = own_heads(crossed).astype(BF16)


def attend_back(w, qkv, probs, grad_attended, grad_bias, grad_rows):
    rows = window_rows(w)
    for p in range(PAIRS):
        query = both_heads(qkv[rows, 128 * p : 128 * p + 128])
        keys = qkv[rows, D + 128 * p : D + 128 * p + 128]
        values = qkv[rows, 2 * D + 128 * p : 2 * D + 128 * p + 128]
        grads = both_heads(grad_attended[rows, 128 * p : 128 * p + 128])
        each = probs[w, p]
        grad_probs = mm_nt(values, grads)
        grad_scores = each * (grad_probs - jnp.sum(each * grad_probs, axis=0, keepdims=True))
        grad_bias[p] += grad_scores
        low = grad_scores.astype(BF16)
        grad_query = own_heads(mm_tn(low, keys)) * 0.125
        grad_rows[rows, 128 * p : 128 * p + 128] = grad_query.astype(BF16)
        grad_rows[rows, D + 128 * p : D + 128 * p + 128] = mm(low, query).astype(BF16)
        grad_rows[rows, 2 * D + 128 * p : 2 * D + 128 * p + 128] = mm(
            each.astype(BF16), grads
        ).astype(BF16)


GELU_SCALE = 0.7978845608028654
GELU_CUBE = 0.044715


def gelu_both(hidden):
    square = hidden * hidden
    swing = jnp.tanh(GELU_SCALE * hidden * (1.0 + GELU_CUBE * square))
    half = 0.5 + 0.5 * swing
    slope = half + (0.5 * GELU_SCALE) * hidden * (1.0 - swing * swing) * (
        1.0 + 3.0 * GELU_CUBE * square
    )
    return hidden * half, slope


def eight(tile):
    return tile[0:8] + tile[8:16]


COMPUTE_SCRATCH = [
    ("hat1", (TOKENS, D), F32),
    ("factor1", (TOKENS, 128), F32),
    ("norm1", (TOKENS, D), BF16),
    ("qkv", (TOKENS, 3 * D), BF16),
    ("attended", (TOKENS, D), BF16),
    ("resid", (TOKENS, D), F32),
    ("hat2", (TOKENS, D), F32),
    ("factor2", (TOKENS, 128), F32),
    ("norm2", (TOKENS, D), BF16),
    ("turned", (D, TOKENS), BF16),
    ("order_y", (D, D), BF16),
    ("order_x", (D, D), BF16),
    ("cot", (TOKENS, D), BF16),
    ("hidden", (TOKENS, D), F32),
    ("grad_active", (TOKENS, D), F32),
    ("active", (TOKENS, 4 * D), BF16),
    ("grad_hidden", (TOKENS, 4 * D), BF16),
    ("mlp_out", (TOKENS, D), F32),
    ("grad_norm", (TOKENS, D), F32),
    ("grad_resid", (TOKENS, D), F32),
    ("grad_resid_low", (TOKENS, D), BF16),
    ("grad_attended", (TOKENS, D), BF16),
    ("grad_rows", (TOKENS, 3 * D), BF16),
    ("probs", (WINDOWS, PAIRS, 64, 128), F32),
    ("bias", (PAIRS, 64, 128), F32),
    ("grad_bias", (PAIRS, 64, 128), F32),
    ("table", (8, 256), F32),
    ("shifted", (2, 64, 128), F32),
    ("gain_sums", (2, 8, D), F32),
]


class Block:
    def __init__(self, refs):
        for (name, _, _), ref in zip(COMPUTE_SCRATCH, refs):
            setattr(self, name, ref)


def attention_forward(s, x_grid, gain_attn, w_qkv):
    def first_norm(i, rows):
        normal, factor = normalise(grid_tile(x_grid, i))
        s.hat1[rows] = normal
        s.factor1[rows] = jnp.broadcast_to(factor, (TILE, 128))
        s.norm1[rows] = (normal * gain_attn[...]).astype(BF16)

    tiles(first_norm)
    for i in range(3):
        columns = slice(D * i, D * i + D)
        part = mm(s.norm1[...], w_qkv[:, columns])
        s.qkv[:, columns] = (part * 0.125 if i == 0 else part).astype(BF16)

    @pl.loop(0, WINDOWS, unroll=3)
    def _(w):
        attend(w, s.qkv, s.bias, s.probs, s.attended)


def before_mlp(s, x_grid, c_grid, gain_mlp):
    def second_norm(i, rows):
        resid = s.resid[rows] + grid_tile(x_grid, i)
        normal, factor = normalise(resid)
        s.resid[rows] = resid
        s.hat2[rows] = normal
        s.factor2[rows] = jnp.broadcast_to(factor, (TILE, 128))
        s.norm2[rows] = (normal * gain_mlp[...]).astype(BF16)
        s.cot[rows] = grid_tile(c_grid, i).astype(BF16)

    tiles(second_norm)
    s.turned[...] = mm_nt(s.order_x[...], s.norm2[...]).astype(BF16)


def mlp_step(s, j, block, w_fc1, w_fc2, own_fc2, own_fc1):
    columns = pl.ds(pl.multiple_of(j * D, D), D)
    s.hidden[...] = mm(s.norm2[...], w_fc1[:, columns])
    s.grad_active[...] = mm_nt(s.cot[...], w_fc2[columns])

    def bend(_, rows):
        active, slope = gelu_both(s.hidden[rows])
        s.active[rows, columns] = active.astype(BF16)
        s.grad_hidden[rows, columns] = (slope * s.grad_active[rows]).astype(BF16)

    tiles(bend)
    grad_fc2 = mm_tn(s.active[:, columns], s.cot[...]).astype(BF16).reshape(2, 2, 4, 2, 16, D)
    for low in range(2):
        for high in range(2):
            for x in range(4):
                for c in range(2):
                    own_fc2[c, j, 2 * high + low, 16 * x : 16 * x + 16, :] = grad_fc2[
                        low, high, x, c
                    ]
    grad_fc1 = mm(s.turned[...], s.grad_hidden[:, columns]).astype(BF16)
    own_fc1[:, :, :, block, :] = grad_fc1.reshape(2, 4, 4, 16, D)


def mlp_result(s, w_fc2, out_grid):
    s.mlp_out[...] = mm(s.active[...], w_fc2[...])

    def add(i, rows):
        store_grid_tile(out_grid, i, s.resid[rows] + s.mlp_out[rows])

    tiles(add)


def after_mlp(s, gain_mlp, w_fc1):
    s.grad_norm[...] = mm_nt(s.grad_hidden[...], w_fc1[...])
    s.gain_sums[...] = jnp.zeros_like(s.gain_sums)

    def second_back(i, rows):
        grad, normal = s.grad_norm[rows], s.hat2[rows]
        s.gain_sums[1] += eight(grad * normal)
        grad_resid = s.cot[rows].astype(F32) + normalise_back(
            grad, normal, s.factor2[rows][:, 0:1], gain_mlp[...]
        )
        s.grad_resid[rows] = grad_resid
        s.grad_resid_low[rows] = grad_resid.astype(BF16)

    tiles(second_back)


def attention_after(s, gain_attn, grad_grid, small):
    def first_back(i, rows):
        grad, normal = s.grad_norm[rows], s.hat1[rows]
        s.gain_sums[0] += eight(grad * normal)
        back = normalise_back(grad, normal, s.factor1[rows][:, 0:1], gain_attn[...])
        store_grid_tile(grad_grid, i, s.grad_resid[rows] + back)

    tiles(first_back)
    gains = [jnp.sum(s.gain_sums[i], axis=0, keepdims=True) for i in range(2)]
    rows = [gain[:, 256 * k : 256 * k + 256] for gain in gains for k in range(2)]
    small[...] = jnp.concatenate([s.table[...]] + rows + [jnp.zeros((4, 256), F32)], axis=0)


def whole_kernel(
    tokens, cotangent, gain_attn, rel, gain_mlp, w_qkv_hbm, w_proj_hbm, w_fc1_hbm, w_fc2_hbm,
    output, grad_tokens, qkv_total, fc1_total, fc2_total, small_total, *scratch
):
    refs = list(scratch)

    def take(count):
        taken = refs[:count]
        del refs[:count]
        return taken

    s = Block(take(len(COMPUTE_SCRATCH)))
    weights, weight_sem = take(4), take(1)[0]
    w_qkv, w_proj, w_fc1, w_fc2 = weights
    x_grid, c_grid, out_grid, grad_grid, small = take(5)
    send_sems, recv_sems = take(2)
    at = place()
    copies = Copies(send_sems, recv_sems)
    fc2 = Part(at, copies, ("y", "z", "x"), False, *take(5))
    fc1 = Part(at, copies, ("x", "z", "y"), True, *take(5))
    rest_y = Part(at, copies, ("y", "z", "x"), True, *take(5))
    rest_x = Part(at, copies, ("x", "z", "y"), True, *take(5))
    halves = ((slice(0, 256), s.order_y, rest_y), (slice(256, 512), s.order_x, rest_x))
    held, pair_slots, plane_slots = take(3)
    in_tokens, in_cot = take(3), take(3)
    back_out, back_tokens = take(4), take(4)

    loads = []
    for i, source in enumerate((w_qkv_hbm, w_proj_hbm, w_fc1_hbm, w_fc2_hbm)):
        loads.append(pltpu.make_async_copy(source, weights[i], weight_sem.at[i]))
        loads[-1].start()
    partners = greet(at)
    expand_bias(rel, s.table, s.shifted, s.bias, lax.axis_index("lat") == 0)
    pl.semaphore_wait(pltpu.get_barrier_semaphore(), partners)
    came_tokens = shift_in_start(copies, tokens, *in_tokens)
    s.order_y[...] = line_order(("y", "z", "x"))
    s.order_x[...] = line_order(("x", "z", "y"))
    shift_in_finish(came_tokens, tokens, in_tokens[0], in_tokens[2], x_grid)
    came_cot = shift_in_start(copies, cotangent, *in_cot)
    loads[0].wait()
    attention_forward(s, x_grid, gain_attn, w_qkv)
    for load in loads[1:]:
        load.wait()
    s.resid[...] = mm(s.attended[...], w_proj[...])
    shift_in_finish(came_cot, cotangent, in_cot[0], in_cot[2], c_grid)
    before_mlp(s, x_grid, c_grid, gain_mlp)

    steps = (2, 1, 3, 0)
    blocks = [pl.ds(pl.multiple_of(16 * fc2.slot(step), 16), 16) for step in steps]
    for i in range(4):
        mlp_step(s, fc2.slot(steps[i]), blocks[i], w_fc1, w_fc2, fc2.own, fc1.own)
        fc2.place_start(steps[i])
        fc1.rows_start(i, blocks[i])
        if i:
            fc2.place_send(steps[i - 1])
            fc1.rows_send(i - 1, blocks[i - 1])
    after_mlp(s, gain_mlp, w_fc1)
    fc1.rows_send(3, blocks[3])
    fc2.place_send(0)
    mlp_result(s, w_fc2, out_grid)
    went_out = shift_back_start(copies, out_grid, *back_out)
    for columns, order, part in halves:
        s.turned[...] = mm_nt(order[...], s.attended[...]).astype(BF16)
        grad_proj = mm(s.turned[...], s.grad_resid_low[:, columns]).astype(BF16)
        part.own[:, :, :, 48:64, :] = grad_proj.reshape(2, 4, 4, 16, 256)
        part.rows_start(1, slice(48, 64))
    s.grad_attended[...] = mm_nt(s.grad_resid_low[...], w_proj[...]).astype(BF16)
    s.grad_bias[...] = jnp.zeros_like(s.grad_bias)
    rest_y.rows_send(1, slice(48, 64))
    rest_x.rows_send(1, slice(48, 64))

    @pl.loop(0, WINDOWS, unroll=2)
    def _(w):
        attend_back(w, s.qkv, s.probs, s.grad_attended, s.grad_bias, s.grad_rows)

    fc2.plane_send()
    fc1.plane_send()
    for columns, order, part in halves:
        s.turned[...] = mm_nt(order[...], s.norm1[...]).astype(BF16)
        for i in range(3):
            grad_rows = s.grad_rows[:, D * i + columns.start : D * i + columns.stop]
            grad = mm(s.turned[...], grad_rows).astype(BF16)
            part.own[:, :, :, 16 * i : 16 * i + 16, :] = grad.reshape(2, 4, 4, 16, 256)
        part.rows_start(0, slice(0, 48))
    s.grad_norm[...] = mm_nt(s.grad_rows[...], w_qkv[...])
    rest_y.rows_send(0, slice(0, 48))
    rest_x.rows_send(0, slice(0, 48))
    collect_table(s.grad_bias, s.shifted, s.table)
    attention_after(s, gain_attn, grad_grid, small)
    held[0] = small[...].astype(BF16)
    shared = share(at, copies, ("c", "x"), held.at[0], pair_slots)
    went_tokens = shift_back_start(copies, grad_grid, *back_tokens)
    sum_shared(shared, held.at[1], pair_slots)
    shared = share(at, copies, ("z", "y"), held.at[1], plane_slots)
    rest_y.plane_send()
    rest_x.plane_send()
    shift_back_finish(went_out, out_grid, back_out[1], back_out[3], output)
    fc2_total[...] = fc2.finish()
    shift_back_finish(went_tokens, grad_grid, back_tokens[1], back_tokens[3], grad_tokens)
    fc1_total[...] = fc1.finish()
    sum_shared(shared, small_total, plane_slots)
    qkv_total[:, 0:256] = rest_y.finish()
    qkv_total[:, 256:512] = rest_x.finish()


def whole(tokens, cotangent, gain_attn, w_qkv, w_proj, rel, gain_mlp, w_fc1, w_fc2):
    vmem = pl.BlockSpec(memory_space=pltpu.VMEM)
    copies = 140
    return pl.pallas_call(
        whole_kernel,
        out_shape=(
            jax.ShapeDtypeStruct((8, 48, D), BF16),
            jax.ShapeDtypeStruct((8, 48, D), F32),
            jax.ShapeDtypeStruct((16, D), F32),
            jax.ShapeDtypeStruct((16, D), F32),
            jax.ShapeDtypeStruct((16, D), F32),
            jax.ShapeDtypeStruct((16, 256), F32),
        ),
        in_specs=[vmem] * 5 + [pl.BlockSpec(memory_space=pl.ANY)] * 4,
        out_specs=[vmem] * 6,
        scratch_shapes=[pltpu.VMEM(shape, kind) for _, shape, kind in COMPUTE_SCRATCH]
        + [pltpu.VMEM(w.shape, BF16) for w in (w_qkv, w_proj, w_fc1, w_fc2)]
        + [pltpu.SemaphoreType.DMA((4,))]
        + [pltpu.VMEM((8, 48, D), F32)] * 4
        + [pltpu.VMEM((16, 256), F32)]
        + [pltpu.SemaphoreType.DMA((copies,))] * 2
        + part_scratch(D) * 2
        + part_scratch(256) * 2
        + [
            pltpu.VMEM((2, 16, 256), BF16),
            pltpu.VMEM((8, 16, 256), BF16),
            pltpu.VMEM((16, 16, 256), BF16),
        ]
        + SHIFT_SCRATCH * 2
        + ([pltpu.VMEM((4, 48, D), BF16)] + SHIFT_SCRATCH) * 2,
        compiler_params=pltpu.CompilerParams(
            collective_id=0, has_side_effects=True, vmem_limit_bytes=56 * 2**20
        ),
        name="whole_block",
    )(tokens, cotangent, gain_attn.reshape(1, D), rel, gain_mlp.reshape(1, D), w_qkv, w_proj, w_fc1, w_fc2)


def deliver_kernel(
    output, grad_tokens, qkv_total, fc1_total, fc2_total, small,
    output_to, grad_tokens_to, grad_qkv, grad_proj, table, grad_fc1, grad_fc2, gain_attn, gain_mlp
):
    grad_tokens_to[...] = grad_tokens[...]
    output_to[...] = output[...]
    for i in range(3):
        grad_qkv[:, D * i : D * i + D] = qkv_total[4 * i : 4 * i + 4]
    for i in range(4):
        grad_fc1[:, D * i : D * i + D] = fc1_total[4 * i : 4 * i + 4]
    grad_proj[...] = qkv_total[12:16]
    grad_fc2[...] = fc2_total[...]
    table[...] = small[0:8, 0:225]
    for i in range(2):
        gain_attn[256 * i : 256 * i + 256] = small[8 + i]
        gain_mlp[256 * i : 256 * i + 256] = small[10 + i]


def deliver(*results):
    vmem = pl.BlockSpec(memory_space=pltpu.VMEM)
    return pl.pallas_call(
        deliver_kernel,
        out_shape=(
            jax.ShapeDtypeStruct((8, 48, D), BF16),
            jax.ShapeDtypeStruct((8, 48, D), F32),
            jax.ShapeDtypeStruct((4, 3 * D), F32),
            jax.ShapeDtypeStruct((4, D), F32),
            jax.ShapeDtypeStruct((8, 225), F32),
            jax.ShapeDtypeStruct((4, 4 * D), F32),
            jax.ShapeDtypeStruct((16, D), F32),
            jax.ShapeDtypeStruct((D,), F32),
            jax.ShapeDtypeStruct((D,), F32),
        ),
        in_specs=[vmem] * 6,
        out_specs=[vmem] * 9,
        name="deliver",
    )(*results)


def shards(tokens, cotangent, gain_attn, w_qkv, w_proj, rel_table, gain_mlp, w_fc1, w_fc2):
    return deliver(
        *whole(tokens, cotangent, gain_attn, w_qkv, w_proj, rel_table, gain_mlp, w_fc1, w_fc2)
    )


def solution(mesh):
    placed = (P("lat", "lon", None), P("lat", "lon", None), P(), P(), P(), P(), P(), P(), P())
    return jax.shard_map(
        shards,
        mesh=mesh,
        in_specs=placed,
        out_specs=(
            P("lat", "lon", None),
            P("lat", "lon", None),
            P(("lat", "lon"), None),
            P(("lat", "lon"), None),
            P(),
            P(("lat", "lon"), None),
            P(("lat", "lon"), None),
            P(),
            P(),
        ),
        check_vma=False,
    )
```

```python
import jax
import jax.numpy as jnp
from jax import lax
from jax.experimental import pallas as pl
from jax.experimental.pallas import tpu as pltpu
from jax.sharding import PartitionSpec as P

NORM_EPSILON = 1e-05
D = 512


MESH = pl.DeviceIdType.MESH
F32 = jnp.float32
BF16 = jnp.bfloat16


def place():
    lat = lax.axis_index("lat")
    lon = lax.axis_index("lon")
    return {
        "c": lax.rem(lon, 2),
        "x": lax.rem(lon // 2, 4),
        "y": lat // 2,
        "z": (lon // 8) * 2 + lax.rem(lat, 2),
    }


def moved(at, *hops):
    there = dict(at)
    for axis, step in hops:
        there[axis] = lax.rem(at[axis] + step, 2 if axis == "c" else 4)
    lat = there["y"] * 2 + lax.rem(there["z"], 2)
    lon = (there["z"] // 2) * 8 + there["x"] * 2 + there["c"]
    return (lat, lon)


def neighbour(step_lat, step_lon):
    return (
        lax.rem(lax.axis_index("lat") + step_lat + 8, 8),
        lax.rem(lax.axis_index("lon") + step_lon + 16, 16),
    )


PLANE = [(i, j) for i in range(4) for j in range(4) if (i, j) != (0, 0)]


def greet(at):
    barrier = pltpu.get_barrier_semaphore()
    others = [moved(at, ("c", 1))]
    others += [moved(at, ("z", i), ("x", j)) for i, j in PLANE]
    others += [moved(at, ("z", i), ("y", j)) for i, j in PLANE if j]
    others += [moved(at, ("c", 1), ("x", j)) for j in (1, 2, 3)]
    steps = ((1, 0), (0, 1), (1, 1), (-1, 0), (0, -1), (-1, -1))
    others += [neighbour(*step) for step in steps]
    for other in others:
        pl.semaphore_signal(barrier, inc=1, device_id=other, device_id_type=MESH)
    return len(others)


class Copies:
    def __init__(self, send_sems, recv_sems):
        self.send_sems, self.recv_sems, self.used = send_sems, recv_sems, 0

    def reserve(self, count):
        self.used += count
        return self.used - count

    def make(self, index, src, dst, device):
        return pltpu.make_async_remote_copy(
            src_ref=src,
            dst_ref=dst,
            send_sem=self.send_sems.at[index],
            recv_sem=self.recv_sems.at[index],
            device_id=device,
            device_id_type=MESH,
        )

    def start(self, src, dst, device):
        copy = self.make(self.reserve(1), src, dst, device)
        copy.start()
        return copy


class Part:
    def __init__(self, at, copies, axes, fours, own, pair, piece1, lines, lines_in):
        self.at, self.copies, self.fours = at, copies, fours
        self.first, self.second, self.third = axes
        self.own, self.pair, self.piece1 = own, pair, piece1
        self.lines, self.lines_in = lines, lines_in
        self.pairs, self.sent = {}, []

    def slot(self, step):
        return lax.rem(self.at[self.first] + step, 4)

    def place_start(self, step):
        j = self.slot(step)
        self.pairs[step] = self.copies.start(
            self.own.at[1 - self.at["c"], j], self.pair.at[j], moved(self.at, ("c", 1))
        )

    def place_send(self, step):
        self.pairs[step].wait()
        j, c = self.slot(step), self.at["c"]

        @pl.loop(0, 4)
        def _(i):
            self.pair[j, i] = self.pair[j, i] + self.own[c, j, i]

        if step:
            self.sent.append(
                self.copies.start(
                    self.pair.at[j], self.piece1.at[step - 1], moved(self.at, (self.first, step))
                )
            )

    def rows_start(self, key, rows):
        self.pairs[key] = self.copies.start(
            self.own.at[1 - self.at["c"], :, :, rows],
            self.pair.at[:, :, rows],
            moved(self.at, ("c", 1)),
        )

    def rows_send(self, key, rows):
        self.pairs[key].wait()
        c = self.at["c"]

        @pl.loop(0, 4)
        def _(j):
            self.pair[j, :, rows] = self.pair[j, :, rows] + self.own[c, j, :, rows]

        for step in (2, 1, 3):
            self.sent.append(
                self.copies.start(
                    self.pair.at[self.slot(step), :, rows],
                    self.piece1.at[step - 1, :, rows],
                    moved(self.at, (self.first, step)),
                )
            )

    def plane_send(self):
        for copy in self.sent:
            copy.wait()
        mine, lines = self.slot(0), self.lines
        for i in range(4):
            total = self.pair[mine, i].astype(F32)
            for k in range(3):
                total = total + self.piece1[k, i].astype(F32)
            for k in range(4):
                rows = total[16 * k : 16 * k + 16]
                if self.fours:
                    fours = [total[16 * m + 4 * k : 16 * m + 4 * k + 4] for m in range(4)]
                    rows = jnp.concatenate(fours, axis=0)
                lines[i, k] = rows.astype(BF16)
        at = self.at
        self.sent = [
            self.copies.start(
                lines.at[lax.rem(at[self.second] + i, 4), lax.rem(at[self.third] + j, 4)],
                self.lines_in.at[4 * i + j - 1],
                moved(at, (self.second, i), (self.third, j)),
            )
            for i, j in PLANE
        ]

    def finish(self):
        total = self.lines[self.at[self.second], self.at[self.third]].astype(F32)
        for copy in self.sent:
            copy.wait()
        for i in range(15):
            total = total + self.lines_in[i].astype(F32)
        return total


def part_scratch(columns):
    return [
        pltpu.VMEM((2, 4, 4, 64, columns), BF16),
        pltpu.VMEM((4, 4, 64, columns), BF16),
        pltpu.VMEM((3, 4, 64, columns), BF16),
        pltpu.VMEM((4, 4, 16, columns), BF16),
        pltpu.VMEM((15, 16, columns), BF16),
    ]


def share(at, copies, axes, held, slots):
    outer, inner = axes
    mine = at[outer] * 4 + at[inner]
    slots[mine] = held[...]
    return [
        copies.start(held, slots.at[mine], moved(at, (outer, i), (inner, j)))
        for i, j in PLANE
        if i < slots.shape[0] // 4
    ]


def sum_shared(started, held, slots):
    for copy in started:
        copy.wait()
    total = slots[0].astype(F32)
    for i in range(1, slots.shape[0]):
        total = total + slots[i].astype(F32)
    held[...] = total.astype(held.dtype)


def shift_in_start(copies, source, rows_in, edge, edge_in):
    started = [copies.start(source.at[4:8], rows_in, neighbour(1, 0))]
    for half in range(2):
        ends = [source[4 * half + r, 32:48].astype(F32)[12:16] for r in range(4)]
        edge[half] = jnp.concatenate(ends, axis=0).astype(BF16)
    started.append(copies.start(edge.at[0], edge_in.at[0], neighbour(0, 1)))
    started.append(copies.start(edge.at[1], edge_in.at[1], neighbour(1, 1)))
    return started


def shift_in_finish(started, source, rows_in, edge_in, grid):
    for copy in started:
        copy.wait()
    for row in range(8):
        held = (rows_in[row] if row < 4 else source[row - 4]).astype(F32)
        turned = pltpu.roll(held, 4, 0)
        ends = edge_in[1 if row < 4 else 0].astype(F32)[4 * (row % 4) : 4 * (row % 4) + 4]
        grid[row] = jnp.concatenate(
            [jnp.concatenate([ends, turned[4:8]], axis=0), turned[8:48]], axis=0
        )


def shift_back_start(copies, grid, rows_out, rows_in, edge, edge_in):
    for row in range(4):
        rows_out[row] = pltpu.roll(grid[row], 44, 0).astype(BF16)
    started = [copies.start(rows_out, rows_in, neighbour(-1, 0))]
    for half in range(2):
        firsts = [grid[4 * half + r, 0:8][0:4] for r in range(4)]
        edge[half] = jnp.concatenate(firsts, axis=0).astype(BF16)
    started.append(copies.start(edge.at[1], edge_in.at[1], neighbour(0, -1)))
    started.append(copies.start(edge.at[0], edge_in.at[0], neighbour(-1, -1)))
    return started


def shift_back_finish(started, grid, rows_in, edge_in, result):
    for copy in started:
        copy.wait()
    for row in range(8):
        if row < 4:
            turned = pltpu.roll(grid[row + 4], 44, 0)
        else:
            turned = rows_in[row - 4].astype(F32)
        ends = edge_in[1 if row < 4 else 0].astype(F32)[4 * (row % 4) : 4 * (row % 4) + 4]
        whole = jnp.concatenate(
            [turned[0:40], jnp.concatenate([turned[40:44], ends], axis=0)], axis=0
        )
        result[row] = whole.astype(result.dtype)


SHIFT_SCRATCH = [
    pltpu.VMEM((4, 48, D), BF16),
    pltpu.VMEM((2, 16, D), BF16),
    pltpu.VMEM((2, 16, D), BF16),
]


TOKENS = 384
WINDOWS = 6
PAIRS = 4
TILE = 16


def mm(a, b):
    return lax.dot_general(a, b, (((1,), (0,)), ((), ())), preferred_element_type=F32)


def mm_nt(a, b):
    return lax.dot_general(a, b, (((1,), (1,)), ((), ())), preferred_element_type=F32)


def mm_tn(a, b):
    return lax.dot_general(a, b, (((0,), (0,)), ((), ())), preferred_element_type=F32)


def split_low(value):
    high = value.astype(BF16)
    return high, (value - high.astype(F32)).astype(BF16)


def iota(shape, dim):
    return lax.broadcasted_iota(jnp.int32, shape, dim)


def tiles(body):
    @pl.loop(0, TOKENS // TILE, unroll=8)
    def _(i):
        body(i, pl.ds(pl.multiple_of(i * TILE, TILE), TILE))


def grid_tile(grid, i):
    window, row = i // 4, lax.rem(i, 4) * 2
    columns = pl.ds(pl.multiple_of(window * 8, 8), 8)
    return jnp.concatenate([grid[row, columns], grid[row + 1, columns]], axis=0)


def store_grid_tile(grid, i, tile):
    window, row = i // 4, lax.rem(i, 4) * 2
    columns = pl.ds(pl.multiple_of(window * 8, 8), 8)
    grid[row, columns] = tile[0:8]
    grid[row + 1, columns] = tile[8:16]


def normalise(vectors):
    centred = vectors - jnp.mean(vectors, axis=-1, keepdims=True)
    factor = lax.rsqrt(jnp.mean(centred * centred, axis=-1, keepdims=True) + NORM_EPSILON)
    return centred * factor, factor


def normalise_back(grad_out, normal, factor, gain):
    grad_hat = grad_out * gain
    inner = (
        grad_hat
        - jnp.mean(grad_hat, axis=-1, keepdims=True)
        - normal * jnp.mean(grad_hat * normal, axis=-1, keepdims=True)
    )
    return factor * inner


def line_order(axes):
    place_of = iota((D, 1), 0)
    core, r = place_of >> 8, place_of & 3
    at = {axis: (place_of >> shift) & 3 for axis, shift in zip(axes, (6, 4, 2))}
    z = ((at["z"] & 1) << 6) | ((at["z"] >> 1) << 5)
    feature = (at["y"] << 7) | z | (at["x"] << 3) | (core << 2) | r
    return jnp.where(iota((D, D), 1) == feature, 1.0, 0.0).astype(BF16)


def pair_offsets():
    row, column = iota((256, 128), 0), iota((256, 128), 1)
    target = ((column >> 6) << 7) + 15 * ((column >> 3) & 7) + (column & 7)
    return jnp.where(row == target, 1.0, 0.0).astype(BF16)


def store_wide(halves, i, rows):
    halves[0, 8 * i : 8 * i + 8] = rows[:, 0:128]
    halves[1, 8 * i : 8 * i + 8] = rows[:, 128:256]


def load_strided(halves, first):
    return jnp.concatenate([halves[k, pl.ds(first, 8, stride=8), :] for k in range(2)], axis=1)


def expand_bias(rel, table, shifted, bias, masked):
    table[...] = jnp.zeros_like(table)
    table[:, 0:225] = rel[...]
    whole = table[...]
    for b in range(8):
        store_wide(shifted, b, pltpu.roll(whole, (256 - (7 - b)) % 256, 1))
    spread = pair_offsets()
    key, query = iota((64, 128), 0), iota((64, 128), 1) & 63
    apart = jnp.where((key >> 5) == (query >> 5), 0.0, -1e30)
    apart = jnp.where(masked, apart, 0.0)
    for p in range(PAIRS):
        heads = []
        for h in (2 * p, 2 * p + 1):
            rows = load_strided(shifted, h)
            turned = [pltpu.roll(rows, 256 - (105 - 15 * a), 1)[:, 0:128] for a in range(8)]
            heads.append(jnp.concatenate(turned, axis=0))
        high, low = split_low(jnp.concatenate(heads, axis=1))
        bias[p] = mm(high, spread) + mm(low, spread) + apart


def collect_table(grad_bias, collected, total):
    spread = pair_offsets()
    for p in range(PAIRS):
        high, low = split_low(grad_bias[p])
        both = mm_nt(high, spread) + mm_nt(low, spread)
        for k in range(2):
            one = both[:, 128 * k : 128 * k + 128]
            one = jnp.concatenate([one, jnp.zeros_like(one)], axis=1)
            rows = one[56:64]
            for a in range(7):
                rows = rows + pltpu.roll(one[8 * a : 8 * a + 8], 105 - 15 * a, 1)
            h = 2 * p + k
            store_wide(collected, h, rows)
    table = load_strided(collected, 7)
    for b in range(7):
        table = table + pltpu.roll(load_strided(collected, b), 7 - b, 1)
    total[...] = table


def both_heads(pair):
    left = iota(pair.shape, 1) < 64
    zero = jnp.zeros_like(pair)
    return jnp.concatenate([jnp.where(left, pair, zero), jnp.where(left, zero, pair)], axis=0)


def own_heads(crossed):
    return jnp.where(iota((64, 128), 1) < 64, crossed[0:64], crossed[64:128])


def window_rows(w):
    return pl.ds(pl.multiple_of(w * 64, 64), 64)


def attend(w, qkv, bias, probs, attended):
    rows = window_rows(w)
    for p in range(PAIRS):
        query = qkv[rows, 128 * p : 128 * p + 128]
        keys = qkv[rows, D + 128 * p : D + 128 * p + 128]
        values = qkv[rows, 2 * D + 128 * p : 2 * D + 128 * p + 128]
        scores = mm_nt(keys, both_heads(query)) + bias[p]
        powers = jnp.exp(scores - jnp.max(scores, axis=0, keepdims=True))
        each = powers / jnp.sum(powers, axis=0, keepdims=True)
        probs[w, p] = each
        crossed = mm_tn(each.astype(BF16), values)
        attended[rows, 128 * p : 128 * p + 128] = own_heads(crossed).astype(BF16)


def attend_back(w, qkv, probs, grad_attended, grad_bias, grad_rows):
    rows = window_rows(w)
    for p in range(PAIRS):
        query = both_heads(qkv[rows, 128 * p : 128 * p + 128])
        keys = qkv[rows, D + 128 * p : D + 128 * p + 128]
        values = qkv[rows, 2 * D + 128 * p : 2 * D + 128 * p + 128]
        grads = both_heads(grad_attended[rows, 128 * p : 128 * p + 128])
        each = probs[w, p]
        grad_probs = mm_nt(values, grads)
        grad_scores = each * (grad_probs - jnp.sum(each * grad_probs, axis=0, keepdims=True))
        grad_bias[p] += grad_scores
        low = grad_scores.astype(BF16)
        grad_query = own_heads(mm_tn(low, keys)) * 0.125
        grad_rows[rows, 128 * p : 128 * p + 128] = grad_query.astype(BF16)
        grad_rows[rows, D + 128 * p : D + 128 * p + 128] = mm(low, query).astype(BF16)
        grad_rows[rows, 2 * D + 128 * p : 2 * D + 128 * p + 128] = mm(
            each.astype(BF16), grads
        ).astype(BF16)


GELU_SCALE = 0.7978845608028654
GELU_CUBE = 0.044715


def gelu_both(hidden):
    square = hidden * hidden
    swing = jnp.tanh(GELU_SCALE * hidden * (1.0 + GELU_CUBE * square))
    half = 0.5 + 0.5 * swing
    slope = half + (0.5 * GELU_SCALE) * hidden * (1.0 - swing * swing) * (
        1.0 + 3.0 * GELU_CUBE * square
    )
    return hidden * half, slope


def eight(tile):
    return tile[0:8] + tile[8:16]


COMPUTE_SCRATCH = [
    ("hat1", (TOKENS, D), F32),
    ("factor1", (TOKENS, 128), F32),
    ("norm1", (TOKENS, D), BF16),
    ("qkv", (TOKENS, 3 * D), BF16),
    ("attended", (TOKENS, D), BF16),
    ("resid", (TOKENS, D), F32),
    ("hat2", (TOKENS, D), F32),
    ("factor2", (TOKENS, 128), F32),
    ("norm2", (TOKENS, D), BF16),
    ("turned", (D, TOKENS), BF16),
    ("order_y", (D, D), BF16),
    ("order_x", (D, D), BF16),
    ("cot", (TOKENS, D), BF16),
    ("hidden", (TOKENS, D), F32),
    ("grad_active", (TOKENS, D), F32),
    ("active", (TOKENS, 4 * D), BF16),
    ("grad_hidden", (TOKENS, 4 * D), BF16),
    ("mlp_out", (TOKENS, D), F32),
    ("grad_norm", (TOKENS, D), F32),
    ("grad_resid", (TOKENS, D), F32),
    ("grad_resid_low", (TOKENS, D), BF16),
    ("grad_attended", (TOKENS, D), BF16),
    ("grad_rows", (TOKENS, 3 * D), BF16),
    ("probs", (WINDOWS, PAIRS, 64, 128), F32),
    ("bias", (PAIRS, 64, 128), F32),
    ("grad_bias", (PAIRS, 64, 128), F32),
    ("table", (8, 256), F32),
    ("shifted", (2, 64, 128), F32),
    ("gain_sums", (2, 8, D), F32),
]


class Block:
    def __init__(self, refs):
        for (name, _, _), ref in zip(COMPUTE_SCRATCH, refs):
            setattr(self, name, ref)


def attention_forward(s, x_grid, gain_attn, w_qkv):
    def first_norm(i, rows):
        normal, factor = normalise(grid_tile(x_grid, i))
        s.hat1[rows] = normal
        s.factor1[rows] = jnp.broadcast_to(factor, (TILE, 128))
        s.norm1[rows] = (normal * gain_attn[...]).astype(BF16)

    tiles(first_norm)
    for i in range(3):
        columns = slice(D * i, D * i + D)
        part = mm(s.norm1[...], w_qkv[:, columns])
        s.qkv[:, columns] = (part * 0.125 if i == 0 else part).astype(BF16)

    @pl.loop(0, WINDOWS, unroll=3)
    def _(w):
        attend(w, s.qkv, s.bias, s.probs, s.attended)


def before_mlp(s, x_grid, c_grid, gain_mlp):
    def second_norm(i, rows):
        resid = s.resid[rows] + grid_tile(x_grid, i)
        normal, factor = normalise(resid)
        s.resid[rows] = resid
        s.hat2[rows] = normal
        s.factor2[rows] = jnp.broadcast_to(factor, (TILE, 128))
        s.norm2[rows] = (normal * gain_mlp[...]).astype(BF16)
        s.cot[rows] = grid_tile(c_grid, i).astype(BF16)

    tiles(second_norm)
    s.turned[...] = mm_nt(s.order_x[...], s.norm2[...]).astype(BF16)


def mlp_step(s, j, block, w_fc1, w_fc2, own_fc2, own_fc1):
    columns = pl.ds(pl.multiple_of(j * D, D), D)
    s.hidden[...] = mm(s.norm2[...], w_fc1[:, columns])
    s.grad_active[...] = mm_nt(s.cot[...], w_fc2[columns])

    def bend(_, rows):
        active, slope = gelu_both(s.hidden[rows])
        s.active[rows, columns] = active.astype(BF16)
        s.grad_hidden[rows, columns] = (slope * s.grad_active[rows]).astype(BF16)

    tiles(bend)
    grad_fc2 = mm_tn(s.active[:, columns], s.cot[...]).astype(BF16).reshape(2, 2, 4, 2, 16, D)
    for low in range(2):
        for high in range(2):
            for x in range(4):
                for c in range(2):
                    own_fc2[c, j, 2 * high + low, 16 * x : 16 * x + 16, :] = grad_fc2[
                        low, high, x, c
                    ]
    grad_fc1 = mm(s.turned[...], s.grad_hidden[:, columns]).astype(BF16)
    own_fc1[:, :, :, block, :] = grad_fc1.reshape(2, 4, 4, 16, D)


def mlp_result(s, w_fc2, out_grid):
    s.mlp_out[...] = mm(s.active[...], w_fc2[...])

    def add(i, rows):
        store_grid_tile(out_grid, i, s.resid[rows] + s.mlp_out[rows])

    tiles(add)


def after_mlp(s, gain_mlp, w_fc1):
    s.grad_norm[...] = mm_nt(s.grad_hidden[...], w_fc1[...])
    s.gain_sums[...] = jnp.zeros_like(s.gain_sums)

    def second_back(i, rows):
        grad, normal = s.grad_norm[rows], s.hat2[rows]
        s.gain_sums[1] += eight(grad * normal)
        grad_resid = s.cot[rows].astype(F32) + normalise_back(
            grad, normal, s.factor2[rows][:, 0:1], gain_mlp[...]
        )
        s.grad_resid[rows] = grad_resid
        s.grad_resid_low[rows] = grad_resid.astype(BF16)

    tiles(second_back)


def attention_after(s, gain_attn, grad_grid, small):
    def first_back(i, rows):
        grad, normal = s.grad_norm[rows], s.hat1[rows]
        s.gain_sums[0] += eight(grad * normal)
        back = normalise_back(grad, normal, s.factor1[rows][:, 0:1], gain_attn[...])
        store_grid_tile(grad_grid, i, s.grad_resid[rows] + back)

    tiles(first_back)
    gains = [jnp.sum(s.gain_sums[i], axis=0, keepdims=True) for i in range(2)]
    rows = [gain[:, 256 * k : 256 * k + 256] for gain in gains for k in range(2)]
    small[...] = jnp.concatenate([s.table[...]] + rows + [jnp.zeros((4, 256), F32)], axis=0)


def whole_kernel(
    tokens, cotangent, gain_attn, rel, gain_mlp, w_qkv_hbm, w_proj_hbm, w_fc1_hbm, w_fc2_hbm,
    output, grad_tokens, qkv_total, fc1_total, fc2_total, small_total, *scratch
):
    refs = list(scratch)

    def take(count):
        taken = refs[:count]
        del refs[:count]
        return taken

    s = Block(take(len(COMPUTE_SCRATCH)))
    weights, weight_sem = take(4), take(1)[0]
    w_qkv, w_proj, w_fc1, w_fc2 = weights
    x_grid, c_grid, out_grid, grad_grid, small = take(5)
    send_sems, recv_sems = take(2)
    at = place()
    copies = Copies(send_sems, recv_sems)
    fc2 = Part(at, copies, ("y", "z", "x"), False, *take(5))
    fc1 = Part(at, copies, ("x", "z", "y"), True, *take(5))
    rest_y = Part(at, copies, ("y", "z", "x"), True, *take(5))
    rest_x = Part(at, copies, ("x", "z", "y"), True, *take(5))
    halves = ((slice(0, 256), s.order_y, rest_y), (slice(256, 512), s.order_x, rest_x))
    held, pair_slots, plane_slots = take(3)
    in_tokens, in_cot = take(3), take(3)
    back_out, back_tokens = take(4), take(4)

    loads = []
    for i, source in enumerate((w_qkv_hbm, w_proj_hbm, w_fc1_hbm, w_fc2_hbm)):
        loads.append(pltpu.make_async_copy(source, weights[i], weight_sem.at[i]))
        loads[-1].start()
    partners = greet(at)
    expand_bias(rel, s.table, s.shifted, s.bias, lax.axis_index("lat") == 0)
    pl.semaphore_wait(pltpu.get_barrier_semaphore(), partners)
    came_tokens = shift_in_start(copies, tokens, *in_tokens)
    s.order_y[...] = line_order(("y", "z", "x"))
    s.order_x[...] = line_order(("x", "z", "y"))
    shift_in_finish(came_tokens, tokens, in_tokens[0], in_tokens[2], x_grid)
    came_cot = shift_in_start(copies, cotangent, *in_cot)
    loads[0].wait()
    attention_forward(s, x_grid, gain_attn, w_qkv)
    for load in loads[1:]:
        load.wait()
    s.resid[...] = mm(s.attended[...], w_proj[...])
    shift_in_finish(came_cot, cotangent, in_cot[0], in_cot[2], c_grid)
    before_mlp(s, x_grid, c_grid, gain_mlp)

    steps = (2, 1, 3, 0)
    blocks = [pl.ds(pl.multiple_of(16 * fc2.slot(step), 16), 16) for step in steps]
    for i in range(4):
        mlp_step(s, fc2.slot(steps[i]), blocks[i], w_fc1, w_fc2, fc2.own, fc1.own)
        fc2.place_start(steps[i])
        fc1.rows_start(i, blocks[i])
        if i:
            fc2.place_send(steps[i - 1])
            fc1.rows_send(i - 1, blocks[i - 1])
    mlp_result(s, w_fc2, out_grid)
    went_out = shift_back_start(copies, out_grid, *back_out)
    after_mlp(s, gain_mlp, w_fc1)
    fc1.rows_send(3, blocks[3])
    fc2.place_send(0)
    for columns, order, part in halves:
        s.turned[...] = mm_nt(order[...], s.attended[...]).astype(BF16)
        grad_proj = mm(s.turned[...], s.grad_resid_low[:, columns]).astype(BF16)
        part.own[:, :, :, 48:64, :] = grad_proj.reshape(2, 4, 4, 16, 256)
        part.rows_start(1, slice(48, 64))
    s.grad_attended[...] = mm_nt(s.grad_resid_low[...], w_proj[...]).astype(BF16)
    s.grad_bias[...] = jnp.zeros_like(s.grad_bias)
    rest_y.rows_send(1, slice(48, 64))
    rest_x.rows_send(1, slice(48, 64))

    @pl.loop(0, WINDOWS, unroll=2)
    def _(w):
        attend_back(w, s.qkv, s.probs, s.grad_attended, s.grad_bias, s.grad_rows)

    fc2.plane_send()
    fc1.plane_send()
    for columns, order, part in halves:
        s.turned[...] = mm_nt(order[...], s.norm1[...]).astype(BF16)
        for i in range(3):
            grad_rows = s.grad_rows[:, D * i + columns.start : D * i + columns.stop]
            grad = mm(s.turned[...], grad_rows).astype(BF16)
            part.own[:, :, :, 16 * i : 16 * i + 16, :] = grad.reshape(2, 4, 4, 16, 256)
        part.rows_start(0, slice(0, 48))
    s.grad_norm[...] = mm_nt(s.grad_rows[...], w_qkv[...])
    rest_y.rows_send(0, slice(0, 48))
    rest_x.rows_send(0, slice(0, 48))
    collect_table(s.grad_bias, s.shifted, s.table)
    attention_after(s, gain_attn, grad_grid, small)
    held[0] = small[...].astype(BF16)
    shared = share(at, copies, ("c", "x"), held.at[0], pair_slots)
    went_tokens = shift_back_start(copies, grad_grid, *back_tokens)
    sum_shared(shared, held.at[1], pair_slots)
    shared = share(at, copies, ("z", "y"), held.at[1], plane_slots)
    rest_y.plane_send()
    rest_x.plane_send()
    shift_back_finish(went_out, out_grid, back_out[1], back_out[3], output)
    fc2_total[...] = fc2.finish()
    shift_back_finish(went_tokens, grad_grid, back_tokens[1], back_tokens[3], grad_tokens)
    fc1_total[...] = fc1.finish()
    sum_shared(shared, small_total, plane_slots)
    qkv_total[:, 0:256] = rest_y.finish()
    qkv_total[:, 256:512] = rest_x.finish()


def whole(tokens, cotangent, gain_attn, w_qkv, w_proj, rel, gain_mlp, w_fc1, w_fc2):
    vmem = pl.BlockSpec(memory_space=pltpu.VMEM)
    copies = 140
    return pl.pallas_call(
        whole_kernel,
        out_shape=(
            jax.ShapeDtypeStruct((8, 48, D), BF16),
            jax.ShapeDtypeStruct((8, 48, D), F32),
            jax.ShapeDtypeStruct((16, D), F32),
            jax.ShapeDtypeStruct((16, D), F32),
            jax.ShapeDtypeStruct((16, D), F32),
            jax.ShapeDtypeStruct((16, 256), F32),
        ),
        in_specs=[vmem] * 5 + [pl.BlockSpec(memory_space=pl.ANY)] * 4,
        out_specs=[vmem] * 6,
        scratch_shapes=[pltpu.VMEM(shape, kind) for _, shape, kind in COMPUTE_SCRATCH]
        + [pltpu.VMEM(w.shape, BF16) for w in (w_qkv, w_proj, w_fc1, w_fc2)]
        + [pltpu.SemaphoreType.DMA((4,))]
        + [pltpu.VMEM((8, 48, D), F32)] * 4
        + [pltpu.VMEM((16, 256), F32)]
        + [pltpu.SemaphoreType.DMA((copies,))] * 2
        + part_scratch(D) * 2
        + part_scratch(256) * 2
        + [
            pltpu.VMEM((2, 16, 256), BF16),
            pltpu.VMEM((8, 16, 256), BF16),
            pltpu.VMEM((16, 16, 256), BF16),
        ]
        + SHIFT_SCRATCH * 2
        + ([pltpu.VMEM((4, 48, D), BF16)] + SHIFT_SCRATCH) * 2,
        compiler_params=pltpu.CompilerParams(
            collective_id=0, has_side_effects=True, vmem_limit_bytes=56 * 2**20
        ),
        name="whole_block",
    )(tokens, cotangent, gain_attn.reshape(1, D), rel, gain_mlp.reshape(1, D), w_qkv, w_proj, w_fc1, w_fc2)


def deliver_kernel(
    output, grad_tokens, qkv_total, fc1_total, fc2_total, small,
    output_to, grad_tokens_to, grad_qkv, grad_proj, table, grad_fc1, grad_fc2, gain_attn, gain_mlp
):
    grad_tokens_to[...] = grad_tokens[...]
    output_to[...] = output[...]
    for i in range(3):
        grad_qkv[:, D * i : D * i + D] = qkv_total[4 * i : 4 * i + 4]
    for i in range(4):
        grad_fc1[:, D * i : D * i + D] = fc1_total[4 * i : 4 * i + 4]
    grad_proj[...] = qkv_total[12:16]
    grad_fc2[...] = fc2_total[...]
    table[...] = small[0:8, 0:225]
    for i in range(2):
        gain_attn[256 * i : 256 * i + 256] = small[8 + i]
        gain_mlp[256 * i : 256 * i + 256] = small[10 + i]


def deliver(*results):
    vmem = pl.BlockSpec(memory_space=pltpu.VMEM)
    return pl.pallas_call(
        deliver_kernel,
        out_shape=(
            jax.ShapeDtypeStruct((8, 48, D), BF16),
            jax.ShapeDtypeStruct((8, 48, D), F32),
            jax.ShapeDtypeStruct((4, 3 * D), F32),
            jax.ShapeDtypeStruct((4, D), F32),
            jax.ShapeDtypeStruct((8, 225), F32),
            jax.ShapeDtypeStruct((4, 4 * D), F32),
            jax.ShapeDtypeStruct((16, D), F32),
            jax.ShapeDtypeStruct((D,), F32),
            jax.ShapeDtypeStruct((D,), F32),
        ),
        in_specs=[vmem] * 6,
        out_specs=[vmem] * 9,
        name="deliver",
    )(*results)


def shards(tokens, cotangent, gain_attn, w_qkv, w_proj, rel_table, gain_mlp, w_fc1, w_fc2):
    return deliver(
        *whole(tokens, cotangent, gain_attn, w_qkv, w_proj, rel_table, gain_mlp, w_fc1, w_fc2)
    )


def solution(mesh):
    placed = (P("lat", "lon", None), P("lat", "lon", None), P(), P(), P(), P(), P(), P(), P())
    return jax.shard_map(
        shards,
        mesh=mesh,
        in_specs=placed,
        out_specs=(
            P("lat", "lon", None),
            P("lat", "lon", None),
            P(("lat", "lon"), None),
            P(("lat", "lon"), None),
            P(),
            P(("lat", "lon"), None),
            P(("lat", "lon"), None),
            P(),
            P(),
        ),
        check_vma=False,
    )
```
